32 devices in a mesh: dp: 16 (over z, x, core), shard: 2 (over y).
Axes of the slice: x: 2, y: 2, z: 4, core: 2. Of those that a mesh axis runs over, the one named last changes fastest.
Arguments:
- tokens: bfloat16 [16384, 960], P(('dp', 'shard')), may hold values from -6 to 6
- cotangent: bfloat16 [16384, 960], P(('dp', 'shard')), may hold values from -6 to 6
- w_query: bfloat16 [960, 960], P('shard'), may hold values from -0.1875 to 0.1875
- w_key: bfloat16 [960, 320], P('shard'), may hold values from -0.1875 to 0.1875
- w_value: bfloat16 [960, 320], P('shard'), may hold values from -0.1875 to 0.1875
- w_output: bfloat16 [960, 960], P('shard'), may hold values from -1 to 1
- w_gate: bfloat16 [960, 2560], P('shard'), may hold values from -0.1875 to 0.1875
- w_up: bfloat16 [960, 2560], P('shard'), may hold values from -0.1875 to 0.1875
- w_down: bfloat16 [2560, 960], P('shard'), may hold values from -0.125 to 0.125
- attention_gain: bfloat16 [960], P('shard'), may hold values from 0.099609375 to 1.8984375
- feed_gain: bfloat16 [960], P('shard'), may hold values from 0.099609375 to 1.8984375
- seq_lengths: int32 [16], replicated, may hold values from 1 to 2048, 16384 in all
Outputs:
- output: bfloat16 [16384, 960], P(('dp', 'shard'))
- grad_tokens: float32 [16384, 960], P(('dp', 'shard'))
- grad_query: float32 [960, 960], P('shard')
- grad_key: float32 [960, 320], P('shard')
- grad_value: float32 [960, 320], P('shard')
- grad_output: float32 [960, 960], P('shard')
- grad_gate: float32 [960, 2560], P('shard')
- grad_up: float32 [960, 2560], P('shard')
- grad_down: float32 [2560, 960], P('shard')
- grad_attention_gain: float32 [960], P('shard')
- grad_feed_gain: float32 [960], P('shard')
The draws below stay inside these ranges and needn't reach their ends.
Inputs may be any that keep to these rules, and one draw needn't show every extreme that they name: `seq_lengths`: the lengths sum to 16384; the largest is exactly 2048.
All inputs are finite; a program needn't handle non-finite values.
Results may differ from the reference program's by a relative error of at most 0.017.
Values may be sent and summed in bfloat16 or wider, within the bound.
A program may use at most 256 MiB of HBM per device.

```python
import math
import jax
import jax.numpy as jnp
import numpy as np
from jax import lax

D = 960
HEADS = 15
KV_HEADS = 5
HEAD_DIM = 64
FF = 2560
TOK_DEV = 512
REACH_DEVICES = 4
KV = 320
MAXLEN = 2048
TOKENS = 16384
NSEQ = 16


def level_of(stream_key, extent, cuts, low, largest):
    def one(axis_at, parts):
        draws = jax.random.uniform(jax.random.fold_in(jax.random.fold_in(stream_key, 6), axis_at), (parts,), jnp.float32, low / len(cuts), largest / len(cuts))
        return jnp.repeat(jnp.exp(draws), extent[axis_at] // parts).reshape((-1,) + (1,) * (len(extent) - axis_at - 1))

    gain = one(*cuts[0])
    for cut in cuts[1:]:
        gain = gain * one(*cut)
    return gain


def length_profile(number_of, total, bound, slope):
    loads = [(1 << 20) // math.isqrt(grade ** slope) + 1 for grade in range(2, number_of + 1)]
    rest, counts = total - bound - (number_of - 1), [1] * (number_of - 1)
    while rest > 0:
        candidates = [i for i in range(number_of - 1) if counts[i] < bound]
        pool, budget = sum([loads[i] for i in candidates]), rest
        for i in candidates:
            more = min(bound - counts[i], max(1, budget * loads[i] // pool), rest)
            counts[i] = counts[i] + more
            rest = rest - more
    return np.array([bound] + counts)


def ragged_sizes(rng, number_of, total, limit, lean):
    if number_of == 2:
        one = jax.random.randint(rng, (), max(1, total - limit), min(limit, total - 1) + 1)
        return jnp.stack([one, total - one])
    sizes = jnp.asarray(length_profile(number_of, total, limit, lean), jnp.int32)
    pairs = (number_of - 1) // 2
    source_of, sink = sizes[1:1 + 2 * pairs:2], sizes[2:2 + 2 * pairs:2]
    margin = jnp.minimum(source_of - 1, limit - sink)
    moved = jax.random.randint(jax.random.fold_in(rng, 1), (pairs,), 0, 1 << 20) % (margin + 1)
    sizes = sizes.at[1:1 + 2 * pairs:2].set(source_of - moved).at[2:2 + 2 * pairs:2].set(sink + moved)
    return sizes[jax.random.permutation(jax.random.fold_in(rng, 2), number_of)]


def normal_values(own_key, dims, scale, most, pieces=(), kind=jnp.bfloat16):
    level = level_of(own_key, dims, pieces, -0.22, 0.18) if pieces else 1.0
    values = jax.random.normal(own_key, dims, jnp.float32) * scale * level
    return jnp.minimum(jnp.maximum(values, -most), most).astype(kind)


def setup_inputs(seed: int = 0) -> dict:
    seeds = jax.random.split(jax.random.key(seed), 13)
    tokens = normal_values(seeds[0], (TOKENS, D), 1.0, 6.0, ((0, 32),))
    cotangent = normal_values(seeds[1], (TOKENS, D), 1.0, 6.0, ((0, 32),))
    w_query = normal_values(seeds[2], (D, D), D ** -0.5, 0.1875, ((0, 2),))
    w_key = normal_values(seeds[3], (D, KV), D ** -0.5, 0.1875, ((0, 2),))
    w_value = normal_values(seeds[4], (D, KV), D ** -0.5, 0.1875, ((0, 2),))
    w_output = normal_values(seeds[5], (D, D), (D // 32) ** -0.5, 1.0, ((0, 2),))
    w_gate = normal_values(seeds[6], (D, FF), D ** -0.5, 0.1875, ((0, 2),))
    w_up = normal_values(seeds[7], (D, FF), D ** -0.5, 0.1875, ((0, 2),))
    w_down = normal_values(seeds[8], (FF, D), FF ** -0.5, 0.125, ((0, 2),))
    attention_gain = jnp.clip(1.0 + 0.18 * jax.random.normal(seeds[9], (D,), jnp.float32), 0.099609375, 1.8984375).astype(jnp.bfloat16)
    feed_gain = jnp.clip(1.0 + 0.18 * jax.random.normal(seeds[10], (D,), jnp.float32), 0.099609375, 1.8984375).astype(jnp.bfloat16)
    seq_lengths = ragged_sizes(seeds[11], NSEQ, TOKENS, MAXLEN, 2).astype(jnp.int32)
    return {"tokens": tokens, "cotangent": cotangent, "w_query": w_query, "w_key": w_key, "w_value": w_value, "w_output": w_output, "w_gate": w_gate, "w_up": w_up, "w_down": w_down, "attention_gain": attention_gain, "feed_gain": feed_gain, "seq_lengths": seq_lengths}


@jax.custom_vjp
def low(v):
    return lax.optimization_barrier(v.astype(jnp.bfloat16)).astype(jnp.float32)

@jax.custom_vjp
def low_back(v):
    return v

def low_keep(v):
    return (low(v), None)

def low_pass(kept, grad):
    return (grad,)

def back_keep(v):
    return (v, None)

def back_low(kept, grad):
    return (low(grad),)
low.defvjp(low_keep, low_pass)
low_back.defvjp(back_keep, back_low)
EPSILON = 1e-05
THETA = 100000.0
MASKED = -1e+30
highest = lax.Precision.HIGHEST

def segments_and_positions(seq_lengths, first, count):
    ends = jnp.cumsum(seq_lengths).astype(jnp.int32)
    index = first + jnp.arange(count, dtype=jnp.int32)
    passed = index[:, None] >= ends[None, :]
    segment = lax.optimization_barrier(jnp.sum(passed.astype(jnp.int32), axis=1)).astype(jnp.int32)
    begin = lax.optimization_barrier(jnp.max(jnp.where(passed, ends[None, :], 0), axis=1)).astype(jnp.int32)
    return (segment, index - begin)

def rotary_tables(position):
    half = HEAD_DIM // 2
    inverse = jnp.exp(-jnp.arange(half, dtype=jnp.float32) * (2.0 / HEAD_DIM) * jnp.log(THETA))
    angle = position.astype(jnp.float32)[:, None] * inverse[None, :]
    angle = jnp.concatenate([angle, angle], axis=1)
    return (jnp.cos(angle), jnp.sin(angle))

def rotate(values, cosine, sine):
    half = HEAD_DIM // 2
    turned = jnp.concatenate([-values[..., half:], values[..., :half]], axis=-1)
    return values * cosine[:, None, :] + turned * sine[:, None, :]

def reference(tokens, cotangent, w_query, w_key, w_value, w_output, w_gate, w_up, w_down, attention_gain, feed_gain, seq_lengths):
    segment, position = segments_and_positions(seq_lengths, 0, TOKENS)
    cosine, sine = rotary_tables(position)
    window = REACH_DEVICES * TOK_DEV
    group = HEADS // KV_HEADS
    segment_padded = jnp.concatenate([jnp.full((window,), -1, jnp.int32), segment])

    def layer(x, wq, wk, wv, wo, wg, wu, wd, gain_one, gain_two):
        scale_one = lax.rsqrt(lax.optimization_barrier(jnp.mean(x * x, axis=1, keepdims=True)) + EPSILON)
        hidden_one = low(x * scale_one * gain_one)
        queries = low_back(jnp.dot(hidden_one, wq, precision=highest))
        keys = low_back(jnp.dot(hidden_one, wk, precision=highest))
        values = low(low_back(jnp.dot(hidden_one, wv, precision=highest)))
        q_rot = low(rotate(queries.reshape(TOKENS, HEADS, HEAD_DIM), cosine, sine))
        k_rot = low(rotate(keys.reshape(TOKENS, KV_HEADS, HEAD_DIM), cosine, sine))
        v_all = values.reshape(TOKENS, KV_HEADS, HEAD_DIM)
        k_pad = jnp.concatenate([jnp.zeros((window, KV_HEADS, HEAD_DIM), k_rot.dtype), k_rot])
        v_pad = jnp.concatenate([jnp.zeros((window, KV_HEADS, HEAD_DIM), v_all.dtype), v_all])

        def attend(number):
            start = number * TOK_DEV
            q_block = lax.dynamic_slice_in_dim(q_rot, start, TOK_DEV, 0).reshape(TOK_DEV, KV_HEADS, group, HEAD_DIM)
            k_block = lax.dynamic_slice_in_dim(k_pad, start, window + TOK_DEV, 0)
            v_block = lax.dynamic_slice_in_dim(v_pad, start, window + TOK_DEV, 0)
            raw = jnp.einsum('qgrd,kgd->grqk', q_block, k_block, precision=highest)
            scores = low_back(raw) * 0.125
            seg_rows = lax.dynamic_slice_in_dim(segment, start, TOK_DEV, 0)
            seg_cols = lax.dynamic_slice_in_dim(segment_padded, start, window + TOK_DEV, 0)
            rows = start + jnp.arange(TOK_DEV, dtype=jnp.int32)
            cols = start - window + jnp.arange(window + TOK_DEV, dtype=jnp.int32)
            valid = jnp.logical_and(seg_rows[:, None] == seg_cols[None, :], cols[None, :] <= rows[:, None])
            scores = jnp.where(valid[None, None], scores, MASKED)
            top = lax.optimization_barrier(jnp.max(scores, axis=3, keepdims=True))
            weights = jnp.exp(scores - top)
            weights = weights / lax.optimization_barrier(jnp.sum(weights, axis=3, keepdims=True))
            mixed = jnp.einsum('grqk,kgd->qgrd', low(weights), v_block, precision=highest)
            return mixed.reshape(TOK_DEV, D)
        blocks = lax.map(jax.checkpoint(attend), jnp.arange(TOKENS // TOK_DEV, dtype=jnp.int32))
        attended = low_back(low(blocks.reshape(TOKENS, D)))
        middle = x + low_back(jnp.dot(attended, wo, precision=highest))
        scale_two = lax.rsqrt(lax.optimization_barrier(jnp.mean(middle * middle, axis=1, keepdims=True)) + EPSILON)
        hidden_two = low(middle * scale_two * gain_two)
        gate = low_back(jnp.dot(hidden_two, wg, precision=highest))
        upper = low_back(jnp.dot(hidden_two, wu, precision=highest))
        inner = low(jax.nn.silu(gate) * upper)
        return middle + low_back(jnp.dot(inner, wd, precision=highest))
    inputs = (tokens, w_query, w_key, w_value, w_output, w_gate, w_up, w_down, attention_gain, feed_gain)
    inputs = tuple((item.astype(jnp.float32) for item in inputs))
    result, pullback = jax.vjp(layer, *inputs)
    grads = pullback(cotangent.astype(jnp.float32))
    return (result.astype(jnp.bfloat16), grads[0], grads[1], grads[2], grads[3], grads[4], grads[5], grads[6], grads[7], grads[8], grads[9])
```

```python
import functools

import jax
import jax.numpy as jnp
from jax import lax
from jax.experimental import pallas as pl
from jax.experimental.pallas import tpu as pltpu
from jax.sharding import PartitionSpec as P

D = 960
HEADS = 15
KV_HEADS = 5
GROUP = 3
HEAD_DIM = 64

EPSILON = 1e-05
THETA = 100000.0
MASKED = -1e30
LOG2E = 1.4426950408889634
SCALE2 = 0.125 * LOG2E

MESH = pl.DeviceIdType.MESH
WIDE = 512
CHUNK = 256
STRIP = 128
BF16 = jnp.bfloat16
F32 = jnp.float32


def dot(left, right):
    return lax.dot_general(left, right, (((1,), (0,)), ((), ())), preferred_element_type=F32)


def against_rows(left, right):
    return lax.dot_general(left, right, (((1,), (1,)), ((), ())), preferred_element_type=F32)


def over_first(left, right):
    return lax.dot_general(left, right, (((0,), (0,)), ((), ())), preferred_element_type=F32)


def masked(scores, start, low, diagonal):
    rows = start + lax.broadcasted_iota(jnp.int32, scores.shape, 0)
    valid = rows >= low
    if diagonal is not None:
        cols = diagonal + lax.broadcasted_iota(jnp.int32, scores.shape, 1)
        valid = jnp.logical_and(valid, rows <= cols)
    return jnp.where(valid, scores, MASKED)


def place():
    return lax.axis_index("dp"), lax.axis_index("shard")


def other(dp, y, bit):
    step = 1 << bit
    mine = (dp // step) % 2
    return (dp + step - 2 * step * mine, y)


def greet(partners):
    barrier = pltpu.get_barrier_semaphore()
    for partner in partners:
        pl.semaphore_signal(barrier, inc=1, device_id=partner, device_id_type=MESH)
    pl.semaphore_wait(barrier, len(partners))


class Route:
    def __init__(self, src, dst, send, recv, partner):
        self.make = lambda: pltpu.make_async_remote_copy(
            src_ref=src, dst_ref=dst, send_sem=send, recv_sem=recv, device_id=partner, device_id_type=MESH)

    def start(self):
        self.make().start()

    def arrived(self):
        self.make().wait_recv()

    def sent(self):
        self.make().wait_send()


class Sums:
    def __init__(self, bits, wides, tall, outs, scratch, rings=None):
        self.wides, self.tall, self.outs, self.rings = wides, tall, outs, rings
        self.boxes = [scratch[:7]] * len(wides) + [scratch[7:14]] * (tall is not None)
        self.put_sem, self.send_sem, self.recv_sem = scratch[-3:]
        self.arrays = len(self.boxes)
        self.half = D // 4
        dp, y = place()
        self.core, self.x, self.z, self.y = dp % 2, (dp // 2) % 2, (dp // 4) % 2, y
        self.sibling, self.over_y = other(dp, y, 0), (dp, 1 - y)
        self.over_x, self.over_z = other(dp, y, 1), other(dp, y, 2)
        self.extra = [other(dp, y, bit) for bit in range(3, bits)]
        self.partners = [self.sibling, self.over_y, self.over_x, self.over_z] + self.extra
        more = len(self.extra)
        self.stages = [self.start_x, self.start_z]
        self.stages += [functools.partial(self.more, step) for step in range(more + 1)]
        self.stages += [self.back_x, self.back_core, self.finish]

    @staticmethod
    def scratch(bits, wide_arrays, tall, chunks, half):
        more = bits - 3
        count = wide_arrays + tall

        def boxes(n, shapes):
            return [pltpu.VMEM((n, chunks) + shape, BF16) for shape in shapes]

        shared = [(half, 128), (max(more, 1), half, 128)]
        out = []
        if wide_arrays:
            out += boxes(wide_arrays, [(2, half, WIDE)] * 2 + [(half, WIDE), (half, 256)] + shared + [(2 * half, WIDE)])
        else:
            out += [None] * 7
        if tall:
            out += boxes(1, [(2, 2 * half, 256)] * 2 + [(2 * half, 256), (half, 256)] + shared + [(4 * half, 256)])
        return out + [
            pltpu.SemaphoreType.DMA((2, count, chunks)),
            pltpu.SemaphoreType.DMA((8 + more, count, chunks)),
            pltpu.SemaphoreType.DMA((8 + more, count, chunks)),
        ]

    def box(self, which, a, n):
        return self.boxes[a][which].at[0 if self.is_tall(a) else a, n]

    def is_tall(self, a):
        return a == len(self.wides)

    def own_share(self, a, n):
        return self.box(0, a, n)

    def sibling_share(self, a, n):
        ring = self.rings[1 if self.is_tall(a) else 0]
        return ring.at[n % 2] if self.is_tall(a) else ring.at[n % 2, a]

    def source(self, a, n, c, which):
        rows = pl.ds(pl.multiple_of(c * self.half, 16), self.half)
        return self.wides[a].at[which, rows, pl.ds(pl.multiple_of(n * WIDE, 128), WIDE)]

    def x_part(self, a, which):
        if self.is_tall(a):
            return pl.ds(pl.multiple_of(which * self.half, 16), self.half), slice(None)
        return slice(None), pl.ds(pl.multiple_of(which * 256, 128), 256)

    def z_part(self, which):
        return slice(None), pl.ds(pl.multiple_of(which * 128, 128), 128)

    def back_at(self, a, c, x=None, z=None):
        half = self.half
        if self.is_tall(a):
            if x is None:
                return pl.ds(pl.multiple_of(c * 2 * half, 16), 2 * half), slice(None)
            rows = pl.ds(pl.multiple_of(c * 2 * half + x * half, 16), half)
            return rows, slice(None) if z is None else pl.ds(pl.multiple_of(z * 128, 128), 128)
        rows = pl.ds(pl.multiple_of(c * half, 16), half)
        if x is None:
            return rows, slice(None)
        if z is None:
            return rows, pl.ds(pl.multiple_of(x * 256, 128), 256)
        return rows, pl.ds(pl.multiple_of(x * 256 + z * 128, 128), 128)

    def route(self, stage, a, n, src, dst, partner):
        return Route(src, dst, self.send_sem.at[stage, a, n], self.recv_sem.at[stage, a, n], partner)

    def copy(self, stage, a, n):
        loc, core_in, y_in, x_in, z_in, more_in, back = (self.box(i, a, n) for i in range(7))
        more = len(self.extra)
        if stage < 2:
            leaving = self.sibling_share(a, n).at[stage] if self.rings else self.source(a, n, 1 - self.core, stage)
            return self.route(stage, a, n, leaving, core_in.at[stage], self.sibling)
        if stage == 2:
            return self.route(stage, a, n, loc.at[1 - self.y], y_in, self.over_y)
        if stage == 3:
            return self.route(stage, a, n, y_in.at[self.x_part(a, 1 - self.x)], x_in, self.over_x)
        if stage == 4:
            return self.route(stage, a, n, x_in.at[self.z_part(1 - self.z)], z_in, self.over_z)
        if stage < 5 + more:
            so_far = z_in if stage == 5 else more_in.at[stage - 6]
            return self.route(stage, a, n, so_far, more_in.at[stage - 5], self.extra[stage - 5])
        at = [(self.core, self.x, self.z), (self.core, self.x), (self.core,)][stage - 5 - more]
        part = back.at[self.back_at(a, *at)]
        return self.route(stage, a, n, part, part, (self.over_z, self.over_x, self.sibling)[stage - 5 - more])

    def puts(self, a, n):
        box, out = self.box(6, a, n), self.outs[a]
        if self.is_tall(a):
            return [pltpu.make_async_copy(box, out.at[:, pl.ds(pl.multiple_of(n * 256, 128), 256)], self.put_sem.at[0, a, n])]
        if not self.rings:
            return [pltpu.make_async_copy(box, out.at[:, pl.ds(pl.multiple_of(n * WIDE, 128), WIDE)], self.put_sem.at[0, a, n])]
        return [
            pltpu.make_async_copy(
                box.at[:, pl.ds(i * 256, 256)],
                out.at[:, pl.ds(pl.multiple_of(i * (out.shape[1] // 2) + n * 256, 128), 256)],
                self.put_sem.at[i, a, n])
            for i in range(2)
        ]

    def start_core(self, a, n):
        for which in range(2):
            self.copy(which, a, n).start()

    def core_sent(self, a, n):
        for which in range(2):
            self.copy(which, a, n).sent()

    def start_y(self, a, n):
        loc, core_in = self.box(0, a, n), self.box(1, a, n)
        for which in range(2):
            self.copy(which, a, n).arrived()
            mine = loc.at[which] if self.rings else self.source(a, n, self.core, which)
            loc[which] = mine[...] + core_in[which]
        self.copy(2, a, n).start()

    def start_x(self, a, n):
        loc, y_in = self.box(0, a, n), self.box(2, a, n)
        self.copy(2, a, n).arrived()
        y_in[...] = y_in[...] + loc[self.y]
        self.copy(3, a, n).start()

    def start_z(self, a, n):
        y_in, x_in = self.box(2, a, n), self.box(3, a, n)
        self.copy(3, a, n).arrived()
        x_in[...] = x_in[...] + y_in[self.x_part(a, self.x)]
        self.copy(4, a, n).start()

    def more(self, step, a, n):
        x_in, z_in, more_in, back = (self.box(i, a, n) for i in range(3, 7))
        self.copy(4 + step, a, n).arrived()
        if step == 0:
            total = z_in
            value = z_in[...] + x_in[self.z_part(self.z)]
        else:
            total = more_in.at[step - 1]
            value = (z_in if step == 1 else more_in.at[step - 2])[...] + total[...]
        if step < len(self.extra):
            total[...] = value
        else:
            back[self.back_at(a, self.core, self.x, self.z)] = value
        self.copy(5 + step, a, n).start()

    def back_x(self, a, n):
        stage = 5 + len(self.extra)
        self.copy(stage, a, n).arrived()
        self.copy(stage + 1, a, n).start()

    def back_core(self, a, n):
        stage = 6 + len(self.extra)
        self.copy(stage, a, n).arrived()
        self.copy(stage + 1, a, n).start()

    def finish(self, a, n):
        self.copy(7 + len(self.extra), a, n).arrived()
        for put in self.puts(a, n):
            put.start()

    def drain(self, a, n):
        for stage in range(2, 8 + len(self.extra)):
            self.copy(stage, a, n).sent()
        for put in self.puts(a, n):
            put.wait()


OWN_SIB, OWN_Y, OWN_NEXT, PASS_OWN, PREV_SIB, PREV_Y, PASS_PREV = range(7)
WEIGHT_CHUNKS = 5
FIRST_ROWS = (((0, 64), (64, 64)), ((128, 64), (192, 48)))


def forward_kernel(groups, low_ref, cosine, sine, x_ref, qkv_in, gains_in, wo_in, gate_in, up_in, down_in,
                   o_ref, lse_ref, q_ref, h_ref, scale_ref, gains, kv_out, qkv_out, wo_out, gate_out, up_out, down_out,
                   kv, w_qkv, wo, gate, up, down, top, acc, shrink, s_all, p_all,
                   kv_sem, load_sem, store_sem, send_sem, recv_sem, w_send, w_recv, wo_send, wo_recv, first_send, first_recv):
    dp, y = place()
    core, x, z = dp % 2, (dp // 2) % 2, (dp // 4) % 2
    k = dp // 2
    j = 2 * core + y
    j_y = 2 * core + 1 - y
    sibling, over_y, over_x, over_z = other(dp, y, 0), (dp, 1 - y), other(dp, y, 1), other(dp, y, 2)
    own = x_ref.shape[1]
    has_prev, has_next = k > 0, k < groups - 1
    first_core, last_core = core == 0, core == 1

    half, tall = gate_in.shape[0], down_in.shape[1]
    own_rows = pl.ds(pl.multiple_of(y * half, 16), half)
    own_cols = pl.ds(pl.multiple_of(y * tall, 128), tall)
    loads = [
        pltpu.make_async_copy(qkv_in, w_qkv.at[own_rows, :], load_sem.at[0]),
        pltpu.make_async_copy(gains_in, gains.at[own_rows, :], load_sem.at[1]),
        pltpu.make_async_copy(gate_in, gate.at[own_rows, :], load_sem.at[2]),
        pltpu.make_async_copy(up_in, up.at[own_rows, :], load_sem.at[3]),
        pltpu.make_async_copy(down_in, down.at[:, own_cols], load_sem.at[4]),
        pltpu.make_async_copy(wo_in, wo.at[own_rows, :], load_sem.at[5]),
    ]
    for copy in loads[:2]:
        copy.start()

    @pl.when(k == 0)
    def _():
        kv[:, : 4 * own, :] = jnp.zeros((KV_HEADS, 4 * own, 2 * HEAD_DIM), BF16)

    barrier = pltpu.get_barrier_semaphore()
    for partner in (sibling, over_y, over_x, over_z):
        pl.semaphore_signal(barrier, inc=1, device_id=partner, device_id_type=MESH)

    @pl.when(has_prev)
    def _():
        pl.semaphore_signal(barrier, inc=1, device_id=(dp - 2, y), device_id_type=MESH)

    @pl.when(has_next)
    def _():
        pl.semaphore_wait(barrier, 5)

    @pl.when(jnp.logical_not(has_next))
    def _():
        pl.semaphore_wait(barrier, 4)

    def slot(h, n):
        return kv.at[h, pl.ds(pl.multiple_of(n * own, own), own), :]

    def halo(route, h):
        after = jnp.minimum(dp + 2, 2 * groups - 1)
        sems = (send_sem.at[route, h], recv_sem.at[route, h])
        if route == OWN_SIB:
            return Route(slot(h, 4 + j), slot(h, 4 + j), *sems, sibling)
        if route == OWN_Y:
            return Route(slot(h, 4 + j), slot(h, 4 + j), *sems, over_y)
        if route == OWN_NEXT:
            return Route(slot(h, 4 + j), slot(h, j), *sems, (after, y))
        if route == PASS_OWN:
            return Route(slot(h, 4 + j_y), slot(h, 4 + j_y), *sems, sibling)
        if route == PREV_SIB:
            return Route(slot(h, j), slot(h, j), *sems, sibling)
        if route == PREV_Y:
            return Route(slot(h, j), slot(h, j), *sems, over_y)
        return Route(slot(h, j_y), slot(h, j_y), *sems, sibling)

    sent_if = {
        OWN_SIB: first_core, OWN_Y: j != 3, OWN_NEXT: has_next, PASS_OWN: first_core,
        PREV_SIB: jnp.logical_and(last_core, has_prev), PREV_Y: jnp.logical_and(j != 0, has_prev),
        PASS_PREV: jnp.logical_and(last_core, has_prev),
    }
    got_if = {
        OWN_SIB: last_core, OWN_Y: j != 2, OWN_NEXT: has_prev, PASS_OWN: last_core,
        PREV_SIB: jnp.logical_and(first_core, has_prev), PREV_Y: jnp.logical_and(j != 1, has_prev),
        PASS_PREV: jnp.logical_and(first_core, has_prev),
    }

    def start(route, h):
        pl.when(sent_if[route])(lambda: halo(route, h).start())

    def arrived(route, h):
        pl.when(got_if[route])(lambda: halo(route, h).arrived())

    def pass_one(h):
        arrived(OWN_Y, h)
        start(PASS_OWN, h)
        arrived(OWN_NEXT, h)
        start(PREV_SIB, h)
        start(PREV_Y, h)

    def pass_two(h):
        arrived(PREV_Y, h)
        start(PASS_PREV, h)

    part = half // 2

    def wide_at(which, n, width_from, width):
        rows = pl.ds(pl.multiple_of(which * half + core * part, 16), part)
        return rows, pl.ds(pl.multiple_of(n * WIDE + width_from, 128), width)

    def down_at(which, n, row_from, rows, col_from, cols):
        return (pl.ds(pl.multiple_of(row_from, 16), rows),
                pl.ds(pl.multiple_of(which * tall + n * 256 + col_from, 128), cols))

    def weights(stage, a, n):
        out = (gate, up, down)[a]
        which = y if stage == 0 else 1 - y
        rows = core * half
        if a < 2:
            size = [(z * 256 + x * 128, 128), (z * 256 + x * 128, 128), (z * 256, 256), (0, 512)][stage]
            region = out.at[wide_at(which, n, *size)]
        else:
            size = [(rows, half, x * 128, 128), (rows, half, x * 128, 128), None, (rows, half, 0, 256)][stage]
            region = out.at[down_at(which, n, *size)]
        partner = (over_y, over_x, over_z, sibling)[stage]
        return Route(region, region, w_send.at[stage, a, n], w_recv.at[stage, a, n], partner)

    def hand_on(stage, a, n):
        if a == 2 and stage == 2:
            return
        weights(1 if a == 2 and stage == 3 else stage - 1, a, n).arrived()
        weights(stage, a, n).start()

    def store(a, n):
        if a < 2:
            cols = pl.ds(pl.multiple_of(n * WIDE, 128), WIDE)
            box, out = ((gate, gate_out), (up, up_out))[a]
            return [pltpu.make_async_copy(box.at[:, cols], out.at[:, cols], store_sem.at[a, n])]
        copies = []
        for which in range(2):
            some = pl.ds(pl.multiple_of(which * tall + n * 256, 128), 256)
            copies.append(pltpu.make_async_copy(down.at[:, some], down_out.at[:, some], store_sem.at[2 + which, n]))
        return copies

    def keep(a, n):
        weights(3, a, n).arrived()
        for copy in store(a, n):
            copy.start()

    def wo_part(which):
        return wo.at[pl.ds(pl.multiple_of(which * half + core * part, 16), part), :]

    wo_across = Route(wo_part(y), wo_part(y), wo_send.at[0], wo_recv.at[0], over_y)
    wo_within = Route(wo_part(1 - y), wo_part(1 - y), wo_send.at[1], wo_recv.at[1], sibling)
    wo_store = pltpu.make_async_copy(wo, wo_out, store_sem.at[0, WEIGHT_CHUNKS])

    def first(kind, i, which_x):
        row, count = FIRST_ROWS[which_x][i]
        at = (y if kind == 0 else 1 - y) * half + core * part + row
        region = w_qkv.at[pl.ds(pl.multiple_of(at, 16), count), :]
        return Route(region, region, first_send.at[kind, i], first_recv.at[kind, i], over_y if kind == 0 else over_x)

    def by_x(act, swap=False):
        for which_x in range(2):
            @pl.when(x == (1 - which_x if swap else which_x))
            def _(which_x=which_x):
                act(which_x)

    def first_part(which):
        return w_qkv.at[pl.ds(pl.multiple_of(which * half + core * part, 16), part), :]

    first_within = Route(first_part(1 - y), first_part(1 - y), first_send.at[2, 0], first_recv.at[2, 0], sibling)
    gains_across = Route(gains.at[own_rows, :], gains.at[own_rows, :], first_send.at[2, 1], first_recv.at[2, 1], over_y)
    first_store = pltpu.make_async_copy(w_qkv, qkv_out, store_sem.at[1, WEIGHT_CHUNKS])

    def across(n):
        for a in range(3):
            weights(0, a, n).start()

    def onward(stage, n):
        for a in range(3):
            hand_on(stage, a, n)

    loads[0].wait()
    loads[1].wait()
    gains_across.start()
    by_x(lambda which_x: [first(0, i, which_x).start() for i in range(2)])
    for copy in loads[2:]:
        copy.start()

    value = x_ref[...].astype(F32)
    scale = lax.rsqrt(jnp.mean(value * value, axis=0, keepdims=True) + EPSILON)
    scale_ref[...] = scale
    gains_across.arrived()
    h_ref[...] = (value * scale * gains[:, 0:1].astype(F32)).astype(BF16)
    for copy in loads[2:]:
        copy.wait()

    for i in range(2):
        def pass_first(which_x, i=i):
            first(0, i, which_x).arrived()
            first(1, i, which_x).start()

        by_x(pass_first)
        across(i)
    across(2)
    for i in range(2):
        by_x(lambda which_x, i=i: first(1, i, which_x).arrived(), swap=True)
    first_within.start()
    onward(1, 0)
    first_within.arrived()
    first_store.start()

    kv_width = KV_HEADS * HEAD_DIM
    turn = HEAD_DIM // 2

    def rotated(values):
        one, two = values[:turn], values[turn:]
        cos, sin = cosine[...], sine[...]
        return jnp.concatenate([one * cos - two * sin, two * cos + one * sin], axis=0)

    keys_values = over_first(w_qkv[:, : 2 * kv_width], h_ref[...])
    for h in range(KV_HEADS):
        at = h * HEAD_DIM
        both = jnp.concatenate(
            [rotated(keys_values[at : at + HEAD_DIM]), keys_values[kv_width + at : kv_width + at + HEAD_DIM]], axis=0
        ).astype(BF16)
        slot(h, 4 + j)[...] = both.T
        if h < 2:
            for route in (OWN_Y, OWN_NEXT, OWN_SIB):
                start(route, h)
    wo_across.start()
    onward(2, 0)
    onward(1, 1)
    queries_all = over_first(w_qkv[:, 2 * kv_width :], h_ref[...])
    for h in range(HEADS):
        at = h * HEAD_DIM
        q_ref[at : at + HEAD_DIM, :] = rotated(queries_all[at : at + HEAD_DIM]).astype(BF16)
    pass_one(0)
    onward(2, 1)
    pass_two(0)

    def window(h):
        return pltpu.make_async_copy(
            kv.at[h, pl.ds(pl.multiple_of(j * own, own), 5 * own), :], kv_out.at[h], kv_sem.at[h])

    blocks = own // CHUNK
    third = GROUP * CHUNK

    def block(h, n, spans, diagonal):
        both = kv[h, pl.ds(pl.multiple_of(n * own, own), own), :]
        keys = both[:, :HEAD_DIM]
        values = jnp.concatenate([both[:, HEAD_DIM:].T, jnp.ones((16, own), BF16)], axis=0)
        begin_at = (n - 4 - j) * own
        for b in range(blocks):
            low_at, high_at = spans[b]
            low = low_ref[:, b * CHUNK : (b + 1) * CHUNK]
            for r in range(GROUP):
                cols = pl.ds(b * third + r * CHUNK, CHUNK)
                rows = pl.ds(pl.multiple_of(h * GROUP * HEAD_DIM + r * HEAD_DIM, HEAD_DIM), HEAD_DIM)
                queries = q_ref[rows, b * CHUNK : (b + 1) * CHUNK]
                old = top[:, cols]
                high = jnp.full((8, CHUNK), MASKED, F32)
                for at in range(low_at, high_at, STRIP):
                    rows = slice(at, at + STRIP)
                    s = masked(dot(keys[rows], queries), begin_at + at, low, b * CHUNK if diagonal else None)
                    s_all[rows, cols] = s
                    high = jnp.maximum(high, jnp.max(s.reshape(STRIP // 8, 8, CHUNK), axis=0))
                new = jnp.maximum(old, jnp.max(high, axis=0, keepdims=True))
                bound = new * SCALE2
                for at in range(low_at, high_at, STRIP):
                    rows = slice(at, at + STRIP)
                    p_all[rows, cols] = jnp.exp2(s_all[rows, cols] * SCALE2 - bound).astype(BF16)
                shrink[:, cols] = jnp.exp2(old * SCALE2 - bound)
                top[:, cols] = new
        for b in range(blocks):
            low_at, high_at = spans[b]
            cols = pl.ds(b * third, third)
            acc[:, cols] = acc[:, cols] * shrink[:, cols] + dot(values[:, low_at:high_at], p_all[low_at:high_at, cols])

    every = [(0, own)] * blocks
    plan = [(4 + j, [(0, (b + 1) * CHUNK) for b in range(blocks)], True),
            (j, [(b * CHUNK, own) for b in range(blocks)], False),
            (j + 2, every, False), (j + 1 + 2 * y, every, False), (j + 3 - 2 * y, every, False)]
    spots = len(plan)
    steps = [(functools.partial(hand_on, 1), 0, 2), (functools.partial(hand_on, 2), 3, 2),
             (functools.partial(hand_on, 3), 1, 1), (keep, 4, 1)]

    def head(h, carry):
        top[...] = jnp.full(top.shape, MASKED, F32)
        acc[...] = jnp.zeros(acc.shape, F32)

        for p in range(spots):
            if p == 0:
                @pl.when(h < KV_HEADS - 2)
                def _():
                    for route in (OWN_Y, OWN_NEXT, OWN_SIB):
                        start(route, h + 2)

                pl.when(h < KV_HEADS - 3)(lambda: across(h + 3))
                pl.when(h == 0)(lambda: onward(3, 0))
                pl.when(h < KV_HEADS - 1)(lambda: pass_one(h + 1))

                @pl.when(h == 1)
                def _():
                    wo_across.arrived()
                    wo_within.start()
            if p == 2:
                pl.when(h < KV_HEADS - 1)(lambda: pass_two(h + 1))
                arrived(PREV_SIB, h)
                arrived(OWN_SIB, h)
            if p == 4:
                arrived(PASS_PREV, h)
                arrived(PASS_OWN, h)
            if p == 1:
                pl.when(h == 0)(lambda: keep(0, 0))
            block(h, *plan[p])
            for step, spot, ahead in reversed(steps):
                for a in range(3):
                    if (p - a - spot) % spots == 0:
                        n = h + ahead + (p - a - spot) // spots
                        fits = jnp.logical_and(n >= (1 if ahead == 1 and step is not keep else 0), n < WEIGHT_CHUNKS)
                        fits = jnp.logical_and(fits, n >= 2) if ahead == 2 else fits
                        pl.when(fits)(lambda step=step, a=a, n=n: step(a, n))

        window(h).start()
        for r in range(GROUP):
            rows = pl.ds(pl.multiple_of(h * GROUP * HEAD_DIM + r * HEAD_DIM, HEAD_DIM), HEAD_DIM)
            for b in range(blocks):
                cols = pl.ds(b * third + r * CHUNK, CHUNK)
                total = acc[HEAD_DIM : HEAD_DIM + 1, cols]
                o_ref[rows, b * CHUNK : (b + 1) * CHUNK] = (acc[:HEAD_DIM, cols] / total).astype(BF16)
                lse_ref[h, r : r + 1, b * CHUNK : (b + 1) * CHUNK] = top[:, cols] * SCALE2 + jnp.log2(total)
        return carry

    lax.fori_loop(0, KV_HEADS, head, 0)
    wo_within.arrived()
    wo_store.start()

    def finish(h, carry):
        for a in range(3):
            for stage in range(4):
                if a < 2 or stage != 2:
                    weights(stage, a, h).sent()
            for copy in store(a, h):
                copy.wait()
        for route in range(7):
            pl.when(sent_if[route])(lambda route=route: halo(route, h).sent())
        window(h).wait()
        return carry

    lax.fori_loop(0, KV_HEADS, finish, 0)
    for route in (wo_across, wo_within, first_within, gains_across):
        route.sent()
    by_x(lambda which_x: [first(kind, i, which_x).sent() for kind in range(2) for i in range(2)])
    wo_store.wait()
    first_store.wait()


def attend(low, cosine, sine, x, w_qkv, gains, w_output, w_gate, w_up, w_down_t, dp_size):
    own = x.shape[1]
    width = GROUP * own
    any_spec = pl.BlockSpec(memory_space=pl.ANY)
    vmem = pl.BlockSpec(memory_space=pltpu.VMEM)
    later = [jax.ShapeDtypeStruct((2 * w.shape[0], w.shape[1]), BF16) for w in (w_qkv, w_output, w_gate, w_up)]
    later.append(jax.ShapeDtypeStruct((w_down_t.shape[0], 2 * w_down_t.shape[1]), BF16))
    return pl.pallas_call(
        functools.partial(forward_kernel, dp_size // 2),
        out_shape=[
            jax.ShapeDtypeStruct((D, own), BF16),
            jax.ShapeDtypeStruct((KV_HEADS, 8, own), F32),
            jax.ShapeDtypeStruct((D, own), BF16),
            jax.ShapeDtypeStruct((D, own), BF16),
            jax.ShapeDtypeStruct((1, own), F32),
            jax.ShapeDtypeStruct((2 * gains.shape[0], gains.shape[1]), BF16),
            jax.ShapeDtypeStruct((KV_HEADS, 5 * own, 2 * HEAD_DIM), BF16),
        ] + later,
        in_specs=[vmem] * 4 + [any_spec] * 6,
        out_specs=[vmem] * 6 + [any_spec] * 6,
        scratch_shapes=[pltpu.VMEM((KV_HEADS, 8 * own, 2 * HEAD_DIM), BF16)]
        + [pltpu.VMEM(w.shape, BF16) for w in later]
        + [
            pltpu.VMEM((1, width), F32),
            pltpu.VMEM((HEAD_DIM + 16, width), F32),
            pltpu.VMEM((1, width), F32),
            pltpu.VMEM((own, width), F32),
            pltpu.VMEM((own, width), BF16),
            pltpu.SemaphoreType.DMA((KV_HEADS,)),
            pltpu.SemaphoreType.DMA((6,)),
            pltpu.SemaphoreType.DMA((4, WEIGHT_CHUNKS + 1)),
            pltpu.SemaphoreType.DMA((7, KV_HEADS)),
            pltpu.SemaphoreType.DMA((7, KV_HEADS)),
            pltpu.SemaphoreType.DMA((4, 3, WEIGHT_CHUNKS)),
            pltpu.SemaphoreType.DMA((4, 3, WEIGHT_CHUNKS)),
            pltpu.SemaphoreType.DMA((2,)),
            pltpu.SemaphoreType.DMA((2,)),
            pltpu.SemaphoreType.DMA((3, 2)),
            pltpu.SemaphoreType.DMA((3, 2)),
        ],
        compiler_params=pltpu.CompilerParams(
            collective_id=2, has_side_effects=True, vmem_limit_bytes=56 * 1024 * 1024),
        name="attend",
    )(low, cosine, sine, x, w_qkv, gains, w_output, w_gate, w_up, w_down_t)


FEED = 256


def middle_kernel(bits, groups, low_ref, cosine, sine, gains_ref, att_ref, lse_ref,
                  x_in, g_in, q_in, kv_in, wo_in, gate_in, up_in, down_in,
                  out_ref, dx_ref, branch_ref, row_ref, gate_out, up_out, down_out, dq_out, dkv_out,
                  ring, ring_down, far_in, sib_in, far_y, own_y, next_in, halo_send, halo_recv, feed_sem, load_sem, *scratch):
    own = x_in.shape[1]
    half_ff = gate_in.shape[1] // 2
    chunks = half_ff // FEED
    dp, y = place()
    core = dp % 2
    k = dp // 2
    j = 2 * core + y
    j_y = 2 * core + 1 - y
    has_prev, has_next = k > 0, k < groups - 1
    first_core, last_core = core == 0, core == 1
    half = D // 4
    sums = Sums(bits, [None, None], down_in, [gate_out, up_out, down_out], scratch, (ring, ring_down))

    barrier = pltpu.get_barrier_semaphore()
    for partner in sums.partners:
        pl.semaphore_signal(barrier, inc=1, device_id=partner, device_id_type=MESH)

    @pl.when(has_next)
    def _():
        pl.semaphore_signal(barrier, inc=1, device_id=(dp + 2, y), device_id_type=MESH)

    spots = 5
    begins = {0: (-1, 1, 2), 1: (0, 1, 2), 2: (1, 1, 2), 3: (3, 0, 1), 4: (4, 0, 1)}
    events = {(0, 0): [(sums.start_y, a, chunks - 2) for a in range(3)], (0, 2): [(sums.start_y, a, chunks - 1) for a in range(3)]}
    for n in range(chunks):
        turn, spot, lag = begins[n]
        for s in range(len(sums.stages)):
            for a in range(3):
                at = turn * spots + spot + a + lag * s
                events.setdefault((at // spots, at % spots), []).insert(0, (sums.stages[s], a, n))
    last_round = max(turn for turn, spot in events)

    def advance(p, h):
        if isinstance(h, int):
            for step, a, n in events.get((h, p), ()):
                step(a, n)
            return
        for turn in range(KV_HEADS):
            if (turn, p) in events:
                pl.when(h == turn)(lambda turn=turn: advance(p, turn))

    def feed_phase(weights, wo, h_t, g_t, x, h, g, acc):
        def load(n, s):
            cols = pl.ds(pl.multiple_of(s * half_ff + n * FEED, 128), FEED)
            return [pltpu.make_async_copy(w.at[:, cols], weights.at[s, i], feed_sem.at[s, i])
                    for i, w in enumerate((gate_in, up_in, down_in))]

        first = [pltpu.make_async_copy(a, b, load_sem.at[i]) for i, (a, b) in enumerate(((x_in, h_t), (g_in, g_t), (wo_in, wo)))]
        for copy in first + load(0, 0):
            copy.start()
        for copy in first:
            copy.wait()
        gain = gains_ref[:, 1:2].astype(F32)
        x[...] = h_t[...].astype(F32) + over_first(wo[...], att_ref[...])
        scale = lax.rsqrt(jnp.mean(x[...] * x[...], axis=0, keepdims=True) + EPSILON)
        h_t[...] = (x[...] * scale * gain).astype(BF16)
        h[...] = h_t[...].T
        g[...] = g_t[...].T
        acc[...] = x[...]
        dx_ref[...] = jnp.zeros(dx_ref.shape, F32)

        @pl.when(has_prev)
        def _():
            pl.semaphore_wait(barrier, len(sums.partners) + 1)

        @pl.when(jnp.logical_not(has_prev))
        def _():
            pl.semaphore_wait(barrier, len(sums.partners))

        def step(n, s):
            for copy in load(n, s):
                copy.wait()
            if s == 0:
                for copy in load(n, 1):
                    copy.start()
            else:
                @pl.when(n < chunks - 1)
                def _():
                    for copy in load(n + 1, 0):
                        copy.start()

            w_gate, w_up, w_down = weights[s, 0], weights[s, 1], weights[s, 2]
            gate = dot(h[...], w_gate)
            upper = dot(h[...], w_up)
            dm = dot(g[...], w_down)
            sigmoid = 1.0 / (1.0 + jnp.exp(-gate))
            active = gate * sigmoid
            inner = (active * upper).astype(BF16)
            dgate = (dm * upper * sigmoid * (1.0 + gate * (1.0 - sigmoid))).astype(BF16)
            dup = (dm * active).astype(BF16)
            acc[...] += against_rows(w_down, inner)
            dx_ref[...] += against_rows(w_gate, dgate) + against_rows(w_up, dup)
            cols = slice(s * FEED, (s + 1) * FEED)
            for c, shares in ((core, sums.own_share), (1 - core, sums.sibling_share)):
                for which in range(2):
                    rows = pl.ds(pl.multiple_of(which * 2 * half + c * half, 16), half)
                    left = h_t[rows, :]
                    for a, right in enumerate((dgate, dup)):
                        shares(a, n)[which, :, cols] = dot(left, right).astype(BF16)
                rows = pl.ds(pl.multiple_of(c * 2 * half, 16), 2 * half)
                shares(2, n)[s] = dot(g_t[rows, :], inner).astype(BF16)

        def round_of(n, carry):
            @pl.when(n > 1)
            def _():
                for a in range(3):
                    sums.core_sent(a, n - 2)

            step(n, 0)

            @pl.when(jnp.logical_and(n > 0, n < chunks - 1))
            def _():
                for a in range(3):
                    sums.start_y(a, n - 1)

            pl.when(n == chunks - 1)(lambda: (advance(1, -1), advance(2, -1))[0])
            step(n, 1)
            for a in range(3):
                sums.start_core(a, n)
            pl.when(n == chunks - 1)(lambda: (advance(3, -1), advance(4, -1))[0])
            return carry

        lax.fori_loop(0, chunks, round_of, 0)
        out_ref[...] = acc[...].astype(BF16)
        dh = dx_ref[...]
        acc[...] = dh * (x[...] * scale)
        ones = jnp.ones((8, own), F32)
        row_ref[...] = lax.dot_general(ones, acc[...], (((1,), (1,)), ((), ())), precision=lax.Precision.HIGHEST,
                                       preferred_element_type=F32)
        mean = jnp.sum(acc[...] * gain, axis=0, keepdims=True) * (1.0 / D)
        dx = g_t[...].astype(F32) + scale * (dx_ref[...] * gain - x[...] * scale * mean)
        dx_ref[...] = dx
        branch_ref[...] = dx.astype(BF16)

    pl.run_scoped(
        feed_phase,
        pltpu.VMEM((2, 3, D, FEED), BF16),
        pltpu.VMEM((D, D), BF16),
        pltpu.VMEM((D, own), BF16),
        pltpu.VMEM((D, own), BF16),
        pltpu.VMEM((D, own), F32),
        pltpu.VMEM((own, D), BF16),
        pltpu.VMEM((own, D), BF16),
        pltpu.VMEM((D, own), F32),
    )
    for n in (chunks - 2, chunks - 1):
        for a in range(3):
            sums.core_sent(a, n)

    blocks = own // CHUNK
    third = GROUP * CHUNK

    def attention_phase(wo, q, do, kv, q_all, do_all, q_rows, do_rows, delta, dq_acc, p_all, ds_all, part, dq, dkv):
        first = [pltpu.make_async_copy(a, b, load_sem.at[i]) for i, (a, b) in enumerate(((wo_in, wo), (q_in, q)))]

        def window(h, at):
            return pltpu.make_async_copy(kv_in.at[h], kv.at[at], feed_sem.at[at, 0])

        for copy in first + [window(0, 0)]:
            copy.start()
        part[...] = jnp.zeros(part.shape, BF16)
        for copy in first:
            copy.wait()
        do[...] = dot(wo[...], branch_ref[...]).astype(BF16)

        def slot(h, n):
            return part.at[h, pl.ds(pl.multiple_of(n * own, own), own), :]

        def halo(route, h):
            before = jnp.maximum(dp - 2, 0)
            sems = (halo_send.at[route, h], halo_recv.at[route, h])
            if route == PASS_PREV:
                return Route(slot(h, j_y + 2 - 4 * core), far_in.at[h], *sems, sums.sibling)
            if route == PASS_OWN:
                return Route(slot(h, 2 + j_y), far_in.at[h], *sems, sums.sibling)
            if route == PREV_SIB:
                return Route(slot(h, j + 2 - 4 * core), sib_in.at[h], *sems, sums.sibling)
            if route == OWN_SIB:
                return Route(slot(h, 2 + j), sib_in.at[h], *sems, sums.sibling)
            if route == PREV_Y:
                return Route(slot(h, j_y), far_y.at[h], *sems, sums.over_y)
            if route == OWN_Y:
                return Route(slot(h, 4 + j_y), own_y.at[h], *sems, sums.over_y)
            return Route(slot(h, j), next_in.at[h], *sems, (before, y))

        got_if = {
            OWN_SIB: first_core, OWN_Y: j != 3, OWN_NEXT: has_next, PASS_OWN: first_core,
            PREV_SIB: jnp.logical_and(last_core, has_prev), PREV_Y: jnp.logical_and(j != 0, has_prev),
            PASS_PREV: jnp.logical_and(last_core, has_prev),
        }
        sent_if = {
            OWN_SIB: last_core, OWN_Y: j != 2, OWN_NEXT: has_prev, PASS_OWN: last_core,
            PREV_SIB: jnp.logical_and(first_core, has_prev), PREV_Y: jnp.logical_and(j != 1, has_prev),
            PASS_PREV: jnp.logical_and(first_core, has_prev),
        }

        def start(route, h):
            pl.when(sent_if[route])(lambda: halo(route, h).start())

        def take(route, h, n, box):
            @pl.when(got_if[route])
            def _():
                halo(route, h).arrived()
                spot = slot(h, n)
                spot[...] = spot[...] + box[h]

        def return_one(h):
            for route in (PASS_PREV, PASS_OWN, PREV_SIB, OWN_SIB):
                start(route, h)

        def return_two(h):
            take(PASS_PREV, h, j_y, far_in)
            take(PASS_OWN, h, 4 + j_y, far_in)
            start(PREV_Y, h)
            start(OWN_Y, h)

        def return_three(h):
            for route, n, box in ((PREV_SIB, j, sib_in), (OWN_SIB, 4 + j, sib_in), (PREV_Y, j, far_y), (OWN_Y, 4 + j, own_y)):
                take(route, h, n, box)
            start(OWN_NEXT, h)

        def return_four(h):
            dkv[h] = slot(h, 4 + j)[...].astype(F32)

            @pl.when(has_next)
            def _():
                halo(OWN_NEXT, h).arrived()
                dkv[h] = dkv[h] + next_in[h].astype(F32)

        def head_rows(h, r):
            return pl.ds(pl.multiple_of(h * GROUP * HEAD_DIM + r * HEAD_DIM, HEAD_DIM), HEAD_DIM)

        def prepare(h):
            for r in range(GROUP):
                rows = head_rows(h, r)
                for b in range(blocks):
                    cols = pl.ds(b * third + r * CHUNK, CHUNK)
                    from_cols = slice(b * CHUNK, (b + 1) * CHUNK)
                    grad, queries = do[rows, from_cols], q[rows, from_cols]
                    q_all[:, cols] = queries
                    do_all[:, cols] = grad
                    q_rows[cols, :] = queries.T
                    do_rows[cols, :] = grad.T
                    delta[:, cols] = jnp.sum(grad.astype(F32) * att_ref[rows, from_cols].astype(F32), axis=0, keepdims=True)
            dq_acc[...] = jnp.zeros(dq_acc.shape, F32)

        def block(h, at, n, spans, diagonal):
            both = kv[at, n * own : (n + 1) * own, :]
            keys, values = both[:, :HEAD_DIM], both[:, HEAD_DIM:]
            begin_at = (n - 4) * own
            for i in range(own // CHUNK):
                row = i * CHUNK
                some_keys, some_values = keys[row : row + CHUNK], values[row : row + CHUNK]
                using = [b for b in range(blocks) if spans[b][0] <= row < spans[b][1]]
                for b in using:
                    low = low_ref[:, b * CHUNK : (b + 1) * CHUNK]
                    for r in range(GROUP):
                        cols = pl.ds(b * third + r * CHUNK, CHUNK)
                        lse = lse_ref[h, r : r + 1, b * CHUNK : (b + 1) * CHUNK]
                        s = masked(dot(some_keys, q_all[:, cols]), begin_at + row, low, b * CHUNK if diagonal and b == i else None)
                        p = jnp.exp2(s * SCALE2 - lse)
                        p_all[:, cols] = p.astype(BF16)
                        ds_all[:, cols] = (p * (dot(some_values, do_all[:, cols]) - delta[:, cols])).astype(BF16)
                cols = pl.ds(using[0] * third, len(using) * third)
                dq_acc[:, cols] += dot(some_keys.T, ds_all[:, cols])
                dk = dot(ds_all[:, cols], q_rows[cols, :]) * 0.125
                dv = dot(p_all[:, cols], do_rows[cols, :])
                spot = pl.ds(pl.multiple_of((n + j) * own + row, CHUNK), CHUNK)
                part[h, spot, :] = jnp.concatenate([dk, dv], axis=1).astype(BF16)

        every = [(0, own)] * blocks
        plan = [(0, [(b * CHUNK, own) for b in range(blocks)], False), (1, every, False), (2, every, False),
                (3, every, False), (4, [(0, (b + 1) * CHUNK) for b in range(blocks)], True)]
        def guarded(fn, h):
            pl.when(jnp.logical_and(h >= 0, h < KV_HEADS))(lambda: fn(h))

        def head(h, carry):
            at = h % 2
            window(h, at).wait()

            @pl.when(h < KV_HEADS - 1)
            def _():
                window(h + 1, 1 - at).start()

            prepare(h)
            for p in range(spots):
                block(h, at, *plan[p])
                advance(p, h)
                if p == 1:
                    guarded(return_two, h - 1)
                if p == 4:
                    guarded(return_three, h - 3)
            return_one(h)
            for r in range(GROUP):
                rows = head_rows(h, r)
                for b in range(blocks):
                    value = dq_acc[:, pl.ds(b * third + r * CHUNK, CHUNK)] * 0.125
                    spot = slice(b * CHUNK, (b + 1) * CHUNK)
                    cos, sin = cosine[:, spot], sine[:, spot]
                    one, two = value[: HEAD_DIM // 2], value[HEAD_DIM // 2 :]
                    back = jnp.concatenate([one * cos + two * sin, two * cos - one * sin], axis=0)
                    dq[rows, spot] = back.astype(BF16)
            return carry

        lax.fori_loop(0, KV_HEADS, head, 0)
        last = KV_HEADS - 1
        after = [(return_two, last), (return_three, 2), (return_three, 3), (return_four, 0), (return_four, 1),
                 (return_three, last), (return_four, 2), (return_four, 3)]
        for i in range((last_round - KV_HEADS + 1) * spots):
            if i < len(after):
                fn, h = after[i]
                fn(h)
            advance(i % spots, KV_HEADS + i // spots)
        for fn, h in after[(last_round - KV_HEADS + 1) * spots :]:
            fn(h)
        return_four(last)
        stores = [pltpu.make_async_copy(dq, dq_out, load_sem.at[0]), pltpu.make_async_copy(dkv, dkv_out, load_sem.at[1])]
        for store in stores:
            store.start()

        def finish(h, carry):
            for route in range(7):
                pl.when(sent_if[route])(lambda route=route: halo(route, h).sent())
            return carry

        lax.fori_loop(0, KV_HEADS, finish, 0)
        for store in stores:
            store.wait()

    width = GROUP * own
    pl.run_scoped(
        attention_phase,
        pltpu.VMEM((D, D), BF16),
        pltpu.VMEM((D, own), BF16),
        pltpu.VMEM((D, own), BF16),
        pltpu.VMEM((2, 5 * own, 2 * HEAD_DIM), BF16),
        pltpu.VMEM((HEAD_DIM, width), BF16),
        pltpu.VMEM((HEAD_DIM, width), BF16),
        pltpu.VMEM((width, HEAD_DIM), BF16),
        pltpu.VMEM((width, HEAD_DIM), BF16),
        pltpu.VMEM((1, width), F32),
        pltpu.VMEM((HEAD_DIM, width), F32),
        pltpu.VMEM((CHUNK, width), BF16),
        pltpu.VMEM((CHUNK, width), BF16),
        pltpu.VMEM((KV_HEADS, 8 * own, 2 * HEAD_DIM), BF16),
        pltpu.VMEM((D, own), BF16),
        pltpu.VMEM((KV_HEADS, own, 2 * HEAD_DIM), F32),
    )

    def drain(n, carry):
        for a in range(3):
            sums.drain(a, n)
        return carry

    lax.fori_loop(0, chunks, drain, 0)


def middle_and_back(low, cosine, sine, gains, attended, lse, x, cotangent, queries, both, w_output, w_gate, w_up, w_down_t,
           dp_size):
    own = x.shape[1]
    ff = w_gate.shape[1]
    bits = dp_size.bit_length() - 1
    half = D // 4
    chunks = ff // WIDE
    any_spec = pl.BlockSpec(memory_space=pl.ANY)
    vmem = pl.BlockSpec(memory_space=pltpu.VMEM)
    box = pltpu.VMEM((KV_HEADS, own, 2 * HEAD_DIM), BF16)
    return pl.pallas_call(
        functools.partial(middle_kernel, bits, dp_size // 2),
        out_shape=[
            jax.ShapeDtypeStruct((D, own), BF16),
            jax.ShapeDtypeStruct((D, own), F32),
            jax.ShapeDtypeStruct((D, own), BF16),
            jax.ShapeDtypeStruct((8, D), F32),
            jax.ShapeDtypeStruct((D // 2, ff), BF16),
            jax.ShapeDtypeStruct((D // 2, ff), BF16),
            jax.ShapeDtypeStruct((D, ff // 2), BF16),
            jax.ShapeDtypeStruct((D, own), BF16),
            jax.ShapeDtypeStruct((KV_HEADS, own, 2 * HEAD_DIM), F32),
        ],
        in_specs=[vmem] * 6 + [any_spec] * 8,
        out_specs=[vmem] * 4 + [any_spec] * 5,
        scratch_shapes=[
            pltpu.VMEM((2, 2, 2, half, WIDE), BF16),
            pltpu.VMEM((2, 2, 2 * half, FEED), BF16),
            box, box, box, box, box,
            pltpu.SemaphoreType.DMA((7, KV_HEADS)),
            pltpu.SemaphoreType.DMA((7, KV_HEADS)),
            pltpu.SemaphoreType.DMA((2, 3)),
            pltpu.SemaphoreType.DMA((3,)),
        ] + Sums.scratch(bits, 2, 1, chunks, half),
        compiler_params=pltpu.CompilerParams(
            collective_id=3, has_side_effects=True, vmem_limit_bytes=60 * 1024 * 1024),
        name="middle",
    )(low, cosine, sine, gains, attended, lse, x, cotangent, queries, both, w_output, w_gate, w_up, w_down_t)


def finish_kernel(bits, chunks, dq, dkv, cosine, sine, hidden, x, scale, gains, w_qkv, attended, branch, middle, feed_row,
                  out, gains_out, tokens_out, pack, grads, prod, *rest):
    sums = Sums(bits, [pack], None, [out], rest[:-5])
    g_loc, g_in, g_sem, g_send, g_recv = rest[-5:]
    half = HEAD_DIM // 2
    rows = pack.shape[1]
    greet(sums.partners)

    def gain_route(n):
        return Route(g_loc.at[n], g_in.at[n], g_send.at[n], g_recv.at[n], sums.partners[n])

    def unrotate(values, at):
        one, two = values[:half], values[half:]
        cos, sin = cosine[...], sine[...]
        grads[at : at + half, :] = (one * cos + two * sin).astype(BF16)
        grads[at + half : at + HEAD_DIM, :] = (two * cos - one * sin).astype(BF16)

    def columns(low, high):
        parts = []
        if low < D:
            parts.append((attended, branch, low, min(high, D)))
        if high > D:
            parts.append((hidden, grads, max(low, D) - D, high - D))
        return [against_rows(left[...], right[a:b, :]) for left, right, a, b in parts]

    def fill(n):
        parts = columns(n * WIDE, (n + 1) * WIDE)
        value = parts[0] if len(parts) == 1 else jnp.concatenate(parts, axis=1)
        value = value.astype(BF16)
        for which in range(2):
            pack[which, :, n * WIDE : (n + 1) * WIDE] = value[which * rows : (which + 1) * rows]
        sums.start_core(0, n)

    def heads():
        grads[:D, :] = dq[...]
        for h in range(KV_HEADS):
            both = dkv[h].T
            unrotate(both[:HEAD_DIM], D + h * HEAD_DIM)
            at = D + (KV_HEADS + h) * HEAD_DIM
            grads[at : at + HEAD_DIM, :] = both[HEAD_DIM:].astype(BF16)

    def hidden_grad():
        keys_values = 2 * KV_HEADS * HEAD_DIM
        dh = dot(w_qkv[:, keys_values:], grads[:D, :]) + dot(w_qkv[:, :keys_values], grads[D:, :])
        tokens_out[...] = dh
        prod[...] = dh * (x[...].astype(F32) * scale[...])
        g_loc[0] = jnp.zeros(g_loc.shape[1:], F32)
        ones = jnp.ones((8, dh.shape[1]), F32)
        total = lax.dot_general(ones, prod[...], (((1,), (1,)), ((), ())), precision=lax.Precision.HIGHEST,
                                preferred_element_type=F32)
        g_loc[0, 0:1, :] = total[0:1]
        g_loc[0, 1:2, :] = feed_row[0:1, :]
        gain_route(0).start()

    def tokens_grad():
        normed = x[...].astype(F32) * scale[...]
        gain = gains[:, 0:1].astype(F32)
        e = tokens_out[...] * gain
        mean = jnp.sum(prod[...] * gain, axis=0, keepdims=True) * (1.0 / D)
        tokens_out[...] = middle[...] + scale[...] * (e - normed * mean)

    def gain_step(n):
        gain_route(n - 1).arrived()
        g_loc[n] = g_loc[n - 1] + g_in[n - 1]
        if n < len(sums.partners):
            gain_route(n).start()

    work = [lambda: fill(0), lambda: (heads(), fill(1))] + [functools.partial(fill, n) for n in range(2, chunks)]
    work += [hidden_grad, tokens_grad] + [functools.partial(gain_step, n + 1) for n in range(len(sums.partners))]
    steps = [sums.start_y] + sums.stages
    delay = [1, 3]
    while len(delay) < len(steps):
        delay.append(delay[-1] + 1)
    for tick in range(max(chunks + delay[-1], len(work))):
        if tick < len(work):
            work[tick]()
        for s in [0] + list(range(len(steps) - 1, 0, -1)):
            if 0 <= tick - delay[s] < chunks:
                steps[s](0, tick - delay[s])
    store = pltpu.make_async_copy(g_loc.at[len(sums.partners)], gains_out, g_sem.at[0])
    store.start()
    for n in range(chunks):
        sums.core_sent(0, n)
        sums.drain(0, n)
    for n in range(len(sums.partners)):
        gain_route(n).sent()
    store.wait()


def finish(dq, dkv, cosine, sine, hidden, x, scale, gains, w_qkv, attended, branch, middle, feed_row, dp_size):
    bits = dp_size.bit_length() - 1
    own = x.shape[1]
    total = 2 * D + 2 * KV_HEADS * HEAD_DIM
    chunks = total // WIDE
    any_spec = pl.BlockSpec(memory_space=pl.ANY)
    vmem = pl.BlockSpec(memory_space=pltpu.VMEM)
    row = (8, D)
    return pl.pallas_call(
        functools.partial(finish_kernel, bits, chunks),
        out_shape=[
            jax.ShapeDtypeStruct((D // 2, total), BF16),
            jax.ShapeDtypeStruct(row, F32),
            jax.ShapeDtypeStruct((D, own), F32),
        ],
        in_specs=[vmem] * 13,
        out_specs=[any_spec, any_spec, vmem],
        scratch_shapes=[
            pltpu.VMEM((2, D // 2, total), BF16),
            pltpu.VMEM((total - D, own), BF16),
            pltpu.VMEM((D, own), F32),
        ] + Sums.scratch(bits, 1, 0, chunks, D // 4) + [
            pltpu.VMEM((bits + 2,) + row, F32),
            pltpu.VMEM((bits + 1,) + row, F32),
            pltpu.SemaphoreType.DMA((1,)),
            pltpu.SemaphoreType.DMA((bits + 1,)),
            pltpu.SemaphoreType.DMA((bits + 1,)),
        ],
        compiler_params=pltpu.CompilerParams(
            collective_id=0, has_side_effects=True, vmem_limit_bytes=56 * 1024 * 1024),
        name="finish",
    )(dq, dkv, cosine, sine, hidden, x, scale, gains, w_qkv, attended, branch, middle, feed_row)


def positions(seq_lengths, first, count):
    ends = jnp.cumsum(seq_lengths)
    index = first + jnp.arange(count, dtype=jnp.int32)
    passed = index[:, None] >= ends[None, :]
    begin = jnp.max(jnp.where(passed, ends[None, :], 0), axis=1)
    return index - begin


def rotary_tables(position):
    half = HEAD_DIM // 2
    inverse = jnp.exp(-jnp.arange(half, dtype=F32) * (2.0 / HEAD_DIM) * jnp.log(THETA))
    angle = inverse[:, None] * position.astype(F32)[None, :]
    return jnp.cos(angle), jnp.sin(angle)


def shards(tokens, cotangent, w_query, w_key, w_value, w_output, w_gate, w_up, w_down, attention_gain, feed_gain, seq_lengths):
    own = tokens.shape[0]
    kv = KV_HEADS * HEAD_DIM
    first = lax.axis_index(("dp", "shard")) * own
    position = positions(seq_lengths, first, own)
    low = jnp.arange(own, dtype=jnp.int32) - position
    cosine, sine = rotary_tables(position)
    gains = jnp.where(jnp.arange(128)[None, :] == 0, attention_gain[:, None], feed_gain[:, None])
    dp_size = lax.axis_size("dp")
    (attended, log_total, queries, hidden_one, scale_one, gains, both_all,
     qkv_full, output_full, gate_full, up_full, down_full) = attend(
        low[None, :], cosine, sine, tokens.T, jnp.concatenate([w_key, w_value, w_query], axis=1), gains,
        w_output, w_gate, w_up, w_down.T, dp_size
    )
    output, grad_middle, grad_branch, feed_rows, sum_gate, sum_up, sum_down, grad_queries, grad_own = middle_and_back(
        low[None, :], cosine, sine, gains, attended, log_total, tokens.T, cotangent.T, queries,
        both_all, output_full, gate_full, up_full, down_full, dp_size
    )
    sum_pack, sum_gains, grad_tokens = finish(
        grad_queries, grad_own, cosine, sine, hidden_one, tokens.T, scale_one, gains, qkv_full,
        attended, grad_branch, grad_middle, feed_rows, dp_size
    )
    sum_pack = sum_pack.astype(F32)
    half = D // 2
    begin = lax.axis_index("shard") * half
    return (
        output.T,
        grad_tokens.T,
        sum_pack[:, D : 2 * D],
        sum_pack[:, 2 * D : 2 * D + kv],
        sum_pack[:, 2 * D + kv :],
        sum_pack[:, :D],
        sum_gate.astype(F32),
        sum_up.astype(F32),
        sum_down.astype(F32).T,
        lax.dynamic_slice_in_dim(sum_gains[0], begin, half),
        lax.dynamic_slice_in_dim(sum_gains[1], begin, half),
    )


def solution(mesh):
    return jax.shard_map(
        shards,
        mesh=mesh,
        in_specs=(
            P(("dp", "shard"), None),
            P(("dp", "shard"), None),
            P("shard", None),
            P("shard", None),
            P("shard", None),
            P("shard", None),
            P("shard", None),
            P("shard", None),
            P("shard", None),
            P("shard"),
            P("shard"),
            P(),
        ),
        out_specs=(
            P(("dp", "shard"), None),
            P(("dp", "shard"), None),
            P("shard", None),
            P("shard", None),
            P("shard", None),
            P("shard", None),
            P("shard", None),
            P("shard", None),
            P("shard", None),
            P("shard"),
            P("shard"),
        ),
        check_vma=False,
    )
```

```python
import functools

import jax
import jax.numpy as jnp
from jax import lax
from jax.experimental import pallas as pl
from jax.experimental.pallas import tpu as pltpu
from jax.sharding import PartitionSpec as P

D = 960
HEADS = 15
KV_HEADS = 5
GROUP = 3
HEAD_DIM = 64

EPSILON = 1e-05
THETA = 100000.0
MASKED = -1e30
LOG2E = 1.4426950408889634
SCALE2 = 0.125 * LOG2E

MESH = pl.DeviceIdType.MESH
WIDE = 512
CHUNK = 256
STRIP = 128
BF16 = jnp.bfloat16
F32 = jnp.float32


def dot(left, right):
    return lax.dot_general(left, right, (((1,), (0,)), ((), ())), preferred_element_type=F32)


def against_rows(left, right):
    return lax.dot_general(left, right, (((1,), (1,)), ((), ())), preferred_element_type=F32)


def over_first(left, right):
    return lax.dot_general(left, right, (((0,), (0,)), ((), ())), preferred_element_type=F32)


def masked(scores, start, low, diagonal):
    rows = start + lax.broadcasted_iota(jnp.int32, scores.shape, 0)
    valid = rows >= low
    if diagonal is not None:
        cols = diagonal + lax.broadcasted_iota(jnp.int32, scores.shape, 1)
        valid = jnp.logical_and(valid, rows <= cols)
    return jnp.where(valid, scores, MASKED)


def place():
    return lax.axis_index("dp"), lax.axis_index("shard")


def other(dp, y, bit):
    step = 1 << bit
    mine = (dp // step) % 2
    return (dp + step - 2 * step * mine, y)


def greet(partners):
    barrier = pltpu.get_barrier_semaphore()
    for partner in partners:
        pl.semaphore_signal(barrier, inc=1, device_id=partner, device_id_type=MESH)
    pl.semaphore_wait(barrier, len(partners))


class Route:
    def __init__(self, src, dst, send, recv, partner):
        self.make = lambda: pltpu.make_async_remote_copy(
            src_ref=src, dst_ref=dst, send_sem=send, recv_sem=recv, device_id=partner, device_id_type=MESH)

    def start(self):
        self.make().start()

    def arrived(self):
        self.make().wait_recv()

    def sent(self):
        self.make().wait_send()


class Sums:
    def __init__(self, bits, wides, tall, outs, scratch, rings=None, early=()):
        self.wides, self.tall, self.outs, self.rings, self.early = wides, tall, outs, rings, early
        self.boxes = [scratch[:7]] * len(wides) + [scratch[7:14]] * (tall is not None)
        self.put_sem, self.send_sem, self.recv_sem = scratch[-3:]
        self.arrays = len(self.boxes)
        self.half = D // 4
        dp, y = place()
        self.core, self.x, self.z, self.y = dp % 2, (dp // 2) % 2, (dp // 4) % 2, y
        self.sibling, self.over_y = other(dp, y, 0), (dp, 1 - y)
        self.over_x, self.over_z = other(dp, y, 1), other(dp, y, 2)
        self.extra = [other(dp, y, bit) for bit in range(3, bits)]
        self.partners = [self.sibling, self.over_y, self.over_x, self.over_z] + self.extra
        more = len(self.extra)
        self.stages = [self.start_x, self.start_z]
        self.stages += [functools.partial(self.more, step) for step in range(more + 1)]
        self.stages += [self.back_x, self.back_core, self.finish]

    @staticmethod
    def scratch(bits, wide_arrays, tall, chunks, half):
        more = bits - 3
        count = wide_arrays + tall

        def boxes(n, shapes):
            return [pltpu.VMEM((n, chunks) + shape, BF16) for shape in shapes]

        shared = [(half, 128), (max(more, 1), half, 128)]
        out = []
        if wide_arrays:
            out += boxes(wide_arrays, [(2, half, WIDE)] * 2 + [(half, WIDE), (half, 256)] + shared + [(2 * half, WIDE)])
        else:
            out += [None] * 7
        if tall:
            out += boxes(1, [(2, 2 * half, 256)] * 2 + [(2 * half, 256), (half, 256)] + shared + [(4 * half, 256)])
        return out + [
            pltpu.SemaphoreType.DMA((2, count, chunks)),
            pltpu.SemaphoreType.DMA((9 + more, count, chunks)),
            pltpu.SemaphoreType.DMA((9 + more, count, chunks)),
        ]

    def box(self, which, a, n):
        return self.boxes[a][which].at[0 if self.is_tall(a) else a, n]

    def is_tall(self, a):
        return a == len(self.wides)

    def own_share(self, a, n):
        return self.box(0, a, n)

    def sibling_share(self, a, n):
        ring = self.rings[1 if self.is_tall(a) else 0]
        return ring.at[n % 2] if self.is_tall(a) else ring.at[n % 2, a]

    def source(self, a, n, c, which):
        rows = pl.ds(pl.multiple_of(c * self.half, 16), self.half)
        return self.wides[a].at[which, rows, pl.ds(pl.multiple_of(n * WIDE, 128), WIDE)]

    def is_early(self, a, n):
        return isinstance(n, int) and (a, n) in self.early

    def axes(self, a, n):
        x, z = (self.x, self.over_x), (self.z, self.over_z)
        return (z, x) if self.is_early(a, n) else (x, z)

    def first_part(self, a, which):
        if self.is_tall(a):
            return pl.ds(pl.multiple_of(which * self.half, 16), self.half), slice(None)
        return slice(None), pl.ds(pl.multiple_of(which * 256, 128), 256)

    def second_part(self, which):
        return slice(None), pl.ds(pl.multiple_of(which * 128, 128), 128)

    def back_at(self, a, c, x=None, z=None):
        half = self.half
        if self.is_tall(a):
            if x is None:
                return pl.ds(pl.multiple_of(c * 2 * half, 16), 2 * half), slice(None)
            rows = pl.ds(pl.multiple_of(c * 2 * half + x * half, 16), half)
            return rows, slice(None) if z is None else pl.ds(pl.multiple_of(z * 128, 128), 128)
        rows = pl.ds(pl.multiple_of(c * half, 16), half)
        if x is None:
            return rows, slice(None)
        if z is None:
            return rows, pl.ds(pl.multiple_of(x * 256, 128), 256)
        return rows, pl.ds(pl.multiple_of(x * 256 + z * 128, 128), 128)

    def route(self, stage, a, n, src, dst, partner):
        return Route(src, dst, self.send_sem.at[stage, a, n], self.recv_sem.at[stage, a, n], partner)

    def copy(self, stage, a, n):
        loc, core_in, y_in, x_in, z_in, more_in, back = (self.box(i, a, n) for i in range(7))
        (first, over_first), (second, over_second) = self.axes(a, n)
        early = self.is_early(a, n)
        more = len(self.extra)
        if stage < 2:
            leaving = self.sibling_share(a, n).at[stage] if self.rings else self.source(a, n, 1 - self.core, stage)
            return self.route(stage, a, n, leaving, core_in.at[stage], self.sibling)
        if early and stage in (2, 8 + more):
            which = 0 if stage == 2 else 1
            return self.route(stage, a, n, loc.at[(which,) + self.first_part(a, 1 - first)],
                              y_in.at[:, pl.ds(which * 256, 256)], over_first)
        if early and stage == 3:
            return self.route(stage, a, n, loc.at[(1 - self.y,) + self.first_part(a, first)], x_in, self.over_y)
        if stage == 2:
            return self.route(stage, a, n, loc.at[1 - self.y], y_in, self.over_y)
        if stage == 3:
            return self.route(stage, a, n, y_in.at[self.first_part(a, 1 - first)], x_in, over_first)
        if stage == 4:
            return self.route(stage, a, n, x_in.at[self.second_part(1 - second)], z_in, over_second)
        if stage < 5 + more:
            so_far = z_in if stage == 5 else more_in.at[stage - 6]
            return self.route(stage, a, n, so_far, more_in.at[stage - 5], self.extra[stage - 5])
        at = [(self.core, first, second), (self.core, first), (self.core,)][stage - 5 - more]
        part = back.at[self.back_at(a, *at)]
        return self.route(stage, a, n, part, part, (over_second, over_first, self.sibling)[stage - 5 - more])

    def puts(self, a, n):
        box, out = self.box(6, a, n), self.outs[a]
        if self.is_tall(a):
            return [pltpu.make_async_copy(box, out.at[:, pl.ds(pl.multiple_of(n * 256, 128), 256)], self.put_sem.at[0, a, n])]
        if not self.rings:
            return [pltpu.make_async_copy(box, out.at[:, pl.ds(pl.multiple_of(n * WIDE, 128), WIDE)], self.put_sem.at[0, a, n])]
        return [
            pltpu.make_async_copy(
                box.at[:, pl.ds(i * 256, 256)],
                out.at[:, pl.ds(pl.multiple_of(i * (out.shape[1] // 2) + n * 256, 128), 256)],
                self.put_sem.at[i, a, n])
            for i in range(2)
        ]

    def start_core(self, a, n):
        for which in range(2):
            self.copy(which, a, n).start()

    def core_sent(self, a, n):
        for which in range(2):
            self.copy(which, a, n).sent()

    def start_y(self, a, n):
        loc, core_in = self.box(0, a, n), self.box(1, a, n)
        for which in range(2):
            self.copy(which, a, n).arrived()
            mine = loc.at[which] if self.rings else self.source(a, n, self.core, which)
            loc[which] = mine[...] + core_in[which]
        self.copy(2, a, n).start()
        if self.is_early(a, n):
            self.copy(8 + len(self.extra), a, n).start()

    def start_x(self, a, n):
        loc, y_in = self.box(0, a, n), self.box(2, a, n)
        self.copy(2, a, n).arrived()
        if self.is_early(a, n):
            self.copy(8 + len(self.extra), a, n).arrived()
            (first, _), _ = self.axes(a, n)
            for which in range(2):
                spot = (which,) + self.first_part(a, first)
                loc[spot] = loc[spot] + y_in[:, which * 256 : (which + 1) * 256]
        else:
            y_in[...] = y_in[...] + loc[self.y]
        self.copy(3, a, n).start()

    def start_z(self, a, n):
        loc, y_in, x_in = self.box(0, a, n), self.box(2, a, n), self.box(3, a, n)
        (first, _), _ = self.axes(a, n)
        self.copy(3, a, n).arrived()
        if self.is_early(a, n):
            x_in[...] = x_in[...] + loc[(self.y,) + self.first_part(a, first)]
        else:
            x_in[...] = x_in[...] + y_in[self.first_part(a, first)]
        self.copy(4, a, n).start()

    def more(self, step, a, n):
        x_in, z_in, more_in, back = (self.box(i, a, n) for i in range(3, 7))
        (first, _), (second, _) = self.axes(a, n)
        self.copy(4 + step, a, n).arrived()
        if step == 0:
            total = z_in
            value = z_in[...] + x_in[self.second_part(second)]
        else:
            total = more_in.at[step - 1]
            value = (z_in if step == 1 else more_in.at[step - 2])[...] + total[...]
        if step < len(self.extra):
            total[...] = value
        else:
            back[self.back_at(a, self.core, first, second)] = value
        self.copy(5 + step, a, n).start()

    def back_x(self, a, n):
        stage = 5 + len(self.extra)
        self.copy(stage, a, n).arrived()
        self.copy(stage + 1, a, n).start()

    def back_core(self, a, n):
        stage = 6 + len(self.extra)
        self.copy(stage, a, n).arrived()
        self.copy(stage + 1, a, n).start()

    def finish(self, a, n):
        self.copy(7 + len(self.extra), a, n).arrived()
        for put in self.puts(a, n):
            put.start()

    def drain(self, a, n):
        for stage in range(2, 8 + len(self.extra) + self.is_early(a, n)):
            self.copy(stage, a, n).sent()
        for put in self.puts(a, n):
            put.wait()


OWN_SIB, OWN_Y, OWN_NEXT, PASS_OWN, PREV_SIB, PREV_Y, PASS_PREV = range(7)
WEIGHT_CHUNKS = 5
FIRST_ROWS = (((0, 64), (64, 64)), ((128, 64), (192, 48)))


def forward_kernel(groups, low_ref, cosine, sine, x_ref, q_in, k_in, v_in, gains_in, wo_in, gate_in, up_in, down_in,
                   o_ref, lse_ref, q_ref, h_ref, scale_ref, gains, kv_out, qkv_out, wo_out, gate_out, up_out, down_out,
                   kv, kv_flip, w_qkv, wo, gate, up, down, top, acc, shrink, s_all, p_all,
                   kv_sem, load_sem, store_sem, send_sem, recv_sem, w_send, w_recv, wo_send, wo_recv, first_send, first_recv):
    dp, y = place()
    core, x, z = dp % 2, (dp // 2) % 2, (dp // 4) % 2
    k = dp // 2
    j = 2 * core + y
    j_y = 2 * core + 1 - y
    sibling, over_y, over_x, over_z = other(dp, y, 0), (dp, 1 - y), other(dp, y, 1), other(dp, y, 2)
    own = x_ref.shape[1]
    has_prev, has_next = k > 0, k < groups - 1
    first_core, last_core = core == 0, core == 1

    half, tall = gate_in.shape[0], down_in.shape[1]
    own_rows = pl.ds(pl.multiple_of(y * half, 16), half)
    own_cols = pl.ds(pl.multiple_of(y * tall, 128), tall)
    loads = [
        pltpu.make_async_copy(q_in, w_qkv.at[own_rows, pl.ds(2 * KV_HEADS * HEAD_DIM, D)], load_sem.at[0]),
        pltpu.make_async_copy(gains_in, gains.at[own_rows, :], load_sem.at[1]),
        pltpu.make_async_copy(gate_in, gate.at[own_rows, :], load_sem.at[2]),
        pltpu.make_async_copy(up_in, up.at[own_rows, :], load_sem.at[3]),
        pltpu.make_async_copy(down_in, down.at[:, own_cols], load_sem.at[4]),
        pltpu.make_async_copy(wo_in, wo.at[own_rows, :], load_sem.at[5]),
    ]
    flips = [pltpu.make_async_copy(w, kv_flip.at[i], load_sem.at[6 + i]) for i, w in enumerate((k_in, v_in))]
    for copy in flips + loads[:2]:
        copy.start()

    @pl.when(k == 0)
    def _():
        kv[:, : 4 * own, :] = jnp.zeros((KV_HEADS, 4 * own, 2 * HEAD_DIM), BF16)

    barrier = pltpu.get_barrier_semaphore()
    for partner in (sibling, over_y, over_x, over_z):
        pl.semaphore_signal(barrier, inc=1, device_id=partner, device_id_type=MESH)

    @pl.when(has_prev)
    def _():
        pl.semaphore_signal(barrier, inc=1, device_id=(dp - 2, y), device_id_type=MESH)

    @pl.when(has_next)
    def _():
        pl.semaphore_wait(barrier, 5)

    @pl.when(jnp.logical_not(has_next))
    def _():
        pl.semaphore_wait(barrier, 4)

    def slot(h, n):
        return kv.at[h, pl.ds(pl.multiple_of(n * own, own), own), :]

    def halo(route, h):
        after = jnp.minimum(dp + 2, 2 * groups - 1)
        sems = (send_sem.at[route, h], recv_sem.at[route, h])
        if route == OWN_SIB:
            return Route(slot(h, 4 + j), slot(h, 4 + j), *sems, sibling)
        if route == OWN_Y:
            return Route(slot(h, 4 + j), slot(h, 4 + j), *sems, over_y)
        if route == OWN_NEXT:
            return Route(slot(h, 4 + j), slot(h, j), *sems, (after, y))
        if route == PASS_OWN:
            return Route(slot(h, 4 + j_y), slot(h, 4 + j_y), *sems, sibling)
        if route == PREV_SIB:
            return Route(slot(h, j), slot(h, j), *sems, sibling)
        if route == PREV_Y:
            return Route(slot(h, j), slot(h, j), *sems, over_y)
        return Route(slot(h, j_y), slot(h, j_y), *sems, sibling)

    sent_if = {
        OWN_SIB: first_core, OWN_Y: j != 3, OWN_NEXT: has_next, PASS_OWN: first_core,
        PREV_SIB: jnp.logical_and(last_core, has_prev), PREV_Y: jnp.logical_and(j != 0, has_prev),
        PASS_PREV: jnp.logical_and(last_core, has_prev),
    }
    got_if = {
        OWN_SIB: last_core, OWN_Y: j != 2, OWN_NEXT: has_prev, PASS_OWN: last_core,
        PREV_SIB: jnp.logical_and(first_core, has_prev), PREV_Y: jnp.logical_and(j != 1, has_prev),
        PASS_PREV: jnp.logical_and(first_core, has_prev),
    }

    def start(route, h):
        pl.when(sent_if[route])(lambda: halo(route, h).start())

    def arrived(route, h):
        pl.when(got_if[route])(lambda: halo(route, h).arrived())

    def pass_one(h):
        arrived(OWN_Y, h)
        start(PASS_OWN, h)
        arrived(OWN_NEXT, h)
        start(PREV_SIB, h)
        start(PREV_Y, h)

    def pass_two(h):
        arrived(PREV_Y, h)
        start(PASS_PREV, h)

    part = half // 2

    def wide_at(which, n, width_from, width):
        rows = pl.ds(pl.multiple_of(which * half + core * part, 16), part)
        return rows, pl.ds(pl.multiple_of(n * WIDE + width_from, 128), width)

    def down_at(which, n, row_from, rows, col_from, cols):
        return (pl.ds(pl.multiple_of(row_from, 16), rows),
                pl.ds(pl.multiple_of(which * tall + n * 256 + col_from, 128), cols))

    def weights(stage, a, n):
        out = (gate, up, down)[a]
        which = y if stage == 0 else 1 - y
        rows = core * half
        if a < 2:
            size = [(z * 256 + x * 128, 128), (z * 256 + x * 128, 128), (z * 256, 256), (0, 512)][stage]
            region = out.at[wide_at(which, n, *size)]
        else:
            size = [(rows + z * part, part, x * 128, 128), (rows + z * part, part, x * 128, 128),
                    (rows + z * part, part, 0, 256), (rows, half, 0, 256)][stage]
            region = out.at[down_at(which, n, *size)]
        partner = (over_y, over_x, over_z, sibling)[stage]
        return Route(region, region, w_send.at[stage, a, n], w_recv.at[stage, a, n], partner)

    def hand_on(stage, a, n):
        weights(stage - 1, a, n).arrived()
        weights(stage, a, n).start()

    def store(a, n):
        if a < 2:
            cols = pl.ds(pl.multiple_of(n * WIDE, 128), WIDE)
            box, out = ((gate, gate_out), (up, up_out))[a]
            return [pltpu.make_async_copy(box.at[:, cols], out.at[:, cols], store_sem.at[a, n])]
        copies = []
        for which in range(2):
            some = pl.ds(pl.multiple_of(which * tall + n * 256, 128), 256)
            copies.append(pltpu.make_async_copy(down.at[:, some], down_out.at[:, some], store_sem.at[2 + which, n]))
        return copies

    def keep(a, n):
        weights(3, a, n).arrived()
        for copy in store(a, n):
            copy.start()

    def wo_part(which):
        return wo.at[pl.ds(pl.multiple_of(which * half + core * part, 16), part), :]

    wo_across = Route(wo_part(y), wo_part(y), wo_send.at[0], wo_recv.at[0], over_y)
    wo_within = Route(wo_part(1 - y), wo_part(1 - y), wo_send.at[1], wo_recv.at[1], sibling)
    wo_store = pltpu.make_async_copy(wo, wo_out, store_sem.at[0, WEIGHT_CHUNKS])

    def first(kind, i, which_x):
        row, count = FIRST_ROWS[which_x][i]
        at = (y if kind == 0 else 1 - y) * half + core * part + row
        region = w_qkv.at[pl.ds(pl.multiple_of(at, 16), count), :]
        return Route(region, region, first_send.at[kind, i], first_recv.at[kind, i], over_y if kind == 0 else over_x)

    def by_x(act, swap=False):
        for which_x in range(2):
            @pl.when(x == (1 - which_x if swap else which_x))
            def _(which_x=which_x):
                act(which_x)

    def first_part(which):
        return w_qkv.at[pl.ds(pl.multiple_of(which * half + core * part, 16), part), :]

    first_within = Route(first_part(1 - y), first_part(1 - y), first_send.at[2, 0], first_recv.at[2, 0], sibling)
    gains_across = Route(gains.at[own_rows, :], gains.at[own_rows, :], first_send.at[2, 1], first_recv.at[2, 1], over_y)
    first_store = pltpu.make_async_copy(w_qkv, qkv_out, store_sem.at[1, WEIGHT_CHUNKS])

    def across(n):
        for a in range(3):
            weights(0, a, n).start()

    def onward(stage, n):
        for a in range(3):
            hand_on(stage, a, n)

    for copy in flips:
        copy.wait()
    for i in range(2):
        w_qkv[own_rows, i * KV_HEADS * HEAD_DIM : (i + 1) * KV_HEADS * HEAD_DIM] = kv_flip[i].T
    loads[0].wait()
    loads[1].wait()
    gains_across.start()
    by_x(lambda which_x: [first(0, i, which_x).start() for i in range(2)])
    for copy in loads[2:]:
        copy.start()

    value = x_ref[...].astype(F32)
    scale = lax.rsqrt(jnp.mean(value * value, axis=0, keepdims=True) + EPSILON)
    scale_ref[...] = scale
    gains_across.arrived()
    h_ref[...] = (value * scale * gains[:, 0:1].astype(F32)).astype(BF16)
    for copy in loads[2:]:
        copy.wait()

    for i in range(2):
        def pass_first(which_x, i=i):
            first(0, i, which_x).arrived()
            first(1, i, which_x).start()

        by_x(pass_first)
        across(i)
    across(2)
    for i in range(2):
        by_x(lambda which_x, i=i: first(1, i, which_x).arrived(), swap=True)
    first_within.start()
    onward(1, 0)
    first_within.arrived()
    first_store.start()

    kv_width = KV_HEADS * HEAD_DIM
    turn = HEAD_DIM // 2

    def rotated(values):
        one, two = values[:turn], values[turn:]
        cos, sin = cosine[...], sine[...]
        return jnp.concatenate([one * cos - two * sin, two * cos + one * sin], axis=0)

    keys_values = over_first(w_qkv[:, : 2 * kv_width], h_ref[...])
    for h in range(KV_HEADS):
        at = h * HEAD_DIM
        both = jnp.concatenate(
            [rotated(keys_values[at : at + HEAD_DIM]), keys_values[kv_width + at : kv_width + at + HEAD_DIM]], axis=0
        ).astype(BF16)
        slot(h, 4 + j)[...] = both.T
        if h < 2:
            for route in (OWN_Y, OWN_NEXT, OWN_SIB):
                start(route, h)
    onward(2, 0)
    onward(1, 1)
    queries_all = over_first(w_qkv[:, 2 * kv_width :], h_ref[...])
    for h in range(HEADS):
        at = h * HEAD_DIM
        q_ref[at : at + HEAD_DIM, :] = rotated(queries_all[at : at + HEAD_DIM]).astype(BF16)
    pass_one(0)
    onward(2, 1)
    pass_two(0)

    def window(h):
        return pltpu.make_async_copy(
            kv.at[h, pl.ds(pl.multiple_of(j * own, own), 5 * own), :], kv_out.at[h], kv_sem.at[h])

    blocks = own // CHUNK
    third = GROUP * CHUNK

    def block(h, n, spans, diagonal):
        both = kv[h, pl.ds(pl.multiple_of(n * own, own), own), :]
        keys = both[:, :HEAD_DIM]
        values = jnp.concatenate([both[:, HEAD_DIM:].T, jnp.ones((16, own), BF16)], axis=0)
        begin_at = (n - 4 - j) * own
        for b in range(blocks):
            low_at, high_at = spans[b]
            low = low_ref[:, b * CHUNK : (b + 1) * CHUNK]
            for r in range(GROUP):
                cols = pl.ds(b * third + r * CHUNK, CHUNK)
                rows = pl.ds(pl.multiple_of(h * GROUP * HEAD_DIM + r * HEAD_DIM, HEAD_DIM), HEAD_DIM)
                queries = q_ref[rows, b * CHUNK : (b + 1) * CHUNK]
                old = top[:, cols]
                high = jnp.full((8, CHUNK), MASKED, F32)
                for at in range(low_at, high_at, STRIP):
                    rows = slice(at, at + STRIP)
                    s = masked(dot(keys[rows], queries), begin_at + at, low, b * CHUNK if diagonal else None)
                    s_all[rows, cols] = s
                    high = jnp.maximum(high, jnp.max(s.reshape(STRIP // 8, 8, CHUNK), axis=0))
                new = jnp.maximum(old, jnp.max(high, axis=0, keepdims=True))
                bound = new * SCALE2
                for at in range(low_at, high_at, STRIP):
                    rows = slice(at, at + STRIP)
                    p_all[rows, cols] = jnp.exp2(s_all[rows, cols] * SCALE2 - bound).astype(BF16)
                shrink[:, cols] = jnp.exp2(old * SCALE2 - bound)
                top[:, cols] = new
        for b in range(blocks):
            low_at, high_at = spans[b]
            cols = pl.ds(b * third, third)
            acc[:, cols] = acc[:, cols] * shrink[:, cols] + dot(values[:, low_at:high_at], p_all[low_at:high_at, cols])

    every = [(0, own)] * blocks
    plan = [(4 + j, [(0, (b + 1) * CHUNK) for b in range(blocks)], True),
            (j, [(b * CHUNK, own) for b in range(blocks)], False),
            (j + 2, every, False), (j + 1 + 2 * y, every, False), (j + 3 - 2 * y, every, False)]
    spots = len(plan)
    steps = [(functools.partial(hand_on, 1), 0, 2), (functools.partial(hand_on, 2), 3, 2),
             (functools.partial(hand_on, 3), 1, 1), (keep, 4, 1)]

    def head(h, carry):
        top[...] = jnp.full(top.shape, MASKED, F32)
        acc[...] = jnp.zeros(acc.shape, F32)

        for p in range(spots):
            if p == 0:
                @pl.when(h < KV_HEADS - 1)
                def _():
                    pass_one(h + 1)

                @pl.when(h < KV_HEADS - 2)
                def _():
                    for route in (OWN_Y, OWN_NEXT, OWN_SIB):
                        start(route, h + 2)

                pl.when(h == 0)(lambda: onward(3, 0))
            if p == 1:
                pl.when(h < KV_HEADS - 3)(lambda: across(h + 3))
                pl.when(h == 2)(lambda: wo_across.start())
            if p == 2:
                arrived(PREV_SIB, h)
                arrived(OWN_SIB, h)
            if p == 4:
                pl.when(h < KV_HEADS - 1)(lambda: pass_two(h + 1))
                arrived(PASS_PREV, h)
                arrived(PASS_OWN, h)

                @pl.when(h == KV_HEADS - 1)
                def _():
                    wo_across.arrived()
                    wo_within.start()
            if p == 1:
                pl.when(h == 0)(lambda: keep(0, 0))
            block(h, *plan[p])
            for step, spot, ahead in reversed(steps):
                for a in range(3):
                    if (p - a - spot) % spots == 0:
                        n = h + ahead + (p - a - spot) // spots
                        fits = jnp.logical_and(n >= (1 if ahead == 1 and step is not keep else 0), n < WEIGHT_CHUNKS)
                        fits = jnp.logical_and(fits, n >= 2) if ahead == 2 else fits
                        pl.when(fits)(lambda step=step, a=a, n=n: step(a, n))

        window(h).start()
        for r in range(GROUP):
            rows = pl.ds(pl.multiple_of(h * GROUP * HEAD_DIM + r * HEAD_DIM, HEAD_DIM), HEAD_DIM)
            for b in range(blocks):
                cols = pl.ds(b * third + r * CHUNK, CHUNK)
                total = acc[HEAD_DIM : HEAD_DIM + 1, cols]
                o_ref[rows, b * CHUNK : (b + 1) * CHUNK] = (acc[:HEAD_DIM, cols] / total).astype(BF16)
                lse_ref[h, r : r + 1, b * CHUNK : (b + 1) * CHUNK] = top[:, cols] * SCALE2 + jnp.log2(total)
        return carry

    lax.fori_loop(0, KV_HEADS, head, 0)
    wo_within.arrived()
    wo_store.start()

    def finish(h, carry):
        for a in range(3):
            for stage in range(4):
                weights(stage, a, h).sent()
            for copy in store(a, h):
                copy.wait()
        for route in range(7):
            pl.when(sent_if[route])(lambda route=route: halo(route, h).sent())
        window(h).wait()
        return carry

    lax.fori_loop(0, KV_HEADS, finish, 0)
    for route in (wo_across, wo_within, first_within, gains_across):
        route.sent()
    by_x(lambda which_x: [first(kind, i, which_x).sent() for kind in range(2) for i in range(2)])
    wo_store.wait()
    first_store.wait()


def attend(low, cosine, sine, x, w_query, w_key_t, w_value_t, gains, w_output, w_gate, w_up, w_down_t, dp_size):
    own = x.shape[1]
    width = GROUP * own
    any_spec = pl.BlockSpec(memory_space=pl.ANY)
    vmem = pl.BlockSpec(memory_space=pltpu.VMEM)
    later = [jax.ShapeDtypeStruct((2 * w.shape[0], w.shape[1]), BF16) for w in (w_output, w_gate, w_up)]
    later.insert(0, jax.ShapeDtypeStruct((D, D + 2 * w_key_t.shape[0]), BF16))
    later.append(jax.ShapeDtypeStruct((w_down_t.shape[0], 2 * w_down_t.shape[1]), BF16))
    return pl.pallas_call(
        functools.partial(forward_kernel, dp_size // 2),
        out_shape=[
            jax.ShapeDtypeStruct((D, own), BF16),
            jax.ShapeDtypeStruct((KV_HEADS, 8, own), F32),
            jax.ShapeDtypeStruct((D, own), BF16),
            jax.ShapeDtypeStruct((D, own), BF16),
            jax.ShapeDtypeStruct((1, own), F32),
            jax.ShapeDtypeStruct((2 * gains.shape[0], gains.shape[1]), BF16),
            jax.ShapeDtypeStruct((KV_HEADS, 5 * own, 2 * HEAD_DIM), BF16),
        ] + later,
        in_specs=[vmem] * 4 + [any_spec] * 8,
        out_specs=[vmem] * 6 + [any_spec] * 6,
        scratch_shapes=[pltpu.VMEM((KV_HEADS, 8 * own, 2 * HEAD_DIM), BF16), pltpu.VMEM((2,) + w_key_t.shape, BF16)]
        + [pltpu.VMEM(w.shape, BF16) for w in later]
        + [
            pltpu.VMEM((1, width), F32),
            pltpu.VMEM((HEAD_DIM + 16, width), F32),
            pltpu.VMEM((1, width), F32),
            pltpu.VMEM((own, width), F32),
            pltpu.VMEM((own, width), BF16),
            pltpu.SemaphoreType.DMA((KV_HEADS,)),
            pltpu.SemaphoreType.DMA((8,)),
            pltpu.SemaphoreType.DMA((4, WEIGHT_CHUNKS + 1)),
            pltpu.SemaphoreType.DMA((7, KV_HEADS)),
            pltpu.SemaphoreType.DMA((7, KV_HEADS)),
            pltpu.SemaphoreType.DMA((4, 3, WEIGHT_CHUNKS)),
            pltpu.SemaphoreType.DMA((4, 3, WEIGHT_CHUNKS)),
            pltpu.SemaphoreType.DMA((2,)),
            pltpu.SemaphoreType.DMA((2,)),
            pltpu.SemaphoreType.DMA((3, 2)),
            pltpu.SemaphoreType.DMA((3, 2)),
        ],
        compiler_params=pltpu.CompilerParams(
            collective_id=2, has_side_effects=True, vmem_limit_bytes=56 * 1024 * 1024),
        name="attend",
    )(low, cosine, sine, x, w_query, w_key_t, w_value_t, gains, w_output, w_gate, w_up, w_down_t)


FEED = 256


def middle_kernel(bits, groups, low_ref, cosine, sine, gains_ref, att_ref, lse_ref,
                  x_in, g_in, q_in, kv_in, wo_in, gate_in, up_in, down_in,
                  out_ref, dx_ref, branch_ref, row_ref, gate_out, up_out, down_out, dq_out, dkv_out,
                  ring, ring_down, far_in, sib_in, far_y, own_y, next_in, halo_send, halo_recv, feed_sem, load_sem, *scratch):
    own = x_in.shape[1]
    half_ff = gate_in.shape[1] // 2
    chunks = half_ff // FEED
    dp, y = place()
    core = dp % 2
    k = dp // 2
    j = 2 * core + y
    j_y = 2 * core + 1 - y
    has_prev, has_next = k > 0, k < groups - 1
    first_core, last_core = core == 0, core == 1
    half = D // 4
    sums = Sums(bits, [None, None], down_in, [gate_out, up_out, down_out], scratch, (ring, ring_down))

    barrier = pltpu.get_barrier_semaphore()
    for partner in sums.partners:
        pl.semaphore_signal(barrier, inc=1, device_id=partner, device_id_type=MESH)

    @pl.when(has_next)
    def _():
        pl.semaphore_signal(barrier, inc=1, device_id=(dp + 2, y), device_id_type=MESH)

    spots = 5
    begins = {0: (-1, 1, 4), 1: (0, 1, 3), 2: (1, 1, 3), 3: (3, 0, 2), 4: (4, 0, 1)}
    events = {(0, 0): [(sums.start_y, a, chunks - 2) for a in range(3)], (0, 2): [(sums.start_y, a, chunks - 1) for a in range(3)]}
    for n in range(chunks):
        turn, spot, lag = begins[n]
        for s in range(len(sums.stages)):
            for a in range(3):
                at = turn * spots + spot + a + lag * s
                events.setdefault((at // spots, at % spots), []).insert(0, (sums.stages[s], a, n))
    last_round = max(turn for turn, spot in events)

    def advance(p, h):
        if isinstance(h, int):
            for step, a, n in events.get((h, p), ()):
                step(a, n)
            return
        for turn in range(KV_HEADS):
            if (turn, p) in events:
                pl.when(h == turn)(lambda turn=turn: advance(p, turn))

    def feed_phase(weights, wo, h_t, g_t, x, h, g, acc):
        def load(n, s):
            cols = pl.ds(pl.multiple_of(s * half_ff + n * FEED, 128), FEED)
            return [pltpu.make_async_copy(w.at[:, cols], weights.at[s, i], feed_sem.at[s, i])
                    for i, w in enumerate((gate_in, up_in, down_in))]

        first = [pltpu.make_async_copy(a, b, load_sem.at[i]) for i, (a, b) in enumerate(((x_in, h_t), (g_in, g_t), (wo_in, wo)))]
        for copy in first + load(0, 0):
            copy.start()
        for copy in first:
            copy.wait()
        gain = gains_ref[:, 1:2].astype(F32)
        x[...] = h_t[...].astype(F32) + over_first(wo[...], att_ref[...])
        scale = lax.rsqrt(jnp.mean(x[...] * x[...], axis=0, keepdims=True) + EPSILON)
        h_t[...] = (x[...] * scale * gain).astype(BF16)
        h[...] = h_t[...].T
        g[...] = g_t[...].T
        acc[...] = x[...]
        dx_ref[...] = jnp.zeros(dx_ref.shape, F32)

        @pl.when(has_prev)
        def _():
            pl.semaphore_wait(barrier, len(sums.partners) + 1)

        @pl.when(jnp.logical_not(has_prev))
        def _():
            pl.semaphore_wait(barrier, len(sums.partners))

        def step(n, s):
            for copy in load(n, s):
                copy.wait()
            if s == 0:
                for copy in load(n, 1):
                    copy.start()
            else:
                @pl.when(n < chunks - 1)
                def _():
                    for copy in load(n + 1, 0):
                        copy.start()

            w_gate, w_up, w_down = weights[s, 0], weights[s, 1], weights[s, 2]
            gate = dot(h[...], w_gate)
            upper = dot(h[...], w_up)
            dm = dot(g[...], w_down)
            sigmoid = 1.0 / (1.0 + jnp.exp(-gate))
            active = gate * sigmoid
            inner = (active * upper).astype(BF16)
            dgate = (dm * upper * sigmoid * (1.0 + gate * (1.0 - sigmoid))).astype(BF16)
            dup = (dm * active).astype(BF16)
            acc[...] += against_rows(w_down, inner)
            dx_ref[...] += against_rows(w_gate, dgate) + against_rows(w_up, dup)
            cols = slice(s * FEED, (s + 1) * FEED)
            for c, shares in ((core, sums.own_share), (1 - core, sums.sibling_share)):
                for which in range(2):
                    rows = pl.ds(pl.multiple_of(which * 2 * half + c * half, 16), half)
                    left = h_t[rows, :]
                    for a, right in enumerate((dgate, dup)):
                        shares(a, n)[which, :, cols] = dot(left, right).astype(BF16)
                rows = pl.ds(pl.multiple_of(c * 2 * half, 16), 2 * half)
                shares(2, n)[s] = dot(g_t[rows, :], inner).astype(BF16)

        def round_of(n, carry):
            @pl.when(n > 1)
            def _():
                for a in range(3):
                    sums.core_sent(a, n - 2)

            step(n, 0)

            @pl.when(jnp.logical_and(n > 0, n < chunks - 1))
            def _():
                for a in range(3):
                    sums.start_y(a, n - 1)

            pl.when(n == chunks - 1)(lambda: (advance(1, -1), advance(2, -1))[0])
            step(n, 1)
            for a in range(3):
                sums.start_core(a, n)
            pl.when(n == chunks - 1)(lambda: (advance(3, -1), advance(4, -1))[0])
            return carry

        lax.fori_loop(0, chunks, round_of, 0)
        out_ref[...] = acc[...].astype(BF16)
        dh = dx_ref[...]
        acc[...] = dh * (x[...] * scale)
        ones = jnp.ones((8, own), F32)
        row_ref[...] = lax.dot_general(ones, acc[...], (((1,), (1,)), ((), ())), precision=lax.Precision.HIGHEST,
                                       preferred_element_type=F32)
        mean = jnp.sum(acc[...] * gain, axis=0, keepdims=True) * (1.0 / D)
        dx = g_t[...].astype(F32) + scale * (dx_ref[...] * gain - x[...] * scale * mean)
        dx_ref[...] = dx
        branch_ref[...] = dx.astype(BF16)

    pl.run_scoped(
        feed_phase,
        pltpu.VMEM((2, 3, D, FEED), BF16),
        pltpu.VMEM((D, D), BF16),
        pltpu.VMEM((D, own), BF16),
        pltpu.VMEM((D, own), BF16),
        pltpu.VMEM((D, own), F32),
        pltpu.VMEM((own, D), BF16),
        pltpu.VMEM((own, D), BF16),
        pltpu.VMEM((D, own), F32),
    )
    for n in (chunks - 2, chunks - 1):
        for a in range(3):
            sums.core_sent(a, n)

    blocks = own // CHUNK
    third = GROUP * CHUNK

    def attention_phase(wo, q, do, kv, q_all, do_all, q_rows, do_rows, delta, dq_acc, p_all, ds_all, part, dq, dkv):
        first = [pltpu.make_async_copy(a, b, load_sem.at[i]) for i, (a, b) in enumerate(((wo_in, wo), (q_in, q)))]

        def window(h, at):
            return pltpu.make_async_copy(kv_in.at[h], kv.at[at], feed_sem.at[at, 0])

        for copy in first + [window(0, 0)]:
            copy.start()
        part[...] = jnp.zeros(part.shape, BF16)
        for copy in first:
            copy.wait()
        do[...] = dot(wo[...], branch_ref[...]).astype(BF16)

        def slot(h, n):
            return part.at[h, pl.ds(pl.multiple_of(n * own, own), own), :]

        def halo(route, h):
            before = jnp.maximum(dp - 2, 0)
            sems = (halo_send.at[route, h], halo_recv.at[route, h])
            if route == PASS_PREV:
                return Route(slot(h, j_y + 2 - 4 * core), far_in.at[h], *sems, sums.sibling)
            if route == PASS_OWN:
                return Route(slot(h, 2 + j_y), far_in.at[h], *sems, sums.sibling)
            if route == PREV_SIB:
                return Route(slot(h, j + 2 - 4 * core), sib_in.at[h], *sems, sums.sibling)
            if route == OWN_SIB:
                return Route(slot(h, 2 + j), sib_in.at[h], *sems, sums.sibling)
            if route == PREV_Y:
                return Route(slot(h, j_y), far_y.at[h], *sems, sums.over_y)
            if route == OWN_Y:
                return Route(slot(h, 4 + j_y), own_y.at[h], *sems, sums.over_y)
            return Route(slot(h, j), next_in.at[h], *sems, (before, y))

        got_if = {
            OWN_SIB: first_core, OWN_Y: j != 3, OWN_NEXT: has_next, PASS_OWN: first_core,
            PREV_SIB: jnp.logical_and(last_core, has_prev), PREV_Y: jnp.logical_and(j != 0, has_prev),
            PASS_PREV: jnp.logical_and(last_core, has_prev),
        }
        sent_if = {
            OWN_SIB: last_core, OWN_Y: j != 2, OWN_NEXT: has_prev, PASS_OWN: last_core,
            PREV_SIB: jnp.logical_and(first_core, has_prev), PREV_Y: jnp.logical_and(j != 1, has_prev),
            PASS_PREV: jnp.logical_and(first_core, has_prev),
        }

        def start(route, h):
            pl.when(sent_if[route])(lambda: halo(route, h).start())

        def take(route, h, n, box):
            @pl.when(got_if[route])
            def _():
                halo(route, h).arrived()
                spot = slot(h, n)
                spot[...] = spot[...] + box[h]

        def return_one(h):
            for route in (PASS_PREV, PASS_OWN, PREV_SIB, OWN_SIB):
                start(route, h)

        def return_two(h):
            take(PASS_PREV, h, j_y, far_in)
            take(PASS_OWN, h, 4 + j_y, far_in)
            start(PREV_Y, h)
            start(OWN_Y, h)

        def return_three(h):
            for route, n, box in ((PREV_SIB, j, sib_in), (OWN_SIB, 4 + j, sib_in), (PREV_Y, j, far_y), (OWN_Y, 4 + j, own_y)):
                take(route, h, n, box)
            start(OWN_NEXT, h)

        def return_four(h):
            dkv[h] = slot(h, 4 + j)[...].astype(F32)

            @pl.when(has_next)
            def _():
                halo(OWN_NEXT, h).arrived()
                dkv[h] = dkv[h] + next_in[h].astype(F32)

        def head_rows(h, r):
            return pl.ds(pl.multiple_of(h * GROUP * HEAD_DIM + r * HEAD_DIM, HEAD_DIM), HEAD_DIM)

        def prepare(h):
            for r in range(GROUP):
                rows = head_rows(h, r)
                for b in range(blocks):
                    cols = pl.ds(b * third + r * CHUNK, CHUNK)
                    from_cols = slice(b * CHUNK, (b + 1) * CHUNK)
                    grad, queries = do[rows, from_cols], q[rows, from_cols]
                    q_all[:, cols] = queries
                    do_all[:, cols] = grad
                    q_rows[cols, :] = queries.T
                    do_rows[cols, :] = grad.T
                    delta[:, cols] = jnp.sum(grad.astype(F32) * att_ref[rows, from_cols].astype(F32), axis=0, keepdims=True)
            dq_acc[...] = jnp.zeros(dq_acc.shape, F32)

        def block(h, at, n, spans, diagonal):
            both = kv[at, n * own : (n + 1) * own, :]
            keys, values = both[:, :HEAD_DIM], both[:, HEAD_DIM:]
            begin_at = (n - 4) * own
            for i in range(own // CHUNK):
                row = i * CHUNK
                some_keys, some_values = keys[row : row + CHUNK], values[row : row + CHUNK]
                using = [b for b in range(blocks) if spans[b][0] <= row < spans[b][1]]
                for b in using:
                    low = low_ref[:, b * CHUNK : (b + 1) * CHUNK]
                    for r in range(GROUP):
                        cols = pl.ds(b * third + r * CHUNK, CHUNK)
                        lse = lse_ref[h, r : r + 1, b * CHUNK : (b + 1) * CHUNK]
                        s = masked(dot(some_keys, q_all[:, cols]), begin_at + row, low, b * CHUNK if diagonal and b == i else None)
                        p = jnp.exp2(s * SCALE2 - lse)
                        p_all[:, cols] = p.astype(BF16)
                        ds_all[:, cols] = (p * (dot(some_values, do_all[:, cols]) - delta[:, cols])).astype(BF16)
                cols = pl.ds(using[0] * third, len(using) * third)
                dq_acc[:, cols] += dot(some_keys.T, ds_all[:, cols])
                dk = dot(ds_all[:, cols], q_rows[cols, :]) * 0.125
                dv = dot(p_all[:, cols], do_rows[cols, :])
                spot = pl.ds(pl.multiple_of((n + j) * own + row, CHUNK), CHUNK)
                part[h, spot, :] = jnp.concatenate([dk, dv], axis=1).astype(BF16)

        every = [(0, own)] * blocks
        plan = [(0, [(b * CHUNK, own) for b in range(blocks)], False), (1, every, False), (2, every, False),
                (3, every, False), (4, [(0, (b + 1) * CHUNK) for b in range(blocks)], True)]
        def guarded(fn, h):
            pl.when(jnp.logical_and(h >= 0, h < KV_HEADS))(lambda: fn(h))

        def head(h, carry):
            at = h % 2
            window(h, at).wait()

            @pl.when(h < KV_HEADS - 1)
            def _():
                window(h + 1, 1 - at).start()

            prepare(h)
            for p in range(spots):
                block(h, at, *plan[p])
                advance(p, h)
                if p == 1:
                    guarded(return_two, h - 1)
                if p == 4:
                    guarded(return_three, h - 3)
            return_one(h)
            for r in range(GROUP):
                rows = head_rows(h, r)
                for b in range(blocks):
                    value = dq_acc[:, pl.ds(b * third + r * CHUNK, CHUNK)] * 0.125
                    spot = slice(b * CHUNK, (b + 1) * CHUNK)
                    cos, sin = cosine[:, spot], sine[:, spot]
                    one, two = value[: HEAD_DIM // 2], value[HEAD_DIM // 2 :]
                    back = jnp.concatenate([one * cos + two * sin, two * cos - one * sin], axis=0)
                    dq[rows, spot] = back.astype(BF16)
            return carry

        lax.fori_loop(0, KV_HEADS, head, 0)
        last = KV_HEADS - 1
        after = [(return_two, last), (return_three, 2), (return_three, 3), (return_four, 0), (return_four, 1),
                 (return_three, last), (return_four, 2), (return_four, 3)]
        for i in range((last_round - KV_HEADS + 1) * spots):
            if i < len(after):
                fn, h = after[i]
                fn(h)
            advance(i % spots, KV_HEADS + i // spots)
        for fn, h in after[(last_round - KV_HEADS + 1) * spots :]:
            fn(h)
        return_four(last)
        stores = [pltpu.make_async_copy(dq, dq_out, load_sem.at[0]), pltpu.make_async_copy(dkv, dkv_out, load_sem.at[1])]
        for store in stores:
            store.start()

        def finish(h, carry):
            for route in range(7):
                pl.when(sent_if[route])(lambda route=route: halo(route, h).sent())
            return carry

        lax.fori_loop(0, KV_HEADS, finish, 0)
        for store in stores:
            store.wait()

    width = GROUP * own
    pl.run_scoped(
        attention_phase,
        pltpu.VMEM((D, D), BF16),
        pltpu.VMEM((D, own), BF16),
        pltpu.VMEM((D, own), BF16),
        pltpu.VMEM((2, 5 * own, 2 * HEAD_DIM), BF16),
        pltpu.VMEM((HEAD_DIM, width), BF16),
        pltpu.VMEM((HEAD_DIM, width), BF16),
        pltpu.VMEM((width, HEAD_DIM), BF16),
        pltpu.VMEM((width, HEAD_DIM), BF16),
        pltpu.VMEM((1, width), F32),
        pltpu.VMEM((HEAD_DIM, width), F32),
        pltpu.VMEM((CHUNK, width), BF16),
        pltpu.VMEM((CHUNK, width), BF16),
        pltpu.VMEM((KV_HEADS, 8 * own, 2 * HEAD_DIM), BF16),
        pltpu.VMEM((D, own), BF16),
        pltpu.VMEM((KV_HEADS, own, 2 * HEAD_DIM), F32),
    )

    for n in range(chunks):
        for a in range(3):
            sums.drain(a, n)


def middle_and_back(low, cosine, sine, gains, attended, lse, x, cotangent, queries, both, w_output, w_gate, w_up, w_down_t,
           dp_size):
    own = x.shape[1]
    ff = w_gate.shape[1]
    bits = dp_size.bit_length() - 1
    half = D // 4
    chunks = ff // WIDE
    any_spec = pl.BlockSpec(memory_space=pl.ANY)
    vmem = pl.BlockSpec(memory_space=pltpu.VMEM)
    box = pltpu.VMEM((KV_HEADS, own, 2 * HEAD_DIM), BF16)
    return pl.pallas_call(
        functools.partial(middle_kernel, bits, dp_size // 2),
        out_shape=[
            jax.ShapeDtypeStruct((D, own), BF16),
            jax.ShapeDtypeStruct((D, own), F32),
            jax.ShapeDtypeStruct((D, own), BF16),
            jax.ShapeDtypeStruct((8, D), F32),
            jax.ShapeDtypeStruct((D // 2, ff), BF16),
            jax.ShapeDtypeStruct((D // 2, ff), BF16),
            jax.ShapeDtypeStruct((D, ff // 2), BF16),
            jax.ShapeDtypeStruct((D, own), BF16),
            jax.ShapeDtypeStruct((KV_HEADS, own, 2 * HEAD_DIM), F32),
        ],
        in_specs=[vmem] * 6 + [any_spec] * 8,
        out_specs=[vmem] * 4 + [any_spec] * 5,
        scratch_shapes=[
            pltpu.VMEM((2, 2, 2, half, WIDE), BF16),
            pltpu.VMEM((2, 2, 2 * half, FEED), BF16),
            box, box, box, box, box,
            pltpu.SemaphoreType.DMA((7, KV_HEADS)),
            pltpu.SemaphoreType.DMA((7, KV_HEADS)),
            pltpu.SemaphoreType.DMA((2, 3)),
            pltpu.SemaphoreType.DMA((3,)),
        ] + Sums.scratch(bits, 2, 1, chunks, half),
        compiler_params=pltpu.CompilerParams(
            collective_id=3, has_side_effects=True, vmem_limit_bytes=60 * 1024 * 1024),
        name="middle",
    )(low, cosine, sine, gains, attended, lse, x, cotangent, queries, both, w_output, w_gate, w_up, w_down_t)


def finish_kernel(bits, chunks, dq, dkv, cosine, sine, hidden, x, scale, gains, w_qkv, attended, branch, middle, feed_row,
                  out, gains_out, tokens_out, pack, grads, prod, *rest):
    sums = Sums(bits, [pack], None, [out], rest[:-5])
    g_loc, g_in, g_sem, g_send, g_recv = rest[-5:]
    half = HEAD_DIM // 2
    rows = pack.shape[1]
    greet(sums.partners)

    def gain_route(n):
        return Route(g_loc.at[n], g_in.at[n], g_send.at[n], g_recv.at[n], sums.partners[n])

    def unrotate(values, at):
        one, two = values[:half], values[half:]
        cos, sin = cosine[...], sine[...]
        grads[at : at + half, :] = (one * cos + two * sin).astype(BF16)
        grads[at + half : at + HEAD_DIM, :] = (two * cos - one * sin).astype(BF16)

    def columns(low, high):
        parts = []
        if low < D:
            parts.append((attended, branch, low, min(high, D)))
        if high > D:
            parts.append((hidden, grads, max(low, D) - D, high - D))
        return [against_rows(left[...], right[a:b, :]) for left, right, a, b in parts]

    def fill(n):
        parts = columns(n * WIDE, (n + 1) * WIDE)
        value = parts[0] if len(parts) == 1 else jnp.concatenate(parts, axis=1)
        value = value.astype(BF16)
        for which in range(2):
            pack[which, :, n * WIDE : (n + 1) * WIDE] = value[which * rows : (which + 1) * rows]
        sums.start_core(0, n)

    def heads():
        grads[:D, :] = dq[...]
        for h in range(KV_HEADS):
            both = dkv[h].T
            unrotate(both[:HEAD_DIM], D + h * HEAD_DIM)
            at = D + (KV_HEADS + h) * HEAD_DIM
            grads[at : at + HEAD_DIM, :] = both[HEAD_DIM:].astype(BF16)

    def hidden_grad():
        keys_values = 2 * KV_HEADS * HEAD_DIM
        dh = dot(w_qkv[:, keys_values:], grads[:D, :]) + dot(w_qkv[:, :keys_values], grads[D:, :])
        tokens_out[...] = dh
        prod[...] = dh * (x[...].astype(F32) * scale[...])
        g_loc[0] = jnp.zeros(g_loc.shape[1:], F32)
        ones = jnp.ones((8, dh.shape[1]), F32)
        total = lax.dot_general(ones, prod[...], (((1,), (1,)), ((), ())), precision=lax.Precision.HIGHEST,
                                preferred_element_type=F32)
        g_loc[0, 0:1, :] = total[0:1]
        g_loc[0, 1:2, :] = feed_row[0:1, :]
        gain_route(0).start()

    def tokens_grad():
        normed = x[...].astype(F32) * scale[...]
        gain = gains[:, 0:1].astype(F32)
        e = tokens_out[...] * gain
        mean = jnp.sum(prod[...] * gain, axis=0, keepdims=True) * (1.0 / D)
        tokens_out[...] = middle[...] + scale[...] * (e - normed * mean)

    def gain_step(n):
        gain_route(n - 1).arrived()
        g_loc[n] = g_loc[n - 1] + g_in[n - 1]
        if n < len(sums.partners):
            gain_route(n).start()

    work = [lambda: fill(0), lambda: (heads(), fill(1))] + [functools.partial(fill, n) for n in range(2, chunks)]
    work += [hidden_grad, tokens_grad] + [functools.partial(gain_step, n + 1) for n in range(len(sums.partners))]
    steps = [sums.start_y] + sums.stages
    delay = [1, 3]
    while len(delay) < len(steps):
        delay.append(delay[-1] + 1)
    for tick in range(max(chunks + delay[-1], len(work))):
        if tick < len(work):
            work[tick]()
        for s in [0] + list(range(len(steps) - 1, 0, -1)):
            if 0 <= tick - delay[s] < chunks:
                steps[s](0, tick - delay[s])
    store = pltpu.make_async_copy(g_loc.at[len(sums.partners)], gains_out, g_sem.at[0])
    store.start()
    for n in range(chunks):
        sums.core_sent(0, n)
        sums.drain(0, n)
    for n in range(len(sums.partners)):
        gain_route(n).sent()
    store.wait()


def finish(dq, dkv, cosine, sine, hidden, x, scale, gains, w_qkv, attended, branch, middle, feed_row, dp_size):
    bits = dp_size.bit_length() - 1
    own = x.shape[1]
    total = 2 * D + 2 * KV_HEADS * HEAD_DIM
    chunks = total // WIDE
    any_spec = pl.BlockSpec(memory_space=pl.ANY)
    vmem = pl.BlockSpec(memory_space=pltpu.VMEM)
    row = (8, D)
    return pl.pallas_call(
        functools.partial(finish_kernel, bits, chunks),
        out_shape=[
            jax.ShapeDtypeStruct((D // 2, total), BF16),
            jax.ShapeDtypeStruct(row, F32),
            jax.ShapeDtypeStruct((D, own), F32),
        ],
        in_specs=[vmem] * 13,
        out_specs=[any_spec, any_spec, vmem],
        scratch_shapes=[
            pltpu.VMEM((2, D // 2, total), BF16),
            pltpu.VMEM((total - D, own), BF16),
            pltpu.VMEM((D, own), F32),
        ] + Sums.scratch(bits, 1, 0, chunks, D // 4) + [
            pltpu.VMEM((bits + 2,) + row, F32),
            pltpu.VMEM((bits + 1,) + row, F32),
            pltpu.SemaphoreType.DMA((1,)),
            pltpu.SemaphoreType.DMA((bits + 1,)),
            pltpu.SemaphoreType.DMA((bits + 1,)),
        ],
        compiler_params=pltpu.CompilerParams(
            collective_id=0, has_side_effects=True, vmem_limit_bytes=56 * 1024 * 1024),
        name="finish",
    )(dq, dkv, cosine, sine, hidden, x, scale, gains, w_qkv, attended, branch, middle, feed_row)


def positions(seq_lengths, first, count):
    ends = jnp.cumsum(seq_lengths)
    index = first + jnp.arange(count, dtype=jnp.int32)
    passed = index[:, None] >= ends[None, :]
    begin = jnp.max(jnp.where(passed, ends[None, :], 0), axis=1)
    return index - begin


def rotary_tables(position):
    half = HEAD_DIM // 2
    inverse = jnp.exp(-jnp.arange(half, dtype=F32) * (2.0 / HEAD_DIM) * jnp.log(THETA))
    angle = inverse[:, None] * position.astype(F32)[None, :]
    return jnp.cos(angle), jnp.sin(angle)


def shards(tokens, cotangent, w_query, w_key, w_value, w_output, w_gate, w_up, w_down, attention_gain, feed_gain, seq_lengths):
    own = tokens.shape[0]
    kv = KV_HEADS * HEAD_DIM
    first = lax.axis_index(("dp", "shard")) * own
    position = positions(seq_lengths, first, own)
    low = jnp.arange(own, dtype=jnp.int32) - position
    cosine, sine = rotary_tables(position)
    gains = jnp.where(jnp.arange(128)[None, :] == 0, attention_gain[:, None], feed_gain[:, None])
    dp_size = lax.axis_size("dp")
    (attended, log_total, queries, hidden_one, scale_one, gains, both_all,
     qkv_full, output_full, gate_full, up_full, down_full) = attend(
        low[None, :], cosine, sine, tokens.T, w_query, w_key.T, w_value.T, gains,
        w_output, w_gate, w_up, w_down.T, dp_size
    )
    output, grad_middle, grad_branch, feed_rows, sum_gate, sum_up, sum_down, grad_queries, grad_own = middle_and_back(
        low[None, :], cosine, sine, gains, attended, log_total, tokens.T, cotangent.T, queries,
        both_all, output_full, gate_full, up_full, down_full, dp_size
    )
    sum_pack, sum_gains, grad_tokens = finish(
        grad_queries, grad_own, cosine, sine, hidden_one, tokens.T, scale_one, gains, qkv_full,
        attended, grad_branch, grad_middle, feed_rows, dp_size
    )
    sum_pack = sum_pack.astype(F32)
    half = D // 2
    begin = lax.axis_index("shard") * half
    return (
        output.T,
        grad_tokens.T,
        sum_pack[:, D : 2 * D],
        sum_pack[:, 2 * D : 2 * D + kv],
        sum_pack[:, 2 * D + kv :],
        sum_pack[:, :D],
        sum_gate.astype(F32),
        sum_up.astype(F32),
        sum_down.astype(F32).T,
        lax.dynamic_slice_in_dim(sum_gains[0], begin, half),
        lax.dynamic_slice_in_dim(sum_gains[1], begin, half),
    )


def solution(mesh):
    return jax.shard_map(
        shards,
        mesh=mesh,
        in_specs=(
            P(("dp", "shard"), None),
            P(("dp", "shard"), None),
            P("shard", None),
            P("shard", None),
            P("shard", None),
            P("shard", None),
            P("shard", None),
            P("shard", None),
            P("shard", None),
            P("shard"),
            P("shard"),
            P(),
        ),
        out_specs=(
            P(("dp", "shard"), None),
            P(("dp", "shard"), None),
            P("shard", None),
            P("shard", None),
            P("shard", None),
            P("shard", None),
            P("shard", None),
            P("shard", None),
            P("shard", None),
            P("shard"),
            P("shard"),
        ),
        check_vma=False,
    )
```

```python
import functools

import jax
import jax.numpy as jnp
from jax import lax
from jax.experimental import pallas as pl
from jax.experimental.pallas import tpu as pltpu
from jax.sharding import PartitionSpec as P

D = 960
HEADS = 15
KV_HEADS = 5
GROUP = 3
HEAD_DIM = 64

EPSILON = 1e-05
THETA = 100000.0
MASKED = -1e30
LOG2E = 1.4426950408889634
SCALE2 = 0.125 * LOG2E

MESH = pl.DeviceIdType.MESH
WIDE = 512
CHUNK = 256
STRIP = 128
BF16 = jnp.bfloat16
F32 = jnp.float32


def dot(left, right):
    return lax.dot_general(left, right, (((1,), (0,)), ((), ())), preferred_element_type=F32)


def against_rows(left, right):
    return lax.dot_general(left, right, (((1,), (1,)), ((), ())), preferred_element_type=F32)


def over_first(left, right):
    return lax.dot_general(left, right, (((0,), (0,)), ((), ())), preferred_element_type=F32)


def masked(scores, start, low, diagonal):
    rows = start + lax.broadcasted_iota(jnp.int32, scores.shape, 0)
    valid = rows >= low
    if diagonal is not None:
        cols = diagonal + lax.broadcasted_iota(jnp.int32, scores.shape, 1)
        valid = jnp.logical_and(valid, rows <= cols)
    return jnp.where(valid, scores, MASKED)


def place():
    return lax.axis_index("dp"), lax.axis_index("shard")


def other(dp, y, bit):
    step = 1 << bit
    mine = (dp // step) % 2
    return (dp + step - 2 * step * mine, y)


def greet(partners):
    barrier = pltpu.get_barrier_semaphore()
    for partner in partners:
        pl.semaphore_signal(barrier, inc=1, device_id=partner, device_id_type=MESH)
    pl.semaphore_wait(barrier, len(partners))


class Route:
    def __init__(self, src, dst, send, recv, partner):
        self.make = lambda: pltpu.make_async_remote_copy(
            src_ref=src, dst_ref=dst, send_sem=send, recv_sem=recv, device_id=partner, device_id_type=MESH)

    def start(self):
        self.make().start()

    def arrived(self):
        self.make().wait_recv()

    def sent(self):
        self.make().wait_send()


S = slice(None)


class Sums:
    def __init__(self, bits, pack, outs, scratch, rings=None):
        self.pack, self.outs, self.rings = pack, outs, rings
        self.boxes = [scratch[:7], scratch[7:14]][: len(outs)]
        self.put_sem, self.send_sem, self.recv_sem = scratch[-3:]
        self.arrays = range(len(outs))
        self.half = D // 4
        dp, y = place()
        self.core, self.x, self.z, self.y = dp % 2, (dp // 2) % 2, (dp // 4) % 2, y
        self.sibling, self.over_y = other(dp, y, 0), (dp, 1 - y)
        self.over_x, self.over_z = other(dp, y, 1), other(dp, y, 2)
        self.extra = [other(dp, y, bit) for bit in range(3, bits)]
        self.partners = [self.sibling, self.over_y, self.over_x, self.over_z] + self.extra
        self.stages = [self.start_x, self.start_z]
        self.stages += [functools.partial(self.more, step) for step in range(len(self.extra) + 1)]
        self.stages += [self.back_x, self.back_core, self.finish]

    @staticmethod
    def scratch(bits, wide_arrays, tall, chunks, half):
        more = bits - 3

        def boxes(n, shapes):
            return [pltpu.VMEM((n, chunks) + shape, BF16) for shape in shapes]

        shared = [(half, 128), (max(more, 1), half, 128)]
        out = boxes(wide_arrays, [(2, half, WIDE)] * 2 + [(half, WIDE), (half, 256)] + shared + [(2 * half, WIDE)])
        if tall:
            out += boxes(1, [(2, 2 * half, 256)] * 2 + [(2 * half, 256), (half, 256)] + shared + [(4 * half, 256)])
        return out + [
            pltpu.SemaphoreType.DMA((4, 1 + tall, chunks)),
            pltpu.SemaphoreType.DMA((8 + more, 1 + tall, chunks)),
            pltpu.SemaphoreType.DMA((8 + more, 1 + tall, chunks)),
        ]

    def box(self, which, a, n):
        return self.boxes[a][which].at[:, n]

    def own_share(self, a, n):
        return self.box(0, a, n)

    def sibling_share(self, a, n):
        return self.rings[a].at[n % 2]

    def source(self, n, c, which):
        rows = pl.ds(pl.multiple_of(c * self.half, 16), self.half)
        return self.pack.at[:, which, rows, pl.ds(pl.multiple_of(n * WIDE, 128), WIDE)]

    def x_part(self, a, which):
        if a == 1:
            return S, pl.ds(pl.multiple_of(which * self.half, 16), self.half), S
        return S, S, pl.ds(pl.multiple_of(which * 256, 128), 256)

    def z_part(self, which):
        return S, S, pl.ds(pl.multiple_of(which * 128, 128), 128)

    def back_at(self, a, c, x=None, z=None):
        half = self.half
        if a == 1:
            if x is None:
                return S, pl.ds(pl.multiple_of(c * 2 * half, 16), 2 * half), S
            rows = pl.ds(pl.multiple_of(c * 2 * half + x * half, 16), half)
            return S, rows, S if z is None else pl.ds(pl.multiple_of(z * 128, 128), 128)
        rows = pl.ds(pl.multiple_of(c * half, 16), half)
        if x is None:
            return S, rows, S
        if z is None:
            return S, rows, pl.ds(pl.multiple_of(x * 256, 128), 256)
        return S, rows, pl.ds(pl.multiple_of(x * 256 + z * 128, 128), 128)

    def route(self, stage, a, n, src, dst, partner):
        return Route(src, dst, self.send_sem.at[stage, a, n], self.recv_sem.at[stage, a, n], partner)

    def copy(self, stage, a, n):
        loc, core_in, y_in, x_in, z_in, more_in, back = (self.box(i, a, n) for i in range(7))
        more = len(self.extra)
        if stage < 2:
            leaving = self.sibling_share(a, n).at[:, stage] if self.rings else self.source(n, 1 - self.core, stage)
            return self.route(stage, a, n, leaving, core_in.at[:, stage], self.sibling)
        if stage == 2:
            return self.route(stage, a, n, loc.at[:, 1 - self.y], y_in, self.over_y)
        if stage == 3:
            return self.route(stage, a, n, y_in.at[self.x_part(a, 1 - self.x)], x_in, self.over_x)
        if stage == 4:
            return self.route(stage, a, n, x_in.at[self.z_part(1 - self.z)], z_in, self.over_z)
        if stage < 5 + more:
            so_far = z_in if stage == 5 else more_in.at[:, stage - 6]
            return self.route(stage, a, n, so_far, more_in.at[:, stage - 5], self.extra[stage - 5])
        at = [(self.core, self.x, self.z), (self.core, self.x), (self.core,)][stage - 5 - more]
        part = back.at[self.back_at(a, *at)]
        return self.route(stage, a, n, part, part, (self.over_z, self.over_x, self.sibling)[stage - 5 - more])

    def puts(self, a, n):
        copies = []
        for i, out in enumerate(self.outs[a]):
            box = self.boxes[a][6].at[i, n]
            if a == 1:
                moves = [(box, n * 256, 256)]
            elif not self.rings:
                moves = [(box, n * WIDE, WIDE)]
            else:
                moves = [(box.at[:, pl.ds(part * 256, 256)], part * (out.shape[1] // 2) + n * 256, 256) for part in range(2)]
            for part, (src, at, width) in enumerate(moves):
                dst = out.at[:, pl.ds(pl.multiple_of(at, 128), width)]
                copies.append(pltpu.make_async_copy(src, dst, self.put_sem.at[2 * i + part, a, n]))
        return copies

    def start_core(self, a, n):
        for which in range(2):
            self.copy(which, a, n).start()

    def core_sent(self, a, n):
        for which in range(2):
            self.copy(which, a, n).sent()

    def start_y(self, a, n):
        loc, core_in = self.box(0, a, n), self.box(1, a, n)
        for which in range(2):
            self.copy(which, a, n).arrived()
            mine = loc.at[:, which] if self.rings else self.source(n, self.core, which)
            loc[:, which] = mine[...] + core_in[:, which]
        self.copy(2, a, n).start()

    def start_x(self, a, n):
        loc, y_in = self.box(0, a, n), self.box(2, a, n)
        self.copy(2, a, n).arrived()
        y_in[...] = y_in[...] + loc[:, self.y]
        self.copy(3, a, n).start()

    def start_z(self, a, n):
        y_in, x_in = self.box(2, a, n), self.box(3, a, n)
        self.copy(3, a, n).arrived()
        x_in[...] = x_in[...] + y_in[self.x_part(a, self.x)]
        self.copy(4, a, n).start()

    def more(self, step, a, n):
        x_in, z_in, more_in, back = (self.box(i, a, n) for i in range(3, 7))
        self.copy(4 + step, a, n).arrived()
        if step == 0:
            total = z_in
            value = z_in[...] + x_in[self.z_part(self.z)]
        else:
            total = more_in.at[:, step - 1]
            value = (z_in if step == 1 else more_in.at[:, step - 2])[...] + total[...]
        if step < len(self.extra):
            total[...] = value
        else:
            back[self.back_at(a, self.core, self.x, self.z)] = value
        self.copy(5 + step, a, n).start()

    def back_x(self, a, n):
        stage = 5 + len(self.extra)
        self.copy(stage, a, n).arrived()
        self.copy(stage + 1, a, n).start()

    def back_core(self, a, n):
        stage = 6 + len(self.extra)
        self.copy(stage, a, n).arrived()
        self.copy(stage + 1, a, n).start()

    def finish(self, a, n):
        self.copy(7 + len(self.extra), a, n).arrived()
        for put in self.puts(a, n):
            put.start()

    def drain(self, a, n):
        for stage in range(2, 8 + len(self.extra)):
            self.copy(stage, a, n).sent()
        for put in self.puts(a, n):
            put.wait()


OWN_SIB, OWN_Y, OWN_NEXT, PASS_OWN, PREV_SIB, PREV_Y, PASS_PREV = range(7)
WEIGHT_CHUNKS = 5
FIRST_ROWS = (((0, 64), (64, 64)), ((128, 64), (192, 48)))


def forward_kernel(groups, low_ref, cosine, sine, x_ref, q_in, k_in, v_in, gains_in, wo_in, gate_in, up_in, down_in,
                   o_ref, lse_ref, q_ref, h_ref, scale_ref, gains, kv_out, qkv_out, wo_out, gate_out, up_out, down_out,
                   kv, kv_flip, w_qkv, wo, pair, down, top, acc, shrink, s_all, p_all,
                   kv_sem, load_sem, store_sem, send_sem, recv_sem, w_send, w_recv, wo_send, wo_recv, first_send, first_recv):
    dp, y = place()
    core, x, z = dp % 2, (dp // 2) % 2, (dp // 4) % 2
    k = dp // 2
    j = 2 * core + y
    j_y = 2 * core + 1 - y
    sibling, over_y, over_x, over_z = other(dp, y, 0), (dp, 1 - y), other(dp, y, 1), other(dp, y, 2)
    own = x_ref.shape[1]
    has_prev, has_next = k > 0, k < groups - 1
    first_core, last_core = core == 0, core == 1

    half, tall = gate_in.shape[0], down_in.shape[1]
    own_rows = pl.ds(pl.multiple_of(y * half, 16), half)
    own_cols = pl.ds(pl.multiple_of(y * tall, 128), tall)
    loads = [
        pltpu.make_async_copy(q_in, w_qkv.at[own_rows, pl.ds(2 * KV_HEADS * HEAD_DIM, D)], load_sem.at[0]),
        pltpu.make_async_copy(gains_in, gains.at[own_rows, :], load_sem.at[1]),
        pltpu.make_async_copy(gate_in, pair.at[0, own_rows, :], load_sem.at[2]),
        pltpu.make_async_copy(up_in, pair.at[1, own_rows, :], load_sem.at[3]),
        pltpu.make_async_copy(down_in, down.at[:, own_cols], load_sem.at[4]),
        pltpu.make_async_copy(wo_in, wo.at[own_rows, :], load_sem.at[5]),
    ]
    flips = [pltpu.make_async_copy(w, kv_flip.at[i], load_sem.at[6 + i]) for i, w in enumerate((k_in, v_in))]
    for copy in flips + loads[:2]:
        copy.start()

    @pl.when(k == 0)
    def _():
        kv[:, : 4 * own, :] = jnp.zeros((KV_HEADS, 4 * own, 2 * HEAD_DIM), BF16)

    barrier = pltpu.get_barrier_semaphore()
    for partner in (sibling, over_y, over_x, over_z):
        pl.semaphore_signal(barrier, inc=1, device_id=partner, device_id_type=MESH)

    @pl.when(has_prev)
    def _():
        pl.semaphore_signal(barrier, inc=1, device_id=(dp - 2, y), device_id_type=MESH)

    @pl.when(has_next)
    def _():
        pl.semaphore_wait(barrier, 5)

    @pl.when(jnp.logical_not(has_next))
    def _():
        pl.semaphore_wait(barrier, 4)

    def slot(h, n):
        return kv.at[h, pl.ds(pl.multiple_of(n * own, own), own), :]

    def halo(route, h):
        after = jnp.minimum(dp + 2, 2 * groups - 1)
        sems = (send_sem.at[route, h], recv_sem.at[route, h])
        if route == OWN_SIB:
            return Route(slot(h, 4 + j), slot(h, 4 + j), *sems, sibling)
        if route == OWN_Y:
            return Route(slot(h, 4 + j), slot(h, 4 + j), *sems, over_y)
        if route == OWN_NEXT:
            return Route(slot(h, 4 + j), slot(h, j), *sems, (after, y))
        if route == PASS_OWN:
            return Route(slot(h, 4 + j_y), slot(h, 4 + j_y), *sems, sibling)
        if route == PREV_SIB:
            return Route(slot(h, j), slot(h, j), *sems, sibling)
        if route == PREV_Y:
            return Route(slot(h, j), slot(h, j), *sems, over_y)
        return Route(slot(h, j_y), slot(h, j_y), *sems, sibling)

    sent_if = {
        OWN_SIB: first_core, OWN_Y: j != 3, OWN_NEXT: has_next, PASS_OWN: first_core,
        PREV_SIB: jnp.logical_and(last_core, has_prev), PREV_Y: jnp.logical_and(j != 0, has_prev),
        PASS_PREV: jnp.logical_and(last_core, has_prev),
    }
    got_if = {
        OWN_SIB: last_core, OWN_Y: j != 2, OWN_NEXT: has_prev, PASS_OWN: last_core,
        PREV_SIB: jnp.logical_and(first_core, has_prev), PREV_Y: jnp.logical_and(j != 1, has_prev),
        PASS_PREV: jnp.logical_and(first_core, has_prev),
    }

    def start(route, h):
        pl.when(sent_if[route])(lambda: halo(route, h).start())

    def arrived(route, h):
        pl.when(got_if[route])(lambda: halo(route, h).arrived())

    def pass_one(h):
        arrived(OWN_Y, h)
        start(PASS_OWN, h)
        arrived(OWN_NEXT, h)
        start(PREV_SIB, h)
        start(PREV_Y, h)

    def pass_two(h):
        arrived(PREV_Y, h)
        start(PASS_PREV, h)

    part = half // 2

    def wide_at(which, n, width_from, width):
        rows = pl.ds(pl.multiple_of(which * half + core * part, 16), part)
        return S, rows, pl.ds(pl.multiple_of(n * WIDE + width_from, 128), width)

    def down_at(which, n, row_from, rows, col_from, cols):
        return (pl.ds(pl.multiple_of(row_from, 16), rows),
                pl.ds(pl.multiple_of(which * tall + n * 256 + col_from, 128), cols))

    def weights(stage, a, n):
        which = y if stage == 0 else 1 - y
        rows = core * half
        if a == 0:
            size = [(z * 256 + x * 128, 128), (z * 256 + x * 128, 128), (z * 256, 256), (0, 512)][stage]
            region = pair.at[wide_at(which, n, *size)]
        else:
            size = [(rows + z * part, part, x * 128, 128), (rows + z * part, part, x * 128, 128),
                    (rows + z * part, part, 0, 256), (rows, half, 0, 256)][stage]
            region = down.at[down_at(which, n, *size)]
        partner = (over_y, over_x, over_z, sibling)[stage]
        return Route(region, region, w_send.at[stage, a, n], w_recv.at[stage, a, n], partner)

    def hand_on(stage, a, n):
        weights(stage - 1, a, n).arrived()
        weights(stage, a, n).start()

    def store(a, n):
        if a == 0:
            cols = pl.ds(pl.multiple_of(n * WIDE, 128), WIDE)
            return [pltpu.make_async_copy(pair.at[i, :, cols], out.at[:, cols], store_sem.at[i, n])
                    for i, out in enumerate((gate_out, up_out))]
        copies = []
        for which in range(2):
            some = pl.ds(pl.multiple_of(which * tall + n * 256, 128), 256)
            copies.append(pltpu.make_async_copy(down.at[:, some], down_out.at[:, some], store_sem.at[2 + which, n]))
        return copies

    def keep(a, n):
        weights(3, a, n).arrived()
        for copy in store(a, n):
            copy.start()

    def wo_part(which):
        return wo.at[pl.ds(pl.multiple_of(which * half + core * part, 16), part), :]

    wo_across = Route(wo_part(y), wo_part(y), wo_send.at[0], wo_recv.at[0], over_y)
    wo_within = Route(wo_part(1 - y), wo_part(1 - y), wo_send.at[1], wo_recv.at[1], sibling)
    wo_store = pltpu.make_async_copy(wo, wo_out, store_sem.at[0, WEIGHT_CHUNKS])

    def first(kind, i, which_x):
        row, count = FIRST_ROWS[which_x][i]
        at = (y if kind == 0 else 1 - y) * half + core * part + row
        region = w_qkv.at[pl.ds(pl.multiple_of(at, 16), count), :]
        return Route(region, region, first_send.at[kind, i], first_recv.at[kind, i], over_y if kind == 0 else over_x)

    def by_x(act, swap=False):
        for which_x in range(2):
            @pl.when(x == (1 - which_x if swap else which_x))
            def _(which_x=which_x):
                act(which_x)

    def first_part(which):
        return w_qkv.at[pl.ds(pl.multiple_of(which * half + core * part, 16), part), :]

    first_within = Route(first_part(1 - y), first_part(1 - y), first_send.at[2, 0], first_recv.at[2, 0], sibling)
    gains_across = Route(gains.at[own_rows, :], gains.at[own_rows, :], first_send.at[2, 1], first_recv.at[2, 1], over_y)
    first_store = pltpu.make_async_copy(w_qkv, qkv_out, store_sem.at[1, WEIGHT_CHUNKS])

    def across(n):
        for a in range(2):
            weights(0, a, n).start()

    def onward(stage, n):
        for a in range(2):
            hand_on(stage, a, n)

    for copy in flips:
        copy.wait()
    for i in range(2):
        w_qkv[own_rows, i * KV_HEADS * HEAD_DIM : (i + 1) * KV_HEADS * HEAD_DIM] = kv_flip[i].T
    loads[0].wait()
    loads[1].wait()
    gains_across.start()
    by_x(lambda which_x: [first(0, i, which_x).start() for i in range(2)])
    for copy in loads[2:]:
        copy.start()

    value = x_ref[...].astype(F32)
    scale = lax.rsqrt(jnp.mean(value * value, axis=0, keepdims=True) + EPSILON)
    scale_ref[...] = scale
    gains_across.arrived()
    h_ref[...] = (value * scale * gains[:, 0:1].astype(F32)).astype(BF16)
    for copy in loads[2:]:
        copy.wait()

    for i in range(2):
        def pass_first(which_x, i=i):
            first(0, i, which_x).arrived()
            first(1, i, which_x).start()

        by_x(pass_first)
        across(i)
    across(2)
    for i in range(2):
        by_x(lambda which_x, i=i: first(1, i, which_x).arrived(), swap=True)
    first_within.start()
    onward(1, 0)
    first_within.arrived()
    first_store.start()

    kv_width = KV_HEADS * HEAD_DIM
    turn = HEAD_DIM // 2

    def rotated(values):
        one, two = values[:turn], values[turn:]
        cos, sin = cosine[...], sine[...]
        return jnp.concatenate([one * cos - two * sin, two * cos + one * sin], axis=0)

    keys_values = over_first(w_qkv[:, : 2 * kv_width], h_ref[...])
    for h in range(KV_HEADS):
        at = h * HEAD_DIM
        both = jnp.concatenate(
            [rotated(keys_values[at : at + HEAD_DIM]), keys_values[kv_width + at : kv_width + at + HEAD_DIM]], axis=0
        ).astype(BF16)
        slot(h, 4 + j)[...] = both.T
        if h < 2:
            for route in (OWN_Y, OWN_NEXT, OWN_SIB):
                start(route, h)
    onward(2, 0)
    onward(1, 1)
    queries_all = over_first(w_qkv[:, 2 * kv_width :], h_ref[...])
    for h in range(HEADS):
        at = h * HEAD_DIM
        q_ref[at : at + HEAD_DIM, :] = rotated(queries_all[at : at + HEAD_DIM]).astype(BF16)
    pass_one(0)
    onward(2, 1)
    pass_two(0)

    def window(h):
        return pltpu.make_async_copy(
            kv.at[h, pl.ds(pl.multiple_of(j * own, own), 5 * own), :], kv_out.at[h], kv_sem.at[h])

    blocks = own // CHUNK
    third = GROUP * CHUNK

    def block(h, n, spans, diagonal):
        both = kv[h, pl.ds(pl.multiple_of(n * own, own), own), :]
        keys = both[:, :HEAD_DIM]
        values = jnp.concatenate([both[:, HEAD_DIM:].T, jnp.ones((16, own), BF16)], axis=0)
        begin_at = (n - 4 - j) * own
        for b in range(blocks):
            low_at, high_at = spans[b]
            low = low_ref[:, b * CHUNK : (b + 1) * CHUNK]
            for r in range(GROUP):
                cols = pl.ds(b * third + r * CHUNK, CHUNK)
                rows = pl.ds(pl.multiple_of(h * GROUP * HEAD_DIM + r * HEAD_DIM, HEAD_DIM), HEAD_DIM)
                queries = q_ref[rows, b * CHUNK : (b + 1) * CHUNK]
                old = top[:, cols]
                high = jnp.full((8, CHUNK), MASKED, F32)
                for at in range(low_at, high_at, STRIP):
                    rows = slice(at, at + STRIP)
                    s = masked(dot(keys[rows], queries), begin_at + at, low, b * CHUNK if diagonal else None)
                    s_all[rows, cols] = s
                    high = jnp.maximum(high, jnp.max(s.reshape(STRIP // 8, 8, CHUNK), axis=0))
                new = jnp.maximum(old, jnp.max(high, axis=0, keepdims=True))
                bound = new * SCALE2
                for at in range(low_at, high_at, STRIP):
                    rows = slice(at, at + STRIP)
                    p_all[rows, cols] = jnp.exp2(s_all[rows, cols] * SCALE2 - bound).astype(BF16)
                shrink[:, cols] = jnp.exp2(old * SCALE2 - bound)
                top[:, cols] = new
        for b in range(blocks):
            low_at, high_at = spans[b]
            cols = pl.ds(b * third, third)
            acc[:, cols] = acc[:, cols] * shrink[:, cols] + dot(values[:, low_at:high_at], p_all[low_at:high_at, cols])

    every = [(0, own)] * blocks
    plan = [(4 + j, [(0, (b + 1) * CHUNK) for b in range(blocks)], True),
            (j, [(b * CHUNK, own) for b in range(blocks)], False),
            (j + 2, every, False), (j + 1 + 2 * y, every, False), (j + 3 - 2 * y, every, False)]
    spots = len(plan)
    steps = [(functools.partial(hand_on, 1), 0, 2), (functools.partial(hand_on, 2), 3, 2),
             (functools.partial(hand_on, 3), 1, 1), (keep, 4, 1)]

    def head(h, carry):
        top[...] = jnp.full(top.shape, MASKED, F32)
        acc[...] = jnp.zeros(acc.shape, F32)

        for p in range(spots):
            if p == 0:
                @pl.when(h < KV_HEADS - 1)
                def _():
                    pass_one(h + 1)

                @pl.when(h < KV_HEADS - 2)
                def _():
                    for route in (OWN_Y, OWN_NEXT, OWN_SIB):
                        start(route, h + 2)

                pl.when(h == 0)(lambda: onward(3, 0))
            if p == 1:
                pl.when(h < KV_HEADS - 3)(lambda: across(h + 3))
                pl.when(h == 2)(lambda: wo_across.start())
            if p == 2:
                arrived(PREV_SIB, h)
                arrived(OWN_SIB, h)
            if p == 4:
                pl.when(h < KV_HEADS - 1)(lambda: pass_two(h + 1))
                arrived(PASS_PREV, h)
                arrived(PASS_OWN, h)

                @pl.when(h == KV_HEADS - 1)
                def _():
                    wo_across.arrived()
                    wo_within.start()
            if p == 1:
                pl.when(h == 0)(lambda: keep(0, 0))
            block(h, *plan[p])
            for step, spot, ahead in reversed(steps):
                for a in range(2):
                    if (p - a - spot) % spots == 0:
                        n = h + ahead + (p - a - spot) // spots
                        fits = jnp.logical_and(n >= (1 if ahead == 1 and step is not keep else 0), n < WEIGHT_CHUNKS)
                        fits = jnp.logical_and(fits, n >= 2) if ahead == 2 else fits
                        pl.when(fits)(lambda step=step, a=a, n=n: step(a, n))

        window(h).start()
        for r in range(GROUP):
            rows = pl.ds(pl.multiple_of(h * GROUP * HEAD_DIM + r * HEAD_DIM, HEAD_DIM), HEAD_DIM)
            for b in range(blocks):
                cols = pl.ds(b * third + r * CHUNK, CHUNK)
                total = acc[HEAD_DIM : HEAD_DIM + 1, cols]
                o_ref[rows, b * CHUNK : (b + 1) * CHUNK] = (acc[:HEAD_DIM, cols] / total).astype(BF16)
                lse_ref[h, r : r + 1, b * CHUNK : (b + 1) * CHUNK] = top[:, cols] * SCALE2 + jnp.log2(total)
        return carry

    lax.fori_loop(0, KV_HEADS, head, 0)
    wo_within.arrived()
    wo_store.start()

    def finish(h, carry):
        for a in range(2):
            for stage in range(4):
                weights(stage, a, h).sent()
            for copy in store(a, h):
                copy.wait()
        for route in range(7):
            pl.when(sent_if[route])(lambda route=route: halo(route, h).sent())
        window(h).wait()
        return carry

    lax.fori_loop(0, KV_HEADS, finish, 0)
    for route in (wo_across, wo_within, first_within, gains_across):
        route.sent()
    by_x(lambda which_x: [first(kind, i, which_x).sent() for kind in range(2) for i in range(2)])
    wo_store.wait()
    first_store.wait()


def attend(low, cosine, sine, x, w_query, w_key_t, w_value_t, gains, w_output, w_gate, w_up, w_down_t, dp_size):
    own = x.shape[1]
    width = GROUP * own
    any_spec = pl.BlockSpec(memory_space=pl.ANY)
    vmem = pl.BlockSpec(memory_space=pltpu.VMEM)
    later = [jax.ShapeDtypeStruct((2 * w.shape[0], w.shape[1]), BF16) for w in (w_output, w_gate, w_up)]
    later.insert(0, jax.ShapeDtypeStruct((D, D + 2 * w_key_t.shape[0]), BF16))
    later.append(jax.ShapeDtypeStruct((w_down_t.shape[0], 2 * w_down_t.shape[1]), BF16))
    return pl.pallas_call(
        functools.partial(forward_kernel, dp_size // 2),
        out_shape=[
            jax.ShapeDtypeStruct((D, own), BF16),
            jax.ShapeDtypeStruct((KV_HEADS, 8, own), F32),
            jax.ShapeDtypeStruct((D, own), BF16),
            jax.ShapeDtypeStruct((D, own), BF16),
            jax.ShapeDtypeStruct((1, own), F32),
            jax.ShapeDtypeStruct((2 * gains.shape[0], gains.shape[1]), BF16),
            jax.ShapeDtypeStruct((KV_HEADS, 5 * own, 2 * HEAD_DIM), BF16),
        ] + later,
        in_specs=[vmem] * 4 + [any_spec] * 8,
        out_specs=[vmem] * 6 + [any_spec] * 6,
        scratch_shapes=[pltpu.VMEM((KV_HEADS, 8 * own, 2 * HEAD_DIM), BF16), pltpu.VMEM((2,) + w_key_t.shape, BF16)]
        + [pltpu.VMEM(shape, BF16) for shape in (later[0].shape, later[1].shape, (2,) + later[2].shape, later[4].shape)]
        + [
            pltpu.VMEM((1, width), F32),
            pltpu.VMEM((HEAD_DIM + 16, width), F32),
            pltpu.VMEM((1, width), F32),
            pltpu.VMEM((own, width), F32),
            pltpu.VMEM((own, width), BF16),
            pltpu.SemaphoreType.DMA((KV_HEADS,)),
            pltpu.SemaphoreType.DMA((8,)),
            pltpu.SemaphoreType.DMA((4, WEIGHT_CHUNKS + 1)),
            pltpu.SemaphoreType.DMA((7, KV_HEADS)),
            pltpu.SemaphoreType.DMA((7, KV_HEADS)),
            pltpu.SemaphoreType.DMA((4, 2, WEIGHT_CHUNKS)),
            pltpu.SemaphoreType.DMA((4, 2, WEIGHT_CHUNKS)),
            pltpu.SemaphoreType.DMA((2,)),
            pltpu.SemaphoreType.DMA((2,)),
            pltpu.SemaphoreType.DMA((3, 2)),
            pltpu.SemaphoreType.DMA((3, 2)),
        ],
        compiler_params=pltpu.CompilerParams(
            collective_id=2, has_side_effects=True, vmem_limit_bytes=56 * 1024 * 1024),
        name="attend",
    )(low, cosine, sine, x, w_query, w_key_t, w_value_t, gains, w_output, w_gate, w_up, w_down_t)


FEED = 256


def middle_kernel(bits, groups, low_ref, cosine, sine, gains_ref, att_ref, lse_ref,
                  x_in, g_in, q_in, kv_in, wo_in, gate_in, up_in, down_in,
                  out_ref, dx_ref, branch_ref, row_ref, gate_out, up_out, down_out, dq_out, dkv_out,
                  ring, ring_down, far_in, sib_in, far_y, own_y, next_in, halo_send, halo_recv, feed_sem, load_sem, *scratch):
    own = x_in.shape[1]
    half_ff = gate_in.shape[1] // 2
    chunks = half_ff // FEED
    dp, y = place()
    core = dp % 2
    k = dp // 2
    j = 2 * core + y
    j_y = 2 * core + 1 - y
    has_prev, has_next = k > 0, k < groups - 1
    first_core, last_core = core == 0, core == 1
    half = D // 4
    sums = Sums(bits, None, [[gate_out, up_out], [down_out]], scratch, (ring, ring_down))

    barrier = pltpu.get_barrier_semaphore()
    for partner in sums.partners:
        pl.semaphore_signal(barrier, inc=1, device_id=partner, device_id_type=MESH)

    @pl.when(has_next)
    def _():
        pl.semaphore_signal(barrier, inc=1, device_id=(dp + 2, y), device_id_type=MESH)

    spots = 5
    begins = {0: (-1, 1, 4), 1: (0, 1, 3), 2: (1, 1, 3), 3: (3, 0, 2), 4: (4, 0, 1)}
    events = {(0, 0): [(sums.start_y, a, chunks - 2) for a in sums.arrays], (0, 2): [(sums.start_y, a, chunks - 1) for a in sums.arrays]}
    for n in range(chunks):
        turn, spot, lag = begins[n]
        for s in range(len(sums.stages)):
            for a in sums.arrays:
                at = turn * spots + spot + a + lag * s
                events.setdefault((at // spots, at % spots), []).insert(0, (sums.stages[s], a, n))
    last_round = max(turn for turn, spot in events)

    def advance(p, h):
        if isinstance(h, int):
            for step, a, n in events.get((h, p), ()):
                step(a, n)
            return
        for turn in range(KV_HEADS):
            if (turn, p) in events:
                pl.when(h == turn)(lambda turn=turn: advance(p, turn))

    def feed_phase(weights, wo, h_t, g_t, x, h, g, acc):
        def load(n, s):
            cols = pl.ds(pl.multiple_of(s * half_ff + n * FEED, 128), FEED)
            return [pltpu.make_async_copy(w.at[:, cols], weights.at[s, i], feed_sem.at[s, i])
                    for i, w in enumerate((gate_in, up_in, down_in))]

        first = [pltpu.make_async_copy(a, b, load_sem.at[i]) for i, (a, b) in enumerate(((x_in, h_t), (g_in, g_t), (wo_in, wo)))]
        for copy in first + load(0, 0):
            copy.start()
        for copy in first:
            copy.wait()
        gain = gains_ref[:, 1:2].astype(F32)
        x[...] = h_t[...].astype(F32) + over_first(wo[...], att_ref[...])
        scale = lax.rsqrt(jnp.mean(x[...] * x[...], axis=0, keepdims=True) + EPSILON)
        h_t[...] = (x[...] * scale * gain).astype(BF16)
        h[...] = h_t[...].T
        g[...] = g_t[...].T
        acc[...] = x[...]
        dx_ref[...] = jnp.zeros(dx_ref.shape, F32)

        @pl.when(has_prev)
        def _():
            pl.semaphore_wait(barrier, len(sums.partners) + 1)

        @pl.when(jnp.logical_not(has_prev))
        def _():
            pl.semaphore_wait(barrier, len(sums.partners))

        def step(n, s):
            for copy in load(n, s):
                copy.wait()
            if s == 0:
                for copy in load(n, 1):
                    copy.start()
            else:
                @pl.when(n < chunks - 1)
                def _():
                    for copy in load(n + 1, 0):
                        copy.start()

            w_gate, w_up, w_down = weights[s, 0], weights[s, 1], weights[s, 2]
            gate = dot(h[...], w_gate)
            upper = dot(h[...], w_up)
            dm = dot(g[...], w_down)
            sigmoid = 1.0 / (1.0 + jnp.exp(-gate))
            active = gate * sigmoid
            inner = (active * upper).astype(BF16)
            dgate = (dm * upper * sigmoid * (1.0 + gate * (1.0 - sigmoid))).astype(BF16)
            dup = (dm * active).astype(BF16)
            acc[...] += against_rows(w_down, inner)
            dx_ref[...] += against_rows(w_gate, dgate) + against_rows(w_up, dup)
            cols = slice(s * FEED, (s + 1) * FEED)
            for c, shares in ((core, sums.own_share), (1 - core, sums.sibling_share)):
                for which in range(2):
                    rows = pl.ds(pl.multiple_of(which * 2 * half + c * half, 16), half)
                    left = h_t[rows, :]
                    for i, right in enumerate((dgate, dup)):
                        shares(0, n)[i, which, :, cols] = dot(left, right).astype(BF16)
                rows = pl.ds(pl.multiple_of(c * 2 * half, 16), 2 * half)
                shares(1, n)[0, s] = dot(g_t[rows, :], inner).astype(BF16)

        def round_of(n, carry):
            @pl.when(n > 1)
            def _():
                for a in sums.arrays:
                    sums.core_sent(a, n - 2)

            step(n, 0)

            @pl.when(jnp.logical_and(n > 0, n < chunks - 1))
            def _():
                for a in sums.arrays:
                    sums.start_y(a, n - 1)

            pl.when(n == chunks - 1)(lambda: (advance(1, -1), advance(2, -1))[0])
            step(n, 1)
            for a in sums.arrays:
                sums.start_core(a, n)
            pl.when(n == chunks - 1)(lambda: (advance(3, -1), advance(4, -1))[0])
            return carry

        lax.fori_loop(0, chunks, round_of, 0)
        out_ref[...] = acc[...].astype(BF16)
        dh = dx_ref[...]
        acc[...] = dh * (x[...] * scale)
        ones = jnp.ones((8, own), F32)
        row_ref[...] = lax.dot_general(ones, acc[...], (((1,), (1,)), ((), ())), precision=lax.Precision.HIGHEST,
                                       preferred_element_type=F32)
        mean = jnp.sum(acc[...] * gain, axis=0, keepdims=True) * (1.0 / D)
        dx = g_t[...].astype(F32) + scale * (dx_ref[...] * gain - x[...] * scale * mean)
        dx_ref[...] = dx
        branch_ref[...] = dx.astype(BF16)

    pl.run_scoped(
        feed_phase,
        pltpu.VMEM((2, 3, D, FEED), BF16),
        pltpu.VMEM((D, D), BF16),
        pltpu.VMEM((D, own), BF16),
        pltpu.VMEM((D, own), BF16),
        pltpu.VMEM((D, own), F32),
        pltpu.VMEM((own, D), BF16),
        pltpu.VMEM((own, D), BF16),
        pltpu.VMEM((D, own), F32),
    )
    for n in (chunks - 2, chunks - 1):
        for a in sums.arrays:
            sums.core_sent(a, n)

    blocks = own // CHUNK
    third = GROUP * CHUNK

    def attention_phase(wo, q, do, kv, q_all, do_all, q_rows, do_rows, delta, dq_acc, p_all, ds_all, part, dq, dkv):
        first = [pltpu.make_async_copy(a, b, load_sem.at[i]) for i, (a, b) in enumerate(((wo_in, wo), (q_in, q)))]

        def window(h, at):
            return pltpu.make_async_copy(kv_in.at[h], kv.at[at], feed_sem.at[at, 0])

        for copy in first + [window(0, 0)]:
            copy.start()
        part[...] = jnp.zeros(part.shape, BF16)
        for copy in first:
            copy.wait()
        do[...] = dot(wo[...], branch_ref[...]).astype(BF16)

        def slot(h, n):
            return part.at[h, pl.ds(pl.multiple_of(n * own, own), own), :]

        def halo(route, h):
            before = jnp.maximum(dp - 2, 0)
            sems = (halo_send.at[route, h], halo_recv.at[route, h])
            if route == PASS_PREV:
                return Route(slot(h, j_y + 2 - 4 * core), far_in.at[h], *sems, sums.sibling)
            if route == PASS_OWN:
                return Route(slot(h, 2 + j_y), far_in.at[h], *sems, sums.sibling)
            if route == PREV_SIB:
                return Route(slot(h, j + 2 - 4 * core), sib_in.at[h], *sems, sums.sibling)
            if route == OWN_SIB:
                return Route(slot(h, 2 + j), sib_in.at[h], *sems, sums.sibling)
            if route == PREV_Y:
                return Route(slot(h, j_y), far_y.at[h], *sems, sums.over_y)
            if route == OWN_Y:
                return Route(slot(h, 4 + j_y), own_y.at[h], *sems, sums.over_y)
            return Route(slot(h, j), next_in.at[h], *sems, (before, y))

        got_if = {
            OWN_SIB: first_core, OWN_Y: j != 3, OWN_NEXT: has_next, PASS_OWN: first_core,
            PREV_SIB: jnp.logical_and(last_core, has_prev), PREV_Y: jnp.logical_and(j != 0, has_prev),
            PASS_PREV: jnp.logical_and(last_core, has_prev),
        }
        sent_if = {
            OWN_SIB: last_core, OWN_Y: j != 2, OWN_NEXT: has_prev, PASS_OWN: last_core,
            PREV_SIB: jnp.logical_and(first_core, has_prev), PREV_Y: jnp.logical_and(j != 1, has_prev),
            PASS_PREV: jnp.logical_and(first_core, has_prev),
        }

        def start(route, h):
            pl.when(sent_if[route])(lambda: halo(route, h).start())

        def take(route, h, n, box):
            @pl.when(got_if[route])
            def _():
                halo(route, h).arrived()
                spot = slot(h, n)
                spot[...] = spot[...] + box[h]

        def return_one(h):
            for route in (PASS_PREV, PASS_OWN, PREV_SIB, OWN_SIB):
                start(route, h)

        def return_two(h):
            take(PASS_PREV, h, j_y, far_in)
            take(PASS_OWN, h, 4 + j_y, far_in)
            start(PREV_Y, h)
            start(OWN_Y, h)

        def return_three(h):
            for route, n, box in ((PREV_SIB, j, sib_in), (OWN_SIB, 4 + j, sib_in), (PREV_Y, j, far_y), (OWN_Y, 4 + j, own_y)):
                take(route, h, n, box)
            start(OWN_NEXT, h)

        def return_four(h):
            dkv[h] = slot(h, 4 + j)[...].astype(F32)

            @pl.when(has_next)
            def _():
                halo(OWN_NEXT, h).arrived()
                dkv[h] = dkv[h] + next_in[h].astype(F32)

        def head_rows(h, r):
            return pl.ds(pl.multiple_of(h * GROUP * HEAD_DIM + r * HEAD_DIM, HEAD_DIM), HEAD_DIM)

        def prepare(h):
            for r in range(GROUP):
                rows = head_rows(h, r)
                for b in range(blocks):
                    cols = pl.ds(b * third + r * CHUNK, CHUNK)
                    from_cols = slice(b * CHUNK, (b + 1) * CHUNK)
                    grad, queries = do[rows, from_cols], q[rows, from_cols]
                    q_all[:, cols] = queries
                    do_all[:, cols] = grad
                    q_rows[cols, :] = queries.T
                    do_rows[cols, :] = grad.T
                    delta[:, cols] = jnp.sum(grad.astype(F32) * att_ref[rows, from_cols].astype(F32), axis=0, keepdims=True)
            dq_acc[...] = jnp.zeros(dq_acc.shape, F32)

        def block(h, at, n, spans, diagonal):
            both = kv[at, n * own : (n + 1) * own, :]
            keys, values = both[:, :HEAD_DIM], both[:, HEAD_DIM:]
            begin_at = (n - 4) * own
            for i in range(own // CHUNK):
                row = i * CHUNK
                some_keys, some_values = keys[row : row + CHUNK], values[row : row + CHUNK]
                using = [b for b in range(blocks) if spans[b][0] <= row < spans[b][1]]
                for b in using:
                    low = low_ref[:, b * CHUNK : (b + 1) * CHUNK]
                    for r in range(GROUP):
                        cols = pl.ds(b * third + r * CHUNK, CHUNK)
                        lse = lse_ref[h, r : r + 1, b * CHUNK : (b + 1) * CHUNK]
                        s = masked(dot(some_keys, q_all[:, cols]), begin_at + row, low, b * CHUNK if diagonal and b == i else None)
                        p = jnp.exp2(s * SCALE2 - lse)
                        p_all[:, cols] = p.astype(BF16)
                        ds_all[:, cols] = (p * (dot(some_values, do_all[:, cols]) - delta[:, cols])).astype(BF16)
                cols = pl.ds(using[0] * third, len(using) * third)
                dq_acc[:, cols] += dot(some_keys.T, ds_all[:, cols])
                dk = dot(ds_all[:, cols], q_rows[cols, :]) * 0.125
                dv = dot(p_all[:, cols], do_rows[cols, :])
                spot = pl.ds(pl.multiple_of((n + j) * own + row, CHUNK), CHUNK)
                part[h, spot, :] = jnp.concatenate([dk, dv], axis=1).astype(BF16)

        every = [(0, own)] * blocks
        plan = [(0, [(b * CHUNK, own) for b in range(blocks)], False), (1, every, False), (2, every, False),
                (3, every, False), (4, [(0, (b + 1) * CHUNK) for b in range(blocks)], True)]
        def guarded(fn, h):
            pl.when(jnp.logical_and(h >= 0, h < KV_HEADS))(lambda: fn(h))

        def head(h, carry):
            at = h % 2
            window(h, at).wait()

            @pl.when(h < KV_HEADS - 1)
            def _():
                window(h + 1, 1 - at).start()

            prepare(h)
            for p in range(spots):
                block(h, at, *plan[p])
                advance(p, h)
                if p == 1:
                    guarded(return_two, h - 1)
                if p == 4:
                    guarded(return_three, h - 3)
            return_one(h)
            for r in range(GROUP):
                rows = head_rows(h, r)
                for b in range(blocks):
                    value = dq_acc[:, pl.ds(b * third + r * CHUNK, CHUNK)] * 0.125
                    spot = slice(b * CHUNK, (b + 1) * CHUNK)
                    cos, sin = cosine[:, spot], sine[:, spot]
                    one, two = value[: HEAD_DIM // 2], value[HEAD_DIM // 2 :]
                    back = jnp.concatenate([one * cos + two * sin, two * cos - one * sin], axis=0)
                    dq[rows, spot] = back.astype(BF16)
            return carry

        lax.fori_loop(0, KV_HEADS, head, 0)
        last = KV_HEADS - 1
        after = [(return_two, last), (return_three, 2), (return_three, 3), (return_four, 0), (return_four, 1),
                 (return_three, last), (return_four, 2), (return_four, 3)]
        for i in range((last_round - KV_HEADS + 1) * spots):
            if i < len(after):
                fn, h = after[i]
                fn(h)
            advance(i % spots, KV_HEADS + i // spots)
        for fn, h in after[(last_round - KV_HEADS + 1) * spots :]:
            fn(h)
        return_four(last)
        stores = [pltpu.make_async_copy(dq, dq_out, load_sem.at[0]), pltpu.make_async_copy(dkv, dkv_out, load_sem.at[1])]
        for store in stores:
            store.start()

        def finish(h, carry):
            for route in range(7):
                pl.when(sent_if[route])(lambda route=route: halo(route, h).sent())
            return carry

        lax.fori_loop(0, KV_HEADS, finish, 0)
        for store in stores:
            store.wait()

    width = GROUP * own
    pl.run_scoped(
        attention_phase,
        pltpu.VMEM((D, D), BF16),
        pltpu.VMEM((D, own), BF16),
        pltpu.VMEM((D, own), BF16),
        pltpu.VMEM((2, 5 * own, 2 * HEAD_DIM), BF16),
        pltpu.VMEM((HEAD_DIM, width), BF16),
        pltpu.VMEM((HEAD_DIM, width), BF16),
        pltpu.VMEM((width, HEAD_DIM), BF16),
        pltpu.VMEM((width, HEAD_DIM), BF16),
        pltpu.VMEM((1, width), F32),
        pltpu.VMEM((HEAD_DIM, width), F32),
        pltpu.VMEM((CHUNK, width), BF16),
        pltpu.VMEM((CHUNK, width), BF16),
        pltpu.VMEM((KV_HEADS, 8 * own, 2 * HEAD_DIM), BF16),
        pltpu.VMEM((D, own), BF16),
        pltpu.VMEM((KV_HEADS, own, 2 * HEAD_DIM), F32),
    )

    for n in range(chunks):
        for a in sums.arrays:
            sums.drain(a, n)


def middle_and_back(low, cosine, sine, gains, attended, lse, x, cotangent, queries, both, w_output, w_gate, w_up, w_down_t,
           dp_size):
    own = x.shape[1]
    ff = w_gate.shape[1]
    bits = dp_size.bit_length() - 1
    half = D // 4
    chunks = ff // WIDE
    any_spec = pl.BlockSpec(memory_space=pl.ANY)
    vmem = pl.BlockSpec(memory_space=pltpu.VMEM)
    box = pltpu.VMEM((KV_HEADS, own, 2 * HEAD_DIM), BF16)
    return pl.pallas_call(
        functools.partial(middle_kernel, bits, dp_size // 2),
        out_shape=[
            jax.ShapeDtypeStruct((D, own), BF16),
            jax.ShapeDtypeStruct((D, own), F32),
            jax.ShapeDtypeStruct((D, own), BF16),
            jax.ShapeDtypeStruct((8, D), F32),
            jax.ShapeDtypeStruct((D // 2, ff), BF16),
            jax.ShapeDtypeStruct((D // 2, ff), BF16),
            jax.ShapeDtypeStruct((D, ff // 2), BF16),
            jax.ShapeDtypeStruct((D, own), BF16),
            jax.ShapeDtypeStruct((KV_HEADS, own, 2 * HEAD_DIM), F32),
        ],
        in_specs=[vmem] * 6 + [any_spec] * 8,
        out_specs=[vmem] * 4 + [any_spec] * 5,
        scratch_shapes=[
            pltpu.VMEM((2, 2, 2, half, WIDE), BF16),
            pltpu.VMEM((2, 1, 2, 2 * half, FEED), BF16),
            box, box, box, box, box,
            pltpu.SemaphoreType.DMA((7, KV_HEADS)),
            pltpu.SemaphoreType.DMA((7, KV_HEADS)),
            pltpu.SemaphoreType.DMA((2, 3)),
            pltpu.SemaphoreType.DMA((3,)),
        ] + Sums.scratch(bits, 2, 1, chunks, half),
        compiler_params=pltpu.CompilerParams(
            collective_id=3, has_side_effects=True, vmem_limit_bytes=60 * 1024 * 1024),
        name="middle",
    )(low, cosine, sine, gains, attended, lse, x, cotangent, queries, both, w_output, w_gate, w_up, w_down_t)


def finish_kernel(bits, chunks, dq, dkv, cosine, sine, hidden, x, scale, gains, w_qkv, attended, branch, middle, feed_row,
                  out, gains_out, tokens_out, pack, grads, prod, *rest):
    sums = Sums(bits, pack, [[out]], rest[:-5])
    g_loc, g_in, g_sem, g_send, g_recv = rest[-5:]
    half = HEAD_DIM // 2
    rows = pack.shape[2]
    greet(sums.partners)

    def gain_route(n):
        return Route(g_loc.at[n], g_in.at[n], g_send.at[n], g_recv.at[n], sums.partners[n])

    def unrotate(values, at):
        one, two = values[:half], values[half:]
        cos, sin = cosine[...], sine[...]
        grads[at : at + half, :] = (one * cos + two * sin).astype(BF16)
        grads[at + half : at + HEAD_DIM, :] = (two * cos - one * sin).astype(BF16)

    def columns(low, high):
        parts = []
        if low < D:
            parts.append((attended, branch, low, min(high, D)))
        if high > D:
            parts.append((hidden, grads, max(low, D) - D, high - D))
        return [against_rows(left[...], right[a:b, :]) for left, right, a, b in parts]

    def fill(n):
        parts = columns(n * WIDE, (n + 1) * WIDE)
        value = parts[0] if len(parts) == 1 else jnp.concatenate(parts, axis=1)
        value = value.astype(BF16)
        for which in range(2):
            pack[0, which, :, n * WIDE : (n + 1) * WIDE] = value[which * rows : (which + 1) * rows]
        sums.start_core(0, n)

    def heads():
        grads[:D, :] = dq[...]
        for h in range(KV_HEADS):
            both = dkv[h].T
            unrotate(both[:HEAD_DIM], D + h * HEAD_DIM)
            at = D + (KV_HEADS + h) * HEAD_DIM
            grads[at : at + HEAD_DIM, :] = both[HEAD_DIM:].astype(BF16)

    def hidden_grad():
        keys_values = 2 * KV_HEADS * HEAD_DIM
        dh = dot(w_qkv[:, keys_values:], grads[:D, :]) + dot(w_qkv[:, :keys_values], grads[D:, :])
        tokens_out[...] = dh
        prod[...] = dh * (x[...].astype(F32) * scale[...])
        g_loc[0] = jnp.zeros(g_loc.shape[1:], F32)
        ones = jnp.ones((8, dh.shape[1]), F32)
        total = lax.dot_general(ones, prod[...], (((1,), (1,)), ((), ())), precision=lax.Precision.HIGHEST,
                                preferred_element_type=F32)
        g_loc[0, 0:1, :] = total[0:1]
        g_loc[0, 1:2, :] = feed_row[0:1, :]
        gain_route(0).start()

    def tokens_grad():
        normed = x[...].astype(F32) * scale[...]
        gain = gains[:, 0:1].astype(F32)
        e = tokens_out[...] * gain
        mean = jnp.sum(prod[...] * gain, axis=0, keepdims=True) * (1.0 / D)
        tokens_out[...] = middle[...] + scale[...] * (e - normed * mean)

    def gain_step(n):
        gain_route(n - 1).arrived()
        g_loc[n] = g_loc[n - 1] + g_in[n - 1]
        if n < len(sums.partners):
            gain_route(n).start()

    work = [lambda: fill(0), lambda: (heads(), fill(1))] + [functools.partial(fill, n) for n in range(2, chunks)]
    work += [hidden_grad, tokens_grad] + [functools.partial(gain_step, n + 1) for n in range(len(sums.partners))]
    steps = [sums.start_y] + sums.stages
    delay = [1, 3]
    while len(delay) < len(steps):
        delay.append(delay[-1] + 1)
    for tick in range(max(chunks + delay[-1], len(work))):
        if tick < len(work):
            work[tick]()
        for s in [0] + list(range(len(steps) - 1, 0, -1)):
            if 0 <= tick - delay[s] < chunks:
                steps[s](0, tick - delay[s])
    store = pltpu.make_async_copy(g_loc.at[len(sums.partners)], gains_out, g_sem.at[0])
    store.start()
    for n in range(chunks):
        sums.core_sent(0, n)
        sums.drain(0, n)
    for n in range(len(sums.partners)):
        gain_route(n).sent()
    store.wait()


def finish(dq, dkv, cosine, sine, hidden, x, scale, gains, w_qkv, attended, branch, middle, feed_row, dp_size):
    bits = dp_size.bit_length() - 1
    own = x.shape[1]
    total = 2 * D + 2 * KV_HEADS * HEAD_DIM
    chunks = total // WIDE
    any_spec = pl.BlockSpec(memory_space=pl.ANY)
    vmem = pl.BlockSpec(memory_space=pltpu.VMEM)
    row = (8, D)
    return pl.pallas_call(
        functools.partial(finish_kernel, bits, chunks),
        out_shape=[
            jax.ShapeDtypeStruct((D // 2, total), BF16),
            jax.ShapeDtypeStruct(row, F32),
            jax.ShapeDtypeStruct((D, own), F32),
        ],
        in_specs=[vmem] * 13,
        out_specs=[any_spec, any_spec, vmem],
        scratch_shapes=[
            pltpu.VMEM((1, 2, D // 2, total), BF16),
            pltpu.VMEM((total - D, own), BF16),
            pltpu.VMEM((D, own), F32),
        ] + Sums.scratch(bits, 1, 0, chunks, D // 4) + [
            pltpu.VMEM((bits + 2,) + row, F32),
            pltpu.VMEM((bits + 1,) + row, F32),
            pltpu.SemaphoreType.DMA((1,)),
            pltpu.SemaphoreType.DMA((bits + 1,)),
            pltpu.SemaphoreType.DMA((bits + 1,)),
        ],
        compiler_params=pltpu.CompilerParams(
            collective_id=0, has_side_effects=True, vmem_limit_bytes=56 * 1024 * 1024),
        name="finish",
    )(dq, dkv, cosine, sine, hidden, x, scale, gains, w_qkv, attended, branch, middle, feed_row)


def positions(seq_lengths, first, count):
    ends = jnp.cumsum(seq_lengths)
    index = first + jnp.arange(count, dtype=jnp.int32)
    passed = index[:, None] >= ends[None, :]
    begin = jnp.max(jnp.where(passed, ends[None, :], 0), axis=1)
    return index - begin


def rotary_tables(position):
    half = HEAD_DIM // 2
    inverse = jnp.exp(-jnp.arange(half, dtype=F32) * (2.0 / HEAD_DIM) * jnp.log(THETA))
    angle = inverse[:, None] * position.astype(F32)[None, :]
    return jnp.cos(angle), jnp.sin(angle)


def shards(tokens, cotangent, w_query, w_key, w_value, w_output, w_gate, w_up, w_down, attention_gain, feed_gain, seq_lengths):
    own = tokens.shape[0]
    kv = KV_HEADS * HEAD_DIM
    first = lax.axis_index(("dp", "shard")) * own
    position = positions(seq_lengths, first, own)
    low = jnp.arange(own, dtype=jnp.int32) - position
    cosine, sine = rotary_tables(position)
    gains = jnp.where(jnp.arange(128)[None, :] == 0, attention_gain[:, None], feed_gain[:, None])
    dp_size = lax.axis_size("dp")
    (attended, log_total, queries, hidden_one, scale_one, gains, both_all,
     qkv_full, output_full, gate_full, up_full, down_full) = attend(
        low[None, :], cosine, sine, tokens.T, w_query, w_key.T, w_value.T, gains,
        w_output, w_gate, w_up, w_down.T, dp_size
    )
    output, grad_middle, grad_branch, feed_rows, sum_gate, sum_up, sum_down, grad_queries, grad_own = middle_and_back(
        low[None, :], cosine, sine, gains, attended, log_total, tokens.T, cotangent.T, queries,
        both_all, output_full, gate_full, up_full, down_full, dp_size
    )
    sum_pack, sum_gains, grad_tokens = finish(
        grad_queries, grad_own, cosine, sine, hidden_one, tokens.T, scale_one, gains, qkv_full,
        attended, grad_branch, grad_middle, feed_rows, dp_size
    )
    sum_pack = sum_pack.astype(F32)
    half = D // 2
    begin = lax.axis_index("shard") * half
    return (
        output.T,
        grad_tokens.T,
        sum_pack[:, D : 2 * D],
        sum_pack[:, 2 * D : 2 * D + kv],
        sum_pack[:, 2 * D + kv :],
        sum_pack[:, :D],
        sum_gate.astype(F32),
        sum_up.astype(F32),
        sum_down.astype(F32).T,
        lax.dynamic_slice_in_dim(sum_gains[0], begin, half),
        lax.dynamic_slice_in_dim(sum_gains[1], begin, half),
    )


def solution(mesh):
    return jax.shard_map(
        shards,
        mesh=mesh,
        in_specs=(
            P(("dp", "shard"), None),
            P(("dp", "shard"), None),
            P("shard", None),
            P("shard", None),
            P("shard", None),
            P("shard", None),
            P("shard", None),
            P("shard", None),
            P("shard", None),
            P("shard"),
            P("shard"),
            P(),
        ),
        out_specs=(
            P(("dp", "shard"), None),
            P(("dp", "shard"), None),
            P("shard", None),
            P("shard", None),
            P("shard", None),
            P("shard", None),
            P("shard", None),
            P("shard", None),
            P("shard", None),
            P("shard"),
            P("shard"),
        ),
        check_vma=False,
    )
```

```python
import functools

import jax
import jax.numpy as jnp
from jax import lax
from jax.experimental import pallas as pl
from jax.experimental.pallas import tpu as pltpu
from jax.sharding import PartitionSpec as P

D = 960
HEADS = 15
KV_HEADS = 5
GROUP = 3
HEAD_DIM = 64

EPSILON = 1e-05
THETA = 100000.0
MASKED = -1e30
LOG2E = 1.4426950408889634
SCALE2 = 0.125 * LOG2E

MESH = pl.DeviceIdType.MESH
WIDE = 512
CHUNK = 256
STRIP = 128
BF16 = jnp.bfloat16
F32 = jnp.float32


def dot(left, right):
    return lax.dot_general(left, right, (((1,), (0,)), ((), ())), preferred_element_type=F32)


def against_rows(left, right):
    return lax.dot_general(left, right, (((1,), (1,)), ((), ())), preferred_element_type=F32)


def over_first(left, right):
    return lax.dot_general(left, right, (((0,), (0,)), ((), ())), preferred_element_type=F32)


def masked(scores, start, low, diagonal):
    rows = start + lax.broadcasted_iota(jnp.int32, scores.shape, 0)
    valid = rows >= low
    if diagonal is not None:
        cols = diagonal + lax.broadcasted_iota(jnp.int32, scores.shape, 1)
        valid = jnp.logical_and(valid, rows <= cols)
    return jnp.where(valid, scores, MASKED)


def place():
    return lax.axis_index("dp"), lax.axis_index("shard")


def other(dp, y, bit):
    step = 1 << bit
    mine = (dp // step) % 2
    return (dp + step - 2 * step * mine, y)


def greet(partners):
    barrier = pltpu.get_barrier_semaphore()
    for partner in partners:
        pl.semaphore_signal(barrier, inc=1, device_id=partner, device_id_type=MESH)
    pl.semaphore_wait(barrier, len(partners))


class Route:
    def __init__(self, src, dst, send, recv, partner):
        self.make = lambda: pltpu.make_async_remote_copy(
            src_ref=src, dst_ref=dst, send_sem=send, recv_sem=recv, device_id=partner, device_id_type=MESH)

    def start(self):
        self.make().start()

    def arrived(self):
        self.make().wait_recv()

    def sent(self):
        self.make().wait_send()


class Sums:
    def __init__(self, bits, wides, tall, outs, scratch, rings=None, early=()):
        self.wides, self.tall, self.outs, self.rings, self.early = wides, tall, outs, rings, early
        self.boxes = [scratch[:7]] * len(wides) + [scratch[7:14]] * (tall is not None)
        self.put_sem, self.send_sem, self.recv_sem = scratch[-3:]
        self.arrays = len(self.boxes)
        self.half = D // 4
        dp, y = place()
        self.core, self.x, self.z, self.y = dp % 2, (dp // 2) % 2, (dp // 4) % 2, y
        self.sibling, self.over_y = other(dp, y, 0), (dp, 1 - y)
        self.over_x, self.over_z = other(dp, y, 1), other(dp, y, 2)
        self.extra = [other(dp, y, bit) for bit in range(3, bits)]
        self.partners = [self.sibling, self.over_y, self.over_x, self.over_z] + self.extra
        more = len(self.extra)
        self.stages = [self.start_x, self.start_z]
        self.stages += [functools.partial(self.more, step) for step in range(more + 1)]
        self.stages += [self.back_x, self.back_core, self.finish]

    @staticmethod
    def scratch(bits, wide_arrays, tall, chunks, half):
        more = bits - 3
        count = wide_arrays + tall

        def boxes(n, shapes):
            return [pltpu.VMEM((n, chunks) + shape, BF16) for shape in shapes]

        shared = [(half, 128), (max(more, 1), half, 128)]
        out = []
        if wide_arrays:
            out += boxes(wide_arrays, [(2, half, WIDE)] * 2 + [(half, WIDE), (half, 256)] + shared + [(2 * half, WIDE)])
        else:
            out += [None] * 7
        if tall:
            out += boxes(1, [(2, 2 * half, 256)] * 2 + [(2 * half, 256), (half, 256)] + shared + [(4 * half, 256)])
        return out + [
            pltpu.SemaphoreType.DMA((2, count, chunks)),
            pltpu.SemaphoreType.DMA((9 + more, count, chunks)),
            pltpu.SemaphoreType.DMA((9 + more, count, chunks)),
        ]

    def box(self, which, a, n):
        return self.boxes[a][which].at[0 if self.is_tall(a) else a, n]

    def is_tall(self, a):
        return a == len(self.wides)

    def own_share(self, a, n):
        return self.box(0, a, n)

    def sibling_share(self, a, n):
        ring = self.rings[1 if self.is_tall(a) else 0]
        return ring.at[n % 2] if self.is_tall(a) else ring.at[n % 2, a]

    def source(self, a, n, c, which):
        rows = pl.ds(pl.multiple_of(c * self.half, 16), self.half)
        return self.wides[a].at[which, rows, pl.ds(pl.multiple_of(n * WIDE, 128), WIDE)]

    def is_early(self, a, n):
        return isinstance(n, int) and (a, n) in self.early

    def axes(self, a, n):
        x, z = (self.x, self.over_x), (self.z, self.over_z)
        return (z, x) if self.is_early(a, n) else (x, z)

    def first_part(self, a, which):
        if self.is_tall(a):
            return pl.ds(pl.multiple_of(which * self.half, 16), self.half), slice(None)
        return slice(None), pl.ds(pl.multiple_of(which * 256, 128), 256)

    def second_part(self, which):
        return slice(None), pl.ds(pl.multiple_of(which * 128, 128), 128)

    def back_at(self, a, c, x=None, z=None):
        half = self.half
        if self.is_tall(a):
            if x is None:
                return pl.ds(pl.multiple_of(c * 2 * half, 16), 2 * half), slice(None)
            rows = pl.ds(pl.multiple_of(c * 2 * half + x * half, 16), half)
            return rows, slice(None) if z is None else pl.ds(pl.multiple_of(z * 128, 128), 128)
        rows = pl.ds(pl.multiple_of(c * half, 16), half)
        if x is None:
            return rows, slice(None)
        if z is None:
            return rows, pl.ds(pl.multiple_of(x * 256, 128), 256)
        return rows, pl.ds(pl.multiple_of(x * 256 + z * 128, 128), 128)

    def route(self, stage, a, n, src, dst, partner):
        return Route(src, dst, self.send_sem.at[stage, a, n], self.recv_sem.at[stage, a, n], partner)

    def copy(self, stage, a, n):
        loc, core_in, y_in, x_in, z_in, more_in, back = (self.box(i, a, n) for i in range(7))
        (first, over_first), (second, over_second) = self.axes(a, n)
        early = self.is_early(a, n)
        more = len(self.extra)
        if stage < 2:
            leaving = self.sibling_share(a, n).at[stage] if self.rings else self.source(a, n, 1 - self.core, stage)
            return self.route(stage, a, n, leaving, core_in.at[stage], self.sibling)
        if early and stage in (2, 8 + more):
            which = 0 if stage == 2 else 1
            return self.route(stage, a, n, loc.at[(which,) + self.first_part(a, 1 - first)],
                              y_in.at[:, pl.ds(which * 256, 256)], over_first)
        if early and stage == 3:
            return self.route(stage, a, n, loc.at[(1 - self.y,) + self.first_part(a, first)], x_in, self.over_y)
        if stage == 2:
            return self.route(stage, a, n, loc.at[1 - self.y], y_in, self.over_y)
        if stage == 3:
            return self.route(stage, a, n, y_in.at[self.first_part(a, 1 - first)], x_in, over_first)
        if stage == 4:
            return self.route(stage, a, n, x_in.at[self.second_part(1 - second)], z_in, over_second)
        if stage < 5 + more:
            so_far = z_in if stage == 5 else more_in.at[stage - 6]
            return self.route(stage, a, n, so_far, more_in.at[stage - 5], self.extra[stage - 5])
        at = [(self.core, first, second), (self.core, first), (self.core,)][stage - 5 - more]
        part = back.at[self.back_at(a, *at)]
        return self.route(stage, a, n, part, part, (over_second, over_first, self.sibling)[stage - 5 - more])

    def puts(self, a, n):
        box, out = self.box(6, a, n), self.outs[a]
        if self.is_tall(a):
            return [pltpu.make_async_copy(box, out.at[:, pl.ds(pl.multiple_of(n * 256, 128), 256)], self.put_sem.at[0, a, n])]
        if not self.rings:
            return [pltpu.make_async_copy(box, out.at[:, pl.ds(pl.multiple_of(n * WIDE, 128), WIDE)], self.put_sem.at[0, a, n])]
        return [
            pltpu.make_async_copy(
                box.at[:, pl.ds(i * 256, 256)],
                out.at[:, pl.ds(pl.multiple_of(i * (out.shape[1] // 2) + n * 256, 128), 256)],
                self.put_sem.at[i, a, n])
            for i in range(2)
        ]

    def start_core(self, a, n):
        for which in range(2):
            self.copy(which, a, n).start()

    def core_sent(self, a, n):
        for which in range(2):
            self.copy(which, a, n).sent()

    def start_y(self, a, n):
        loc, core_in = self.box(0, a, n), self.box(1, a, n)
        for which in range(2):
            self.copy(which, a, n).arrived()
            mine = loc.at[which] if self.rings else self.source(a, n, self.core, which)
            loc[which] = mine[...] + core_in[which]
        self.copy(2, a, n).start()
        if self.is_early(a, n):
            self.copy(8 + len(self.extra), a, n).start()

    def start_x(self, a, n):
        loc, y_in = self.box(0, a, n), self.box(2, a, n)
        self.copy(2, a, n).arrived()
        if self.is_early(a, n):
            self.copy(8 + len(self.extra), a, n).arrived()
            (first, _), _ = self.axes(a, n)
            for which in range(2):
                spot = (which,) + self.first_part(a, first)
                loc[spot] = loc[spot] + y_in[:, which * 256 : (which + 1) * 256]
        else:
            y_in[...] = y_in[...] + loc[self.y]
        self.copy(3, a, n).start()

    def start_z(self, a, n):
        loc, y_in, x_in = self.box(0, a, n), self.box(2, a, n), self.box(3, a, n)
        (first, _), _ = self.axes(a, n)
        self.copy(3, a, n).arrived()
        if self.is_early(a, n):
            x_in[...] = x_in[...] + loc[(self.y,) + self.first_part(a, first)]
        else:
            x_in[...] = x_in[...] + y_in[self.first_part(a, first)]
        self.copy(4, a, n).start()

    def more(self, step, a, n):
        x_in, z_in, more_in, back = (self.box(i, a, n) for i in range(3, 7))
        (first, _), (second, _) = self.axes(a, n)
        self.copy(4 + step, a, n).arrived()
        if step == 0:
            total = z_in
            value = z_in[...] + x_in[self.second_part(second)]
        else:
            total = more_in.at[step - 1]
            value = (z_in if step == 1 else more_in.at[step - 2])[...] + total[...]
        if step < len(self.extra):
            total[...] = value
        else:
            back[self.back_at(a, self.core, first, second)] = value
        self.copy(5 + step, a, n).start()

    def back_x(self, a, n):
        stage = 5 + len(self.extra)
        self.copy(stage, a, n).arrived()
        self.copy(stage + 1, a, n).start()

    def back_core(self, a, n):
        stage = 6 + len(self.extra)
        self.copy(stage, a, n).arrived()
        self.copy(stage + 1, a, n).start()

    def finish(self, a, n):
        self.copy(7 + len(self.extra), a, n).arrived()
        for put in self.puts(a, n):
            put.start()

    def drain(self, a, n):
        for stage in range(2, 8 + len(self.extra) + self.is_early(a, n)):
            self.copy(stage, a, n).sent()
        for put in self.puts(a, n):
            put.wait()


OWN_SIB, OWN_Y, OWN_NEXT, PASS_OWN, PREV_SIB, PREV_Y, PASS_PREV = range(7)
WEIGHT_CHUNKS = 5
FIRST_ROWS = (((0, 64), (64, 64)), ((128, 64), (192, 48)))


def forward_kernel(groups, low_ref, cosine, sine, x_ref, q_in, k_in, v_in, gains_in, wo_in, gate_in, up_in, down_in,
                   o_ref, lse_ref, q_ref, h_ref, scale_ref, gains, kv_out, qkv_out, wo_out, gate_out, up_out, down_out,
                   kv, kv_flip, w_qkv, wo, gate, up, down, top, acc, shrink, s_all, p_all,
                   kv_sem, load_sem, store_sem, send_sem, recv_sem, w_send, w_recv, wo_send, wo_recv, first_send, first_recv):
    dp, y = place()
    core, x, z = dp % 2, (dp // 2) % 2, (dp // 4) % 2
    k = dp // 2
    j = 2 * core + y
    j_y = 2 * core + 1 - y
    sibling, over_y, over_x, over_z = other(dp, y, 0), (dp, 1 - y), other(dp, y, 1), other(dp, y, 2)
    own = x_ref.shape[1]
    has_prev, has_next = k > 0, k < groups - 1
    first_core, last_core = core == 0, core == 1

    half, tall = gate_in.shape[0], down_in.shape[1]
    own_rows = pl.ds(pl.multiple_of(y * half, 16), half)
    own_cols = pl.ds(pl.multiple_of(y * tall, 128), tall)
    loads = [
        pltpu.make_async_copy(q_in, w_qkv.at[own_rows, pl.ds(2 * KV_HEADS * HEAD_DIM, D)], load_sem.at[0]),
        pltpu.make_async_copy(gains_in, gains.at[own_rows, :], load_sem.at[1]),
        pltpu.make_async_copy(gate_in, gate.at[own_rows, :], load_sem.at[2]),
        pltpu.make_async_copy(up_in, up.at[own_rows, :], load_sem.at[3]),
        pltpu.make_async_copy(down_in, down.at[:, own_cols], load_sem.at[4]),
        pltpu.make_async_copy(wo_in, wo.at[own_rows, :], load_sem.at[5]),
    ]
    flips = [pltpu.make_async_copy(w, kv_flip.at[i], load_sem.at[6 + i]) for i, w in enumerate((k_in, v_in))]
    for copy in flips + loads[:2]:
        copy.start()

    @pl.when(k == 0)
    def _():
        kv[:, : 4 * own, :] = jnp.zeros((KV_HEADS, 4 * own, 2 * HEAD_DIM), BF16)

    barrier = pltpu.get_barrier_semaphore()
    for partner in (sibling, over_y, over_x, over_z):
        pl.semaphore_signal(barrier, inc=1, device_id=partner, device_id_type=MESH)

    @pl.when(has_prev)
    def _():
        pl.semaphore_signal(barrier, inc=1, device_id=(dp - 2, y), device_id_type=MESH)

    @pl.when(has_next)
    def _():
        pl.semaphore_wait(barrier, 5)

    @pl.when(jnp.logical_not(has_next))
    def _():
        pl.semaphore_wait(barrier, 4)

    def slot(h, n):
        return kv.at[h, pl.ds(pl.multiple_of(n * own, own), own), :]

    def halo(route, h):
        after = jnp.minimum(dp + 2, 2 * groups - 1)
        sems = (send_sem.at[route, h], recv_sem.at[route, h])
        if route == OWN_SIB:
            return Route(slot(h, 4 + j), slot(h, 4 + j), *sems, sibling)
        if route == OWN_Y:
            return Route(slot(h, 4 + j), slot(h, 4 + j), *sems, over_y)
        if route == OWN_NEXT:
            return Route(slot(h, 4 + j), slot(h, j), *sems, (after, y))
        if route == PASS_OWN:
            return Route(slot(h, 4 + j_y), slot(h, 4 + j_y), *sems, sibling)
        if route == PREV_SIB:
            return Route(slot(h, j), slot(h, j), *sems, sibling)
        if route == PREV_Y:
            return Route(slot(h, j), slot(h, j), *sems, over_y)
        return Route(slot(h, j_y), slot(h, j_y), *sems, sibling)

    sent_if = {
        OWN_SIB: first_core, OWN_Y: j != 3, OWN_NEXT: has_next, PASS_OWN: first_core,
        PREV_SIB: jnp.logical_and(last_core, has_prev), PREV_Y: jnp.logical_and(j != 0, has_prev),
        PASS_PREV: jnp.logical_and(last_core, has_prev),
    }
    got_if = {
        OWN_SIB: last_core, OWN_Y: j != 2, OWN_NEXT: has_prev, PASS_OWN: last_core,
        PREV_SIB: jnp.logical_and(first_core, has_prev), PREV_Y: jnp.logical_and(j != 1, has_prev),
        PASS_PREV: jnp.logical_and(first_core, has_prev),
    }

    def start(route, h):
        pl.when(sent_if[route])(lambda: halo(route, h).start())

    def arrived(route, h):
        pl.when(got_if[route])(lambda: halo(route, h).arrived())

    def pass_one(h):
        arrived(OWN_Y, h)
        start(PASS_OWN, h)
        arrived(OWN_NEXT, h)
        start(PREV_SIB, h)
        start(PREV_Y, h)

    def pass_two(h):
        arrived(PREV_Y, h)
        start(PASS_PREV, h)

    part = half // 2

    def wide_at(which, n, width_from, width):
        rows = pl.ds(pl.multiple_of(which * half + core * part, 16), part)
        return rows, pl.ds(pl.multiple_of(n * WIDE + width_from, 128), width)

    def down_at(which, n, row_from, rows, col_from, cols):
        return (pl.ds(pl.multiple_of(row_from, 16), rows),
                pl.ds(pl.multiple_of(which * tall + n * 256 + col_from, 128), cols))

    def weights(stage, a, n):
        out = (gate, up, down)[a]
        which = y if stage == 0 else 1 - y
        rows = core * half
        if a < 2:
            size = [(z * 256 + x * 128, 128), (z * 256 + x * 128, 128), (z * 256, 256), (0, 512)][stage]
            region = out.at[wide_at(which, n, *size)]
        else:
            size = [(rows + z * part, part, x * 128, 128), (rows + z * part, part, x * 128, 128),
                    (rows + z * part, part, 0, 256), (rows, half, 0, 256)][stage]
            region = out.at[down_at(which, n, *size)]
        partner = (over_y, over_x, over_z, sibling)[stage]
        return Route(region, region, w_send.at[stage, a, n], w_recv.at[stage, a, n], partner)

    def hand_on(stage, a, n):
        weights(stage - 1, a, n).arrived()
        weights(stage, a, n).start()

    def store(a, n):
        if a < 2:
            cols = pl.ds(pl.multiple_of(n * WIDE, 128), WIDE)
            box, out = ((gate, gate_out), (up, up_out))[a]
            return [pltpu.make_async_copy(box.at[:, cols], out.at[:, cols], store_sem.at[a, n])]
        copies = []
        for which in range(2):
            some = pl.ds(pl.multiple_of(which * tall + n * 256, 128), 256)
            copies.append(pltpu.make_async_copy(down.at[:, some], down_out.at[:, some], store_sem.at[2 + which, n]))
        return copies

    def keep(a, n):
        weights(3, a, n).arrived()
        for copy in store(a, n):
            copy.start()

    def wo_part(which):
        return wo.at[pl.ds(pl.multiple_of(which * half + core * part, 16), part), :]

    wo_across = Route(wo_part(y), wo_part(y), wo_send.at[0], wo_recv.at[0], over_y)
    wo_within = Route(wo_part(1 - y), wo_part(1 - y), wo_send.at[1], wo_recv.at[1], sibling)
    wo_store = pltpu.make_async_copy(wo, wo_out, store_sem.at[0, WEIGHT_CHUNKS])

    def first(kind, i, which_x):
        row, count = FIRST_ROWS[which_x][i]
        at = (y if kind == 0 else 1 - y) * half + core * part + row
        region = w_qkv.at[pl.ds(pl.multiple_of(at, 16), count), :]
        return Route(region, region, first_send.at[kind, i], first_recv.at[kind, i], over_y if kind == 0 else over_x)

    def by_x(act, swap=False):
        for which_x in range(2):
            @pl.when(x == (1 - which_x if swap else which_x))
            def _(which_x=which_x):
                act(which_x)

    def first_part(which):
        return w_qkv.at[pl.ds(pl.multiple_of(which * half + core * part, 16), part), :]

    first_within = Route(first_part(1 - y), first_part(1 - y), first_send.at[2, 0], first_recv.at[2, 0], sibling)
    gains_across = Route(gains.at[own_rows, :], gains.at[own_rows, :], first_send.at[2, 1], first_recv.at[2, 1], over_y)
    first_store = pltpu.make_async_copy(w_qkv, qkv_out, store_sem.at[1, WEIGHT_CHUNKS])

    def across(n):
        for a in range(3):
            weights(0, a, n).start()

    def onward(stage, n):
        for a in range(3):
            hand_on(stage, a, n)

    for copy in flips:
        copy.wait()
    for i in range(2):
        w_qkv[own_rows, i * KV_HEADS * HEAD_DIM : (i + 1) * KV_HEADS * HEAD_DIM] = kv_flip[i].T
    loads[0].wait()
    loads[1].wait()
    gains_across.start()
    by_x(lambda which_x: [first(0, i, which_x).start() for i in range(2)])
    for copy in loads[2:]:
        copy.start()

    value = x_ref[...].astype(F32)
    scale = lax.rsqrt(jnp.mean(value * value, axis=0, keepdims=True) + EPSILON)
    scale_ref[...] = scale
    gains_across.arrived()
    h_ref[...] = (value * scale * gains[:, 0:1].astype(F32)).astype(BF16)
    for copy in loads[2:]:
        copy.wait()

    for i in range(2):
        def pass_first(which_x, i=i):
            first(0, i, which_x).arrived()
            first(1, i, which_x).start()

        by_x(pass_first)
        across(i)
    across(2)
    for i in range(2):
        by_x(lambda which_x, i=i: first(1, i, which_x).arrived(), swap=True)
    first_within.start()
    onward(1, 0)
    first_within.arrived()
    first_store.start()

    kv_width = KV_HEADS * HEAD_DIM
    turn = HEAD_DIM // 2

    def rotated(values):
        one, two = values[:turn], values[turn:]
        cos, sin = cosine[...], sine[...]
        return jnp.concatenate([one * cos - two * sin, two * cos + one * sin], axis=0)

    keys_values = over_first(w_qkv[:, : 2 * kv_width], h_ref[...])
    for h in range(KV_HEADS):
        at = h * HEAD_DIM
        both = jnp.concatenate(
            [rotated(keys_values[at : at + HEAD_DIM]), keys_values[kv_width + at : kv_width + at + HEAD_DIM]], axis=0
        ).astype(BF16)
        slot(h, 4 + j)[...] = both.T
        if h < 2:
            for route in (OWN_Y, OWN_NEXT, OWN_SIB):
                start(route, h)
    onward(2, 0)
    onward(1, 1)
    queries_all = over_first(w_qkv[:, 2 * kv_width :], h_ref[...])
    for h in range(HEADS):
        at = h * HEAD_DIM
        q_ref[at : at + HEAD_DIM, :] = rotated(queries_all[at : at + HEAD_DIM]).astype(BF16)
    pass_one(0)
    onward(2, 1)
    pass_two(0)

    def window(h):
        return pltpu.make_async_copy(
            kv.at[h, pl.ds(pl.multiple_of(j * own, own), 5 * own), :], kv_out.at[h], kv_sem.at[h])

    blocks = own // CHUNK
    third = GROUP * CHUNK

    def block(h, n, spans, diagonal):
        both = kv[h, pl.ds(pl.multiple_of(n * own, own), own), :]
        keys = both[:, :HEAD_DIM]
        values = jnp.concatenate([both[:, HEAD_DIM:].T, jnp.ones((16, own), BF16)], axis=0)
        begin_at = (n - 4 - j) * own
        for b in range(blocks):
            low_at, high_at = spans[b]
            low = low_ref[:, b * CHUNK : (b + 1) * CHUNK]
            for r in range(GROUP):
                cols = pl.ds(b * third + r * CHUNK, CHUNK)
                rows = pl.ds(pl.multiple_of(h * GROUP * HEAD_DIM + r * HEAD_DIM, HEAD_DIM), HEAD_DIM)
                queries = q_ref[rows, b * CHUNK : (b + 1) * CHUNK]
                old = top[:, cols]
                high = jnp.full((8, CHUNK), MASKED, F32)
                for at in range(low_at, high_at, STRIP):
                    rows = slice(at, at + STRIP)
                    s = masked(dot(keys[rows], queries), begin_at + at, low, b * CHUNK if diagonal else None)
                    s_all[rows, cols] = s
                    high = jnp.maximum(high, jnp.max(s.reshape(STRIP // 8, 8, CHUNK), axis=0))
                new = jnp.maximum(old, jnp.max(high, axis=0, keepdims=True))
                bound = new * SCALE2
                for at in range(low_at, high_at, STRIP):
                    rows = slice(at, at + STRIP)
                    p_all[rows, cols] = jnp.exp2(s_all[rows, cols] * SCALE2 - bound).astype(BF16)
                shrink[:, cols] = jnp.exp2(old * SCALE2 - bound)
                top[:, cols] = new
        for b in range(blocks):
            low_at, high_at = spans[b]
            cols = pl.ds(b * third, third)
            acc[:, cols] = acc[:, cols] * shrink[:, cols] + dot(values[:, low_at:high_at], p_all[low_at:high_at, cols])

    every = [(0, own)] * blocks
    plan = [(4 + j, [(0, (b + 1) * CHUNK) for b in range(blocks)], True),
            (j, [(b * CHUNK, own) for b in range(blocks)], False),
            (j + 2, every, False), (j + 1 + 2 * y, every, False), (j + 3 - 2 * y, every, False)]
    spots = len(plan)
    steps = [(functools.partial(hand_on, 1), 0, 2), (functools.partial(hand_on, 2), 3, 2),
             (functools.partial(hand_on, 3), 1, 1), (keep, 4, 1)]

    def head(h, carry):
        top[...] = jnp.full(top.shape, MASKED, F32)
        acc[...] = jnp.zeros(acc.shape, F32)

        for p in range(spots):
            if p == 0:
                @pl.when(h < KV_HEADS - 1)
                def _():
                    pass_one(h + 1)

                @pl.when(h < KV_HEADS - 2)
                def _():
                    for route in (OWN_Y, OWN_NEXT, OWN_SIB):
                        start(route, h + 2)

                pl.when(h == 0)(lambda: onward(3, 0))
            if p == 1:
                pl.when(h < KV_HEADS - 3)(lambda: across(h + 3))
                pl.when(h == 2)(lambda: wo_across.start())
            if p == 2:
                arrived(PREV_SIB, h)
                arrived(OWN_SIB, h)
            if p == 4:
                pl.when(h < KV_HEADS - 1)(lambda: pass_two(h + 1))
                arrived(PASS_PREV, h)
                arrived(PASS_OWN, h)

                @pl.when(h == KV_HEADS - 1)
                def _():
                    wo_across.arrived()
                    wo_within.start()
            if p == 1:
                pl.when(h == 0)(lambda: keep(0, 0))
            block(h, *plan[p])
            for step, spot, ahead in reversed(steps):
                for a in range(3):
                    if (p - a - spot) % spots == 0:
                        n = h + ahead + (p - a - spot) // spots
                        fits = jnp.logical_and(n >= (1 if ahead == 1 and step is not keep else 0), n < WEIGHT_CHUNKS)
                        fits = jnp.logical_and(fits, n >= 2) if ahead == 2 else fits
                        pl.when(fits)(lambda step=step, a=a, n=n: step(a, n))

        window(h).start()
        for r in range(GROUP):
            rows = pl.ds(pl.multiple_of(h * GROUP * HEAD_DIM + r * HEAD_DIM, HEAD_DIM), HEAD_DIM)
            for b in range(blocks):
                cols = pl.ds(b * third + r * CHUNK, CHUNK)
                total = acc[HEAD_DIM : HEAD_DIM + 1, cols]
                o_ref[rows, b * CHUNK : (b + 1) * CHUNK] = (acc[:HEAD_DIM, cols] / total).astype(BF16)
                lse_ref[h, r : r + 1, b * CHUNK : (b + 1) * CHUNK] = top[:, cols] * SCALE2 + jnp.log2(total)
        return carry

    lax.fori_loop(0, KV_HEADS, head, 0)
    wo_within.arrived()
    wo_store.start()

    def finish(h, carry):
        for a in range(3):
            for stage in range(4):
                weights(stage, a, h).sent()
            for copy in store(a, h):
                copy.wait()
        for route in range(7):
            pl.when(sent_if[route])(lambda route=route: halo(route, h).sent())
        window(h).wait()
        return carry

    lax.fori_loop(0, KV_HEADS, finish, 0)
    for route in (wo_across, wo_within, first_within, gains_across):
        route.sent()
    by_x(lambda which_x: [first(kind, i, which_x).sent() for kind in range(2) for i in range(2)])
    wo_store.wait()
    first_store.wait()


def attend(low, cosine, sine, x, w_query, w_key_t, w_value_t, gains, w_output, w_gate, w_up, w_down_t, dp_size):
    own = x.shape[1]
    width = GROUP * own
    any_spec = pl.BlockSpec(memory_space=pl.ANY)
    vmem = pl.BlockSpec(memory_space=pltpu.VMEM)
    later = [jax.ShapeDtypeStruct((2 * w.shape[0], w.shape[1]), BF16) for w in (w_output, w_gate, w_up)]
    later.insert(0, jax.ShapeDtypeStruct((D, D + 2 * w_key_t.shape[0]), BF16))
    later.append(jax.ShapeDtypeStruct((w_down_t.shape[0], 2 * w_down_t.shape[1]), BF16))
    return pl.pallas_call(
        functools.partial(forward_kernel, dp_size // 2),
        out_shape=[
            jax.ShapeDtypeStruct((D, own), BF16),
            jax.ShapeDtypeStruct((KV_HEADS, 8, own), F32),
            jax.ShapeDtypeStruct((D, own), BF16),
            jax.ShapeDtypeStruct((D, own), BF16),
            jax.ShapeDtypeStruct((1, own), F32),
            jax.ShapeDtypeStruct((2 * gains.shape[0], gains.shape[1]), BF16),
            jax.ShapeDtypeStruct((KV_HEADS, 5 * own, 2 * HEAD_DIM), BF16),
        ] + later,
        in_specs=[vmem] * 4 + [any_spec] * 8,
        out_specs=[vmem] * 6 + [any_spec] * 6,
        scratch_shapes=[pltpu.VMEM((KV_HEADS, 8 * own, 2 * HEAD_DIM), BF16), pltpu.VMEM((2,) + w_key_t.shape, BF16)]
        + [pltpu.VMEM(w.shape, BF16) for w in later]
        + [
            pltpu.VMEM((1, width), F32),
            pltpu.VMEM((HEAD_DIM + 16, width), F32),
            pltpu.VMEM((1, width), F32),
            pltpu.VMEM((own, width), F32),
            pltpu.VMEM((own, width), BF16),
            pltpu.SemaphoreType.DMA((KV_HEADS,)),
            pltpu.SemaphoreType.DMA((8,)),
            pltpu.SemaphoreType.DMA((4, WEIGHT_CHUNKS + 1)),
            pltpu.SemaphoreType.DMA((7, KV_HEADS)),
            pltpu.SemaphoreType.DMA((7, KV_HEADS)),
            pltpu.SemaphoreType.DMA((4, 3, WEIGHT_CHUNKS)),
            pltpu.SemaphoreType.DMA((4, 3, WEIGHT_CHUNKS)),
            pltpu.SemaphoreType.DMA((2,)),
            pltpu.SemaphoreType.DMA((2,)),
            pltpu.SemaphoreType.DMA((3, 2)),
            pltpu.SemaphoreType.DMA((3, 2)),
        ],
        compiler_params=pltpu.CompilerParams(
            collective_id=2, has_side_effects=True, vmem_limit_bytes=56 * 1024 * 1024),
        name="attend",
    )(low, cosine, sine, x, w_query, w_key_t, w_value_t, gains, w_output, w_gate, w_up, w_down_t)


FEED = 256


def middle_kernel(bits, groups, low_ref, cosine, sine, gains_ref, att_ref, lse_ref,
                  x_in, g_in, q_in, kv_in, wo_in, gate_in, up_in, down_in,
                  out_ref, dx_ref, branch_ref, row_ref, gate_out, up_out, down_out, dq_out, dkv_out,
                  ring, ring_down, far_in, sib_in, far_y, own_y, next_in, halo_send, halo_recv, feed_sem, load_sem, *scratch):
    own = x_in.shape[1]
    half_ff = gate_in.shape[1] // 2
    chunks = half_ff // FEED
    dp, y = place()
    core = dp % 2
    k = dp // 2
    j = 2 * core + y
    j_y = 2 * core + 1 - y
    has_prev, has_next = k > 0, k < groups - 1
    first_core, last_core = core == 0, core == 1
    half = D // 4
    sums = Sums(bits, [None, None], down_in, [gate_out, up_out, down_out], scratch, (ring, ring_down))

    barrier = pltpu.get_barrier_semaphore()
    for partner in sums.partners:
        pl.semaphore_signal(barrier, inc=1, device_id=partner, device_id_type=MESH)

    @pl.when(has_next)
    def _():
        pl.semaphore_signal(barrier, inc=1, device_id=(dp + 2, y), device_id_type=MESH)

    spots = 5
    begins = {0: (-2, 1, 2), 1: (0, 0, 2), 2: (1, 0, 2), 3: (2, 1, 2), 4: (3, 3, 1)}
    events = {(0, 0): [(sums.start_y, a, chunks - 2) for a in range(3)], (0, 2): [(sums.start_y, a, chunks - 1) for a in range(3)]}
    for n in range(chunks):
        turn, spot, lag = begins[n]
        for s in range(len(sums.stages)):
            for a in range(3):
                at = turn * spots + spot + a + lag * s
                events.setdefault((at // spots, at % spots), []).insert(0, (sums.stages[s], a, n))
    last_round = max(turn for turn, spot in events)

    def advance(p, h):
        if isinstance(h, int):
            for step, a, n in events.get((h, p), ()):
                step(a, n)
            return
        for turn in range(KV_HEADS):
            if (turn, p) in events:
                pl.when(h == turn)(lambda turn=turn: advance(p, turn))

    def feed_phase(weights, wo, h_t, g_t, x, h, g, acc):
        def load(n, s):
            cols = pl.ds(pl.multiple_of(s * half_ff + n * FEED, 128), FEED)
            return [pltpu.make_async_copy(w.at[:, cols], weights.at[s, i], feed_sem.at[s, i])
                    for i, w in enumerate((gate_in, up_in, down_in))]

        first = [pltpu.make_async_copy(a, b, load_sem.at[i]) for i, (a, b) in enumerate(((x_in, h_t), (g_in, g_t), (wo_in, wo)))]
        for copy in first + load(0, 0):
            copy.start()
        for copy in first:
            copy.wait()
        gain = gains_ref[:, 1:2].astype(F32)
        x[...] = h_t[...].astype(F32) + over_first(wo[...], att_ref[...])
        scale = lax.rsqrt(jnp.mean(x[...] * x[...], axis=0, keepdims=True) + EPSILON)
        h_t[...] = (x[...] * scale * gain).astype(BF16)
        h[...] = h_t[...].T
        g[...] = g_t[...].T
        acc[...] = x[...]
        dx_ref[...] = jnp.zeros(dx_ref.shape, F32)

        @pl.when(has_prev)
        def _():
            pl.semaphore_wait(barrier, len(sums.partners) + 1)

        @pl.when(jnp.logical_not(has_prev))
        def _():
            pl.semaphore_wait(barrier, len(sums.partners))

        def step(n, s):
            for copy in load(n, s):
                copy.wait()
            if s == 0:
                for copy in load(n, 1):
                    copy.start()
            else:
                @pl.when(n < chunks - 1)
                def _():
                    for copy in load(n + 1, 0):
                        copy.start()

            w_gate, w_up, w_down = weights[s, 0], weights[s, 1], weights[s, 2]
            gate = dot(h[...], w_gate)
            upper = dot(h[...], w_up)
            dm = dot(g[...], w_down)
            sigmoid = 1.0 / (1.0 + jnp.exp(-gate))
            active = gate * sigmoid
            inner = (active * upper).astype(BF16)
            dgate = (dm * upper * sigmoid * (1.0 + gate * (1.0 - sigmoid))).astype(BF16)
            dup = (dm * active).astype(BF16)
            acc[...] += against_rows(w_down, inner)
            dx_ref[...] += against_rows(w_gate, dgate) + against_rows(w_up, dup)
            cols = slice(s * FEED, (s + 1) * FEED)
            for c, shares in ((core, sums.own_share), (1 - core, sums.sibling_share)):
                for which in range(2):
                    rows = pl.ds(pl.multiple_of(which * 2 * half + c * half, 16), half)
                    left = h_t[rows, :]
                    for a, right in enumerate((dgate, dup)):
                        shares(a, n)[which, :, cols] = dot(left, right).astype(BF16)
                rows = pl.ds(pl.multiple_of(c * 2 * half, 16), 2 * half)
                shares(2, n)[s] = dot(g_t[rows, :], inner).astype(BF16)

        def round_of(n, carry):
            @pl.when(n > 1)
            def _():
                for a in range(3):
                    sums.core_sent(a, n - 2)

            step(n, 0)

            @pl.when(jnp.logical_and(n > 0, n < chunks - 1))
            def _():
                for a in range(3):
                    sums.start_y(a, n - 1)

            for turn in (-2, -1):
                @pl.when(n == chunks + turn)
                def _(turn=turn):
                    for p in range(3):
                        advance(p, turn)

            step(n, 1)
            for a in range(3):
                sums.start_core(a, n)
            for turn in (-2, -1):
                @pl.when(n == chunks + turn)
                def _(turn=turn):
                    for p in range(3, spots):
                        advance(p, turn)

            return carry

        lax.fori_loop(0, chunks, round_of, 0)
        out_ref[...] = acc[...].astype(BF16)
        dh = dx_ref[...]
        acc[...] = dh * (x[...] * scale)
        ones = jnp.ones((8, own), F32)
        row_ref[...] = lax.dot_general(ones, acc[...], (((1,), (1,)), ((), ())), precision=lax.Precision.HIGHEST,
                                       preferred_element_type=F32)
        mean = jnp.sum(acc[...] * gain, axis=0, keepdims=True) * (1.0 / D)
        dx = g_t[...].astype(F32) + scale * (dx_ref[...] * gain - x[...] * scale * mean)
        dx_ref[...] = dx
        branch_ref[...] = dx.astype(BF16)

    pl.run_scoped(
        feed_phase,
        pltpu.VMEM((2, 3, D, FEED), BF16),
        pltpu.VMEM((D, D), BF16),
        pltpu.VMEM((D, own), BF16),
        pltpu.VMEM((D, own), BF16),
        pltpu.VMEM((D, own), F32),
        pltpu.VMEM((own, D), BF16),
        pltpu.VMEM((own, D), BF16),
        pltpu.VMEM((D, own), F32),
    )
    for n in (chunks - 2, chunks - 1):
        for a in range(3):
            sums.core_sent(a, n)

    blocks = own // CHUNK
    third = GROUP * CHUNK

    def attention_phase(wo, q, do, kv, q_all, do_all, q_rows, do_rows, delta, dq_acc, p_all, ds_all, part, dq, dkv):
        first = [pltpu.make_async_copy(a, b, load_sem.at[i]) for i, (a, b) in enumerate(((wo_in, wo), (q_in, q)))]

        def window(h, at):
            return pltpu.make_async_copy(kv_in.at[h], kv.at[at], feed_sem.at[at, 0])

        for copy in first + [window(0, 0)]:
            copy.start()
        part[...] = jnp.zeros(part.shape, BF16)
        for copy in first:
            copy.wait()
        do[...] = dot(wo[...], branch_ref[...]).astype(BF16)

        def slot(h, n):
            return part.at[h, pl.ds(pl.multiple_of(n * own, own), own), :]

        def halo(route, h):
            before = jnp.maximum(dp - 2, 0)
            sems = (halo_send.at[route, h], halo_recv.at[route, h])
            if route == PASS_PREV:
                return Route(slot(h, j_y + 2 - 4 * core), far_in.at[h], *sems, sums.sibling)
            if route == PASS_OWN:
                return Route(slot(h, 2 + j_y), far_in.at[h], *sems, sums.sibling)
            if route == PREV_SIB:
                return Route(slot(h, j + 2 - 4 * core), sib_in.at[h], *sems, sums.sibling)
            if route == OWN_SIB:
                return Route(slot(h, 2 + j), sib_in.at[h], *sems, sums.sibling)
            if route == PREV_Y:
                return Route(slot(h, j_y), far_y.at[h], *sems, sums.over_y)
            if route == OWN_Y:
                return Route(slot(h, 4 + j_y), own_y.at[h], *sems, sums.over_y)
            return Route(slot(h, j), next_in.at[h], *sems, (before, y))

        got_if = {
            OWN_SIB: first_core, OWN_Y: j != 3, OWN_NEXT: has_next, PASS_OWN: first_core,
            PREV_SIB: jnp.logical_and(last_core, has_prev), PREV_Y: jnp.logical_and(j != 0, has_prev),
            PASS_PREV: jnp.logical_and(last_core, has_prev),
        }
        sent_if = {
            OWN_SIB: last_core, OWN_Y: j != 2, OWN_NEXT: has_prev, PASS_OWN: last_core,
            PREV_SIB: jnp.logical_and(first_core, has_prev), PREV_Y: jnp.logical_and(j != 1, has_prev),
            PASS_PREV: jnp.logical_and(first_core, has_prev),
        }

        def start(route, h):
            pl.when(sent_if[route])(lambda: halo(route, h).start())

        def take(route, h, n, box):
            @pl.when(got_if[route])
            def _():
                halo(route, h).arrived()
                spot = slot(h, n)
                spot[...] = spot[...] + box[h]

        def return_one(h):
            for route in (PASS_PREV, PASS_OWN, PREV_SIB, OWN_SIB):
                start(route, h)

        def return_two(h):
            take(PASS_PREV, h, j_y, far_in)
            take(PASS_OWN, h, 4 + j_y, far_in)
            start(PREV_Y, h)
            start(OWN_Y, h)

        def return_three(h):
            for route, n, box in ((PREV_SIB, j, sib_in), (OWN_SIB, 4 + j, sib_in), (PREV_Y, j, far_y), (OWN_Y, 4 + j, own_y)):
                take(route, h, n, box)
            start(OWN_NEXT, h)

        def return_four(h):
            dkv[h] = slot(h, 4 + j)[...].astype(F32)

            @pl.when(has_next)
            def _():
                halo(OWN_NEXT, h).arrived()
                dkv[h] = dkv[h] + next_in[h].astype(F32)

        def head_rows(h, r):
            return pl.ds(pl.multiple_of(h * GROUP * HEAD_DIM + r * HEAD_DIM, HEAD_DIM), HEAD_DIM)

        def prepare(h):
            for r in range(GROUP):
                rows = head_rows(h, r)
                for b in range(blocks):
                    cols = pl.ds(b * third + r * CHUNK, CHUNK)
                    from_cols = slice(b * CHUNK, (b + 1) * CHUNK)
                    grad, queries = do[rows, from_cols], q[rows, from_cols]
                    q_all[:, cols] = queries
                    do_all[:, cols] = grad
                    q_rows[cols, :] = queries.T
                    do_rows[cols, :] = grad.T
                    delta[:, cols] = jnp.sum(grad.astype(F32) * att_ref[rows, from_cols].astype(F32), axis=0, keepdims=True)
            dq_acc[...] = jnp.zeros(dq_acc.shape, F32)

        def block(h, at, n, spans, diagonal):
            both = kv[at, n * own : (n + 1) * own, :]
            keys, values = both[:, :HEAD_DIM], both[:, HEAD_DIM:]
            begin_at = (n - 4) * own
            for i in range(own // CHUNK):
                row = i * CHUNK
                some_keys, some_values = keys[row : row + CHUNK], values[row : row + CHUNK]
                using = [b for b in range(blocks) if spans[b][0] <= row < spans[b][1]]
                for b in using:
                    low = low_ref[:, b * CHUNK : (b + 1) * CHUNK]
                    for r in range(GROUP):
                        cols = pl.ds(b * third + r * CHUNK, CHUNK)
                        lse = lse_ref[h, r : r + 1, b * CHUNK : (b + 1) * CHUNK]
                        s = masked(dot(some_keys, q_all[:, cols]), begin_at + row, low, b * CHUNK if diagonal and b == i else None)
                        p = jnp.exp2(s * SCALE2 - lse)
                        p_all[:, cols] = p.astype(BF16)
                        ds_all[:, cols] = (p * (dot(some_values, do_all[:, cols]) - delta[:, cols])).astype(BF16)
                cols = pl.ds(using[0] * third, len(using) * third)
                dq_acc[:, cols] += dot(some_keys.T, ds_all[:, cols])
                dk = dot(ds_all[:, cols], q_rows[cols, :]) * 0.125
                dv = dot(p_all[:, cols], do_rows[cols, :])
                spot = pl.ds(pl.multiple_of((n + j) * own + row, CHUNK), CHUNK)
                part[h, spot, :] = jnp.concatenate([dk, dv], axis=1).astype(BF16)

        every = [(0, own)] * blocks
        plan = [(0, [(b * CHUNK, own) for b in range(blocks)], False), (1, every, False), (2, every, False),
                (3, every, False), (4, [(0, (b + 1) * CHUNK) for b in range(blocks)], True)]
        def guarded(fn, h):
            pl.when(jnp.logical_and(h >= 0, h < KV_HEADS))(lambda: fn(h))

        def head(h, carry):
            at = h % 2
            window(h, at).wait()

            @pl.when(h < KV_HEADS - 1)
            def _():
                window(h + 1, 1 - at).start()

            prepare(h)
            for p in range(spots):
                block(h, at, *plan[p])
                advance(p, h)
                if p == 1:
                    guarded(return_two, h - 1)
                if p == 4:
                    guarded(return_three, h - 3)
            return_one(h)
            for r in range(GROUP):
                rows = head_rows(h, r)
                for b in range(blocks):
                    value = dq_acc[:, pl.ds(b * third + r * CHUNK, CHUNK)] * 0.125
                    spot = slice(b * CHUNK, (b + 1) * CHUNK)
                    cos, sin = cosine[:, spot], sine[:, spot]
                    one, two = value[: HEAD_DIM // 2], value[HEAD_DIM // 2 :]
                    back = jnp.concatenate([one * cos + two * sin, two * cos - one * sin], axis=0)
                    dq[rows, spot] = back.astype(BF16)
            return carry

        lax.fori_loop(0, KV_HEADS, head, 0)
        last = KV_HEADS - 1
        after = [(return_two, last), (return_three, 2), (return_three, 3), (return_four, 0), (return_four, 1),
                 (return_three, last), (return_four, 2), (return_four, 3)]
        for i in range((last_round - KV_HEADS + 1) * spots):
            if i < len(after):
                fn, h = after[i]
                fn(h)
            advance(i % spots, KV_HEADS + i // spots)
        for fn, h in after[(last_round - KV_HEADS + 1) * spots :]:
            fn(h)
        return_four(last)
        stores = [pltpu.make_async_copy(dq, dq_out, load_sem.at[0]), pltpu.make_async_copy(dkv, dkv_out, load_sem.at[1])]
        for store in stores:
            store.start()

        def finish(h, carry):
            for route in range(7):
                pl.when(sent_if[route])(lambda route=route: halo(route, h).sent())
            return carry

        lax.fori_loop(0, KV_HEADS, finish, 0)
        for store in stores:
            store.wait()

    width = GROUP * own
    pl.run_scoped(
        attention_phase,
        pltpu.VMEM((D, D), BF16),
        pltpu.VMEM((D, own), BF16),
        pltpu.VMEM((D, own), BF16),
        pltpu.VMEM((2, 5 * own, 2 * HEAD_DIM), BF16),
        pltpu.VMEM((HEAD_DIM, width), BF16),
        pltpu.VMEM((HEAD_DIM, width), BF16),
        pltpu.VMEM((width, HEAD_DIM), BF16),
        pltpu.VMEM((width, HEAD_DIM), BF16),
        pltpu.VMEM((1, width), F32),
        pltpu.VMEM((HEAD_DIM, width), F32),
        pltpu.VMEM((CHUNK, width), BF16),
        pltpu.VMEM((CHUNK, width), BF16),
        pltpu.VMEM((KV_HEADS, 8 * own, 2 * HEAD_DIM), BF16),
        pltpu.VMEM((D, own), BF16),
        pltpu.VMEM((KV_HEADS, own, 2 * HEAD_DIM), F32),
    )

    for n in range(chunks):
        for a in range(3):
            sums.drain(a, n)


def middle_and_back(low, cosine, sine, gains, attended, lse, x, cotangent, queries, both, w_output, w_gate, w_up, w_down_t,
           dp_size):
    own = x.shape[1]
    ff = w_gate.shape[1]
    bits = dp_size.bit_length() - 1
    half = D // 4
    chunks = ff // WIDE
    any_spec = pl.BlockSpec(memory_space=pl.ANY)
    vmem = pl.BlockSpec(memory_space=pltpu.VMEM)
    box = pltpu.VMEM((KV_HEADS, own, 2 * HEAD_DIM), BF16)
    return pl.pallas_call(
        functools.partial(middle_kernel, bits, dp_size // 2),
        out_shape=[
            jax.ShapeDtypeStruct((D, own), BF16),
            jax.ShapeDtypeStruct((D, own), F32),
            jax.ShapeDtypeStruct((D, own), BF16),
            jax.ShapeDtypeStruct((8, D), F32),
            jax.ShapeDtypeStruct((D // 2, ff), BF16),
            jax.ShapeDtypeStruct((D // 2, ff), BF16),
            jax.ShapeDtypeStruct((D, ff // 2), BF16),
            jax.ShapeDtypeStruct((D, own), BF16),
            jax.ShapeDtypeStruct((KV_HEADS, own, 2 * HEAD_DIM), F32),
        ],
        in_specs=[vmem] * 6 + [any_spec] * 8,
        out_specs=[vmem] * 4 + [any_spec] * 5,
        scratch_shapes=[
            pltpu.VMEM((2, 2, 2, half, WIDE), BF16),
            pltpu.VMEM((2, 2, 2 * half, FEED), BF16),
            box, box, box, box, box,
            pltpu.SemaphoreType.DMA((7, KV_HEADS)),
            pltpu.SemaphoreType.DMA((7, KV_HEADS)),
            pltpu.SemaphoreType.DMA((2, 3)),
            pltpu.SemaphoreType.DMA((3,)),
        ] + Sums.scratch(bits, 2, 1, chunks, half),
        compiler_params=pltpu.CompilerParams(
            collective_id=3, has_side_effects=True, vmem_limit_bytes=60 * 1024 * 1024),
        name="middle",
    )(low, cosine, sine, gains, attended, lse, x, cotangent, queries, both, w_output, w_gate, w_up, w_down_t)


def finish_kernel(bits, chunks, dq, dkv, cosine, sine, hidden, x, scale, gains, w_qkv, attended, branch, middle, feed_row,
                  out, gains_out, tokens_out, pack, grads, prod, *rest):
    sums = Sums(bits, [pack], None, [out], rest[:-5])
    g_loc, g_in, g_sem, g_send, g_recv = rest[-5:]
    half = HEAD_DIM // 2
    rows = pack.shape[1]
    greet(sums.partners)

    def gain_route(n):
        return Route(g_loc.at[n], g_in.at[n], g_send.at[n], g_recv.at[n], sums.partners[n])

    def unrotate(values, at):
        one, two = values[:half], values[half:]
        cos, sin = cosine[...], sine[...]
        grads[at : at + half, :] = (one * cos + two * sin).astype(BF16)
        grads[at + half : at + HEAD_DIM, :] = (two * cos - one * sin).astype(BF16)

    def columns(low, high):
        parts = []
        if low < D:
            parts.append((attended, branch, low, min(high, D)))
        if high > D:
            parts.append((hidden, grads, max(low, D) - D, high - D))
        return [against_rows(left[...], right[a:b, :]) for left, right, a, b in parts]

    def fill(n):
        parts = columns(n * WIDE, (n + 1) * WIDE)
        value = parts[0] if len(parts) == 1 else jnp.concatenate(parts, axis=1)
        value = value.astype(BF16)
        for which in range(2):
            pack[which, :, n * WIDE : (n + 1) * WIDE] = value[which * rows : (which + 1) * rows]
        sums.start_core(0, n)

    def heads():
        grads[:D, :] = dq[...]
        for h in range(KV_HEADS):
            both = dkv[h].T
            unrotate(both[:HEAD_DIM], D + h * HEAD_DIM)
            at = D + (KV_HEADS + h) * HEAD_DIM
            grads[at : at + HEAD_DIM, :] = both[HEAD_DIM:].astype(BF16)

    def hidden_grad():
        keys_values = 2 * KV_HEADS * HEAD_DIM
        dh = dot(w_qkv[:, keys_values:], grads[:D, :]) + dot(w_qkv[:, :keys_values], grads[D:, :])
        tokens_out[...] = dh
        prod[...] = dh * (x[...].astype(F32) * scale[...])
        g_loc[0] = jnp.zeros(g_loc.shape[1:], F32)
        ones = jnp.ones((8, dh.shape[1]), F32)
        total = lax.dot_general(ones, prod[...], (((1,), (1,)), ((), ())), precision=lax.Precision.HIGHEST,
                                preferred_element_type=F32)
        g_loc[0, 0:1, :] = total[0:1]
        g_loc[0, 1:2, :] = feed_row[0:1, :]
        gain_route(0).start()

    def tokens_grad():
        normed = x[...].astype(F32) * scale[...]
        gain = gains[:, 0:1].astype(F32)
        e = tokens_out[...] * gain
        mean = jnp.sum(prod[...] * gain, axis=0, keepdims=True) * (1.0 / D)
        tokens_out[...] = middle[...] + scale[...] * (e - normed * mean)

    def gain_step(n):
        gain_route(n - 1).arrived()
        g_loc[n] = g_loc[n - 1] + g_in[n - 1]
        if n < len(sums.partners):
            gain_route(n).start()

    work = [lambda: fill(0), lambda: (heads(), fill(1))] + [functools.partial(fill, n) for n in range(2, chunks)]
    work += [hidden_grad, tokens_grad] + [functools.partial(gain_step, n + 1) for n in range(len(sums.partners))]
    steps = [sums.start_y] + sums.stages
    delay = [1, 3]
    while len(delay) < len(steps):
        delay.append(delay[-1] + 1)
    for tick in range(max(chunks + delay[-1], len(work))):
        if tick < len(work):
            work[tick]()
        for s in [0] + list(range(len(steps) - 1, 0, -1)):
            if 0 <= tick - delay[s] < chunks:
                steps[s](0, tick - delay[s])
    store = pltpu.make_async_copy(g_loc.at[len(sums.partners)], gains_out, g_sem.at[0])
    store.start()
    for n in range(chunks):
        sums.core_sent(0, n)
        sums.drain(0, n)
    for n in range(len(sums.partners)):
        gain_route(n).sent()
    store.wait()


def finish(dq, dkv, cosine, sine, hidden, x, scale, gains, w_qkv, attended, branch, middle, feed_row, dp_size):
    bits = dp_size.bit_length() - 1
    own = x.shape[1]
    total = 2 * D + 2 * KV_HEADS * HEAD_DIM
    chunks = total // WIDE
    any_spec = pl.BlockSpec(memory_space=pl.ANY)
    vmem = pl.BlockSpec(memory_space=pltpu.VMEM)
    row = (8, D)
    return pl.pallas_call(
        functools.partial(finish_kernel, bits, chunks),
        out_shape=[
            jax.ShapeDtypeStruct((D // 2, total), BF16),
            jax.ShapeDtypeStruct(row, F32),
            jax.ShapeDtypeStruct((D, own), F32),
        ],
        in_specs=[vmem] * 13,
        out_specs=[any_spec, any_spec, vmem],
        scratch_shapes=[
            pltpu.VMEM((2, D // 2, total), BF16),
            pltpu.VMEM((total - D, own), BF16),
            pltpu.VMEM((D, own), F32),
        ] + Sums.scratch(bits, 1, 0, chunks, D // 4) + [
            pltpu.VMEM((bits + 2,) + row, F32),
            pltpu.VMEM((bits + 1,) + row, F32),
            pltpu.SemaphoreType.DMA((1,)),
            pltpu.SemaphoreType.DMA((bits + 1,)),
            pltpu.SemaphoreType.DMA((bits + 1,)),
        ],
        compiler_params=pltpu.CompilerParams(
            collective_id=0, has_side_effects=True, vmem_limit_bytes=56 * 1024 * 1024),
        name="finish",
    )(dq, dkv, cosine, sine, hidden, x, scale, gains, w_qkv, attended, branch, middle, feed_row)


def positions(seq_lengths, first, count):
    ends = jnp.cumsum(seq_lengths)
    index = first + jnp.arange(count, dtype=jnp.int32)
    passed = index[:, None] >= ends[None, :]
    begin = jnp.max(jnp.where(passed, ends[None, :], 0), axis=1)
    return index - begin


def rotary_tables(position):
    half = HEAD_DIM // 2
    inverse = jnp.exp(-jnp.arange(half, dtype=F32) * (2.0 / HEAD_DIM) * jnp.log(THETA))
    angle = inverse[:, None] * position.astype(F32)[None, :]
    return jnp.cos(angle), jnp.sin(angle)


def shards(tokens, cotangent, w_query, w_key, w_value, w_output, w_gate, w_up, w_down, attention_gain, feed_gain, seq_lengths):
    own = tokens.shape[0]
    kv = KV_HEADS * HEAD_DIM
    first = lax.axis_index(("dp", "shard")) * own
    position = positions(seq_lengths, first, own)
    low = jnp.arange(own, dtype=jnp.int32) - position
    cosine, sine = rotary_tables(position)
    gains = jnp.where(jnp.arange(128)[None, :] == 0, attention_gain[:, None], feed_gain[:, None])
    dp_size = lax.axis_size("dp")
    (attended, log_total, queries, hidden_one, scale_one, gains, both_all,
     qkv_full, output_full, gate_full, up_full, down_full) = attend(
        low[None, :], cosine, sine, tokens.T, w_query, w_key.T, w_value.T, gains,
        w_output, w_gate, w_up, w_down.T, dp_size
    )
    output, grad_middle, grad_branch, feed_rows, sum_gate, sum_up, sum_down, grad_queries, grad_own = middle_and_back(
        low[None, :], cosine, sine, gains, attended, log_total, tokens.T, cotangent.T, queries,
        both_all, output_full, gate_full, up_full, down_full, dp_size
    )
    sum_pack, sum_gains, grad_tokens = finish(
        grad_queries, grad_own, cosine, sine, hidden_one, tokens.T, scale_one, gains, qkv_full,
        attended, grad_branch, grad_middle, feed_rows, dp_size
    )
    sum_pack = sum_pack.astype(F32)
    half = D // 2
    begin = lax.axis_index("shard") * half
    return (
        output.T,
        grad_tokens.T,
        sum_pack[:, D : 2 * D],
        sum_pack[:, 2 * D : 2 * D + kv],
        sum_pack[:, 2 * D + kv :],
        sum_pack[:, :D],
        sum_gate.astype(F32),
        sum_up.astype(F32),
        sum_down.astype(F32).T,
        lax.dynamic_slice_in_dim(sum_gains[0], begin, half),
        lax.dynamic_slice_in_dim(sum_gains[1], begin, half),
    )


def solution(mesh):
    return jax.shard_map(
        shards,
        mesh=mesh,
        in_specs=(
            P(("dp", "shard"), None),
            P(("dp", "shard"), None),
            P("shard", None),
            P("shard", None),
            P("shard", None),
            P("shard", None),
            P("shard", None),
            P("shard", None),
            P("shard", None),
            P("shard"),
            P("shard"),
            P(),
        ),
        out_specs=(
            P(("dp", "shard"), None),
            P(("dp", "shard"), None),
            P("shard", None),
            P("shard", None),
            P("shard", None),
            P("shard", None),
            P("shard", None),
            P("shard", None),
            P("shard", None),
            P("shard"),
            P("shard"),
        ),
        check_vma=False,
    )
```

```python
import functools

import jax
import jax.numpy as jnp
from jax import lax
from jax.experimental import pallas as pl
from jax.experimental.pallas import tpu as pltpu
from jax.sharding import PartitionSpec as P

D = 960
HEADS = 15
KV_HEADS = 5
GROUP = 3
HEAD_DIM = 64

EPSILON = 1e-05
THETA = 100000.0
MASKED = -1e30
LOG2E = 1.4426950408889634
SCALE2 = 0.125 * LOG2E

MESH = pl.DeviceIdType.MESH
WIDE = 512
CHUNK = 256
STRIP = 256
BF16 = jnp.bfloat16
F32 = jnp.float32


def dot(left, right):
    return lax.dot_general(left, right, (((1,), (0,)), ((), ())), preferred_element_type=F32)


def against_rows(left, right):
    return lax.dot_general(left, right, (((1,), (1,)), ((), ())), preferred_element_type=F32)


def over_first(left, right):
    return lax.dot_general(left, right, (((0,), (0,)), ((), ())), preferred_element_type=F32)


def masked(scores, start, low, diagonal):
    rows = start + lax.broadcasted_iota(jnp.int32, scores.shape, 0)
    valid = rows >= low
    if diagonal is not None:
        cols = diagonal + lax.broadcasted_iota(jnp.int32, scores.shape, 1)
        valid = jnp.logical_and(valid, rows <= cols)
    return jnp.where(valid, scores, MASKED)


def place():
    return lax.axis_index("dp"), lax.axis_index("shard")


def other(dp, y, bit):
    step = 1 << bit
    mine = (dp // step) % 2
    return (dp + step - 2 * step * mine, y)


def greet(partners):
    barrier = pltpu.get_barrier_semaphore()
    for partner in partners:
        pl.semaphore_signal(barrier, inc=1, device_id=partner, device_id_type=MESH)
    pl.semaphore_wait(barrier, len(partners))


class Route:
    def __init__(self, src, dst, send, recv, partner):
        self.make = lambda: pltpu.make_async_remote_copy(
            src_ref=src, dst_ref=dst, send_sem=send, recv_sem=recv, device_id=partner, device_id_type=MESH)

    def start(self):
        self.make().start()

    def arrived(self):
        self.make().wait_recv()

    def sent(self):
        self.make().wait_send()


class Sums:
    def __init__(self, bits, wides, tall, outs, scratch, rings=None, early=()):
        self.wides, self.tall, self.outs, self.rings, self.early = wides, tall, outs, rings, early
        self.boxes = [scratch[:7]] * len(wides) + [scratch[7:14]] * (tall is not None)
        self.put_sem, self.send_sem, self.recv_sem = scratch[-3:]
        self.arrays = len(self.boxes)
        self.half = D // 4
        dp, y = place()
        self.core, self.x, self.z, self.y = dp % 2, (dp // 2) % 2, (dp // 4) % 2, y
        self.sibling, self.over_y = other(dp, y, 0), (dp, 1 - y)
        self.over_x, self.over_z = other(dp, y, 1), other(dp, y, 2)
        self.extra = [other(dp, y, bit) for bit in range(3, bits)]
        self.partners = [self.sibling, self.over_y, self.over_x, self.over_z] + self.extra
        more = len(self.extra)
        self.stages = [self.start_x, self.start_z]
        self.stages += [functools.partial(self.more, step) for step in range(more + 1)]
        self.stages += [self.back_x, self.back_core, self.finish]

    @staticmethod
    def scratch(bits, wide_arrays, tall, chunks, half):
        more = bits - 3
        count = wide_arrays + tall

        def boxes(n, shapes):
            return [pltpu.VMEM((n, chunks) + shape, BF16) for shape in shapes]

        shared = [(half, 128), (max(more, 1), half, 128)]
        out = []
        if wide_arrays:
            out += boxes(wide_arrays, [(2, half, WIDE)] * 2 + [(half, WIDE), (half, 256)] + shared + [(2 * half, WIDE)])
        else:
            out += [None] * 7
        if tall:
            out += boxes(1, [(2, 2 * half, 256)] * 2 + [(2 * half, 256), (half, 256)] + shared + [(4 * half, 256)])
        return out + [
            pltpu.SemaphoreType.DMA((2, count, chunks)),
            pltpu.SemaphoreType.DMA((9 + more, count, chunks)),
            pltpu.SemaphoreType.DMA((9 + more, count, chunks)),
        ]

    def box(self, which, a, n):
        return self.boxes[a][which].at[0 if self.is_tall(a) else a, n]

    def is_tall(self, a):
        return a == len(self.wides)

    def own_share(self, a, n):
        return self.box(0, a, n)

    def sibling_share(self, a, n):
        ring = self.rings[1 if self.is_tall(a) else 0]
        return ring.at[n % 2] if self.is_tall(a) else ring.at[n % 2, a]

    def source(self, a, n, c, which):
        rows = pl.ds(pl.multiple_of(c * self.half, 16), self.half)
        return self.wides[a].at[which, rows, pl.ds(pl.multiple_of(n * WIDE, 128), WIDE)]

    def is_early(self, a, n):
        return isinstance(n, int) and (a, n) in self.early

    def axes(self, a, n):
        x, z = (self.x, self.over_x), (self.z, self.over_z)
        return (z, x) if self.is_early(a, n) else (x, z)

    def first_part(self, a, which):
        if self.is_tall(a):
            return pl.ds(pl.multiple_of(which * self.half, 16), self.half), slice(None)
        return slice(None), pl.ds(pl.multiple_of(which * 256, 128), 256)

    def second_part(self, which):
        return slice(None), pl.ds(pl.multiple_of(which * 128, 128), 128)

    def back_at(self, a, c, x=None, z=None):
        half = self.half
        if self.is_tall(a):
            if x is None:
                return pl.ds(pl.multiple_of(c * 2 * half, 16), 2 * half), slice(None)
            rows = pl.ds(pl.multiple_of(c * 2 * half + x * half, 16), half)
            return rows, slice(None) if z is None else pl.ds(pl.multiple_of(z * 128, 128), 128)
        rows = pl.ds(pl.multiple_of(c * half, 16), half)
        if x is None:
            return rows, slice(None)
        if z is None:
            return rows, pl.ds(pl.multiple_of(x * 256, 128), 256)
        return rows, pl.ds(pl.multiple_of(x * 256 + z * 128, 128), 128)

    def route(self, stage, a, n, src, dst, partner):
        return Route(src, dst, self.send_sem.at[stage, a, n], self.recv_sem.at[stage, a, n], partner)

    def copy(self, stage, a, n):
        loc, core_in, y_in, x_in, z_in, more_in, back = (self.box(i, a, n) for i in range(7))
        (first, over_first), (second, over_second) = self.axes(a, n)
        early = self.is_early(a, n)
        more = len(self.extra)
        if stage < 2:
            leaving = self.sibling_share(a, n).at[stage] if self.rings else self.source(a, n, 1 - self.core, stage)
            return self.route(stage, a, n, leaving, core_in.at[stage], self.sibling)
        if early and stage in (2, 8 + more):
            which = 0 if stage == 2 else 1
            return self.route(stage, a, n, loc.at[(which,) + self.first_part(a, 1 - first)],
                              y_in.at[:, pl.ds(which * 256, 256)], over_first)
        if early and stage == 3:
            return self.route(stage, a, n, loc.at[(1 - self.y,) + self.first_part(a, first)], x_in, self.over_y)
        if stage == 2:
            return self.route(stage, a, n, loc.at[1 - self.y], y_in, self.over_y)
        if stage == 3:
            return self.route(stage, a, n, y_in.at[self.first_part(a, 1 - first)], x_in, over_first)
        if stage == 4:
            return self.route(stage, a, n, x_in.at[self.second_part(1 - second)], z_in, over_second)
        if stage < 5 + more:
            so_far = z_in if stage == 5 else more_in.at[stage - 6]
            return self.route(stage, a, n, so_far, more_in.at[stage - 5], self.extra[stage - 5])
        at = [(self.core, first, second), (self.core, first), (self.core,)][stage - 5 - more]
        part = back.at[self.back_at(a, *at)]
        return self.route(stage, a, n, part, part, (over_second, over_first, self.sibling)[stage - 5 - more])

    def puts(self, a, n):
        box, out = self.box(6, a, n), self.outs[a]
        if self.is_tall(a):
            return [pltpu.make_async_copy(box, out.at[:, pl.ds(pl.multiple_of(n * 256, 128), 256)], self.put_sem.at[0, a, n])]
        if not self.rings:
            return [pltpu.make_async_copy(box, out.at[:, pl.ds(pl.multiple_of(n * WIDE, 128), WIDE)], self.put_sem.at[0, a, n])]
        return [
            pltpu.make_async_copy(
                box.at[:, pl.ds(i * 256, 256)],
                out.at[:, pl.ds(pl.multiple_of(i * (out.shape[1] // 2) + n * 256, 128), 256)],
                self.put_sem.at[i, a, n])
            for i in range(2)
        ]

    def start_core(self, a, n):
        for which in range(2):
            self.copy(which, a, n).start()

    def core_sent(self, a, n):
        for which in range(2):
            self.copy(which, a, n).sent()

    def start_y(self, a, n):
        loc, core_in = self.box(0, a, n), self.box(1, a, n)
        for which in range(2):
            self.copy(which, a, n).arrived()
            mine = loc.at[which] if self.rings else self.source(a, n, self.core, which)
            loc[which] = mine[...] + core_in[which]
        self.copy(2, a, n).start()
        if self.is_early(a, n):
            self.copy(8 + len(self.extra), a, n).start()

    def start_x(self, a, n):
        loc, y_in = self.box(0, a, n), self.box(2, a, n)
        self.copy(2, a, n).arrived()
        if self.is_early(a, n):
            self.copy(8 + len(self.extra), a, n).arrived()
            (first, _), _ = self.axes(a, n)
            for which in range(2):
                spot = (which,) + self.first_part(a, first)
                loc[spot] = loc[spot] + y_in[:, which * 256 : (which + 1) * 256]
        else:
            y_in[...] = y_in[...] + loc[self.y]
        self.copy(3, a, n).start()

    def start_z(self, a, n):
        loc, y_in, x_in = self.box(0, a, n), self.box(2, a, n), self.box(3, a, n)
        (first, _), _ = self.axes(a, n)
        self.copy(3, a, n).arrived()
        if self.is_early(a, n):
            x_in[...] = x_in[...] + loc[(self.y,) + self.first_part(a, first)]
        else:
            x_in[...] = x_in[...] + y_in[self.first_part(a, first)]
        self.copy(4, a, n).start()

    def more(self, step, a, n):
        x_in, z_in, more_in, back = (self.box(i, a, n) for i in range(3, 7))
        (first, _), (second, _) = self.axes(a, n)
        self.copy(4 + step, a, n).arrived()
        if step == 0:
            total = z_in
            value = z_in[...] + x_in[self.second_part(second)]
        else:
            total = more_in.at[step - 1]
            value = (z_in if step == 1 else more_in.at[step - 2])[...] + total[...]
        if step < len(self.extra):
            total[...] = value
        else:
            back[self.back_at(a, self.core, first, second)] = value
        self.copy(5 + step, a, n).start()

    def back_x(self, a, n):
        stage = 5 + len(self.extra)
        self.copy(stage, a, n).arrived()
        self.copy(stage + 1, a, n).start()

    def back_core(self, a, n):
        stage = 6 + len(self.extra)
        self.copy(stage, a, n).arrived()
        self.copy(stage + 1, a, n).start()

    def finish(self, a, n):
        self.copy(7 + len(self.extra), a, n).arrived()
        for put in self.puts(a, n):
            put.start()

    def drain(self, a, n):
        for stage in range(2, 8 + len(self.extra) + self.is_early(a, n)):
            self.copy(stage, a, n).sent()
        for put in self.puts(a, n):
            put.wait()


OWN_SIB, OWN_Y, OWN_NEXT, PASS_OWN, PREV_SIB, PREV_Y, PASS_PREV = range(7)
WEIGHT_CHUNKS = 5
FIRST_ROWS = (((0, 64), (64, 64)), ((128, 64), (192, 48)))


def forward_kernel(groups, low_ref, cosine, sine, x_ref, q_in, k_in, v_in, gains_in, wo_in, gate_in, up_in, down_in,
                   o_ref, lse_ref, q_ref, h_ref, scale_ref, gains, kv_out, qkv_out, wo_out, gate_out, up_out, down_out,
                   kv, kv_flip, w_qkv, wo, gate, up, down, top, acc, shrink, s_all, p_all,
                   kv_sem, load_sem, store_sem, send_sem, recv_sem, w_send, w_recv, wo_send, wo_recv, first_send, first_recv):
    dp, y = place()
    core, x, z = dp % 2, (dp // 2) % 2, (dp // 4) % 2
    k = dp // 2
    j = 2 * core + y
    j_y = 2 * core + 1 - y
    sibling, over_y, over_x, over_z = other(dp, y, 0), (dp, 1 - y), other(dp, y, 1), other(dp, y, 2)
    own = x_ref.shape[1]
    has_prev, has_next = k > 0, k < groups - 1
    first_core, last_core = core == 0, core == 1

    half, tall = gate_in.shape[0], down_in.shape[1]
    own_rows = pl.ds(pl.multiple_of(y * half, 16), half)
    own_cols = pl.ds(pl.multiple_of(y * tall, 128), tall)
    loads = [
        pltpu.make_async_copy(q_in, w_qkv.at[own_rows, pl.ds(2 * KV_HEADS * HEAD_DIM, D)], load_sem.at[0]),
        pltpu.make_async_copy(gains_in, gains.at[own_rows, :], load_sem.at[1]),
        pltpu.make_async_copy(gate_in, gate.at[own_rows, :], load_sem.at[2]),
        pltpu.make_async_copy(up_in, up.at[own_rows, :], load_sem.at[3]),
        pltpu.make_async_copy(down_in, down.at[:, own_cols], load_sem.at[4]),
        pltpu.make_async_copy(wo_in, wo.at[own_rows, :], load_sem.at[5]),
    ]
    flips = [pltpu.make_async_copy(w, kv_flip.at[i], load_sem.at[6 + i]) for i, w in enumerate((k_in, v_in))]
    for copy in flips + loads[:2]:
        copy.start()

    @pl.when(k == 0)
    def _():
        kv[:, : 4 * own, :] = jnp.zeros((KV_HEADS, 4 * own, 2 * HEAD_DIM), BF16)

    barrier = pltpu.get_barrier_semaphore()
    for partner in (sibling, over_y, over_x, over_z):
        pl.semaphore_signal(barrier, inc=1, device_id=partner, device_id_type=MESH)

    @pl.when(has_prev)
    def _():
        pl.semaphore_signal(barrier, inc=1, device_id=(dp - 2, y), device_id_type=MESH)

    @pl.when(has_next)
    def _():
        pl.semaphore_wait(barrier, 5)

    @pl.when(jnp.logical_not(has_next))
    def _():
        pl.semaphore_wait(barrier, 4)

    def slot(h, n):
        return kv.at[h, pl.ds(pl.multiple_of(n * own, own), own), :]

    def halo(route, h):
        after = jnp.minimum(dp + 2, 2 * groups - 1)
        sems = (send_sem.at[route, h], recv_sem.at[route, h])
        if route == OWN_SIB:
            return Route(slot(h, 4 + j), slot(h, 4 + j), *sems, sibling)
        if route == OWN_Y:
            return Route(slot(h, 4 + j), slot(h, 4 + j), *sems, over_y)
        if route == OWN_NEXT:
            return Route(slot(h, 4 + j), slot(h, j), *sems, (after, y))
        if route == PASS_OWN:
            return Route(slot(h, 4 + j_y), slot(h, 4 + j_y), *sems, sibling)
        if route == PREV_SIB:
            return Route(slot(h, j), slot(h, j), *sems, sibling)
        if route == PREV_Y:
            return Route(slot(h, j), slot(h, j), *sems, over_y)
        return Route(slot(h, j_y), slot(h, j_y), *sems, sibling)

    sent_if = {
        OWN_SIB: first_core, OWN_Y: j != 3, OWN_NEXT: has_next, PASS_OWN: first_core,
        PREV_SIB: jnp.logical_and(last_core, has_prev), PREV_Y: jnp.logical_and(j != 0, has_prev),
        PASS_PREV: jnp.logical_and(last_core, has_prev),
    }
    got_if = {
        OWN_SIB: last_core, OWN_Y: j != 2, OWN_NEXT: has_prev, PASS_OWN: last_core,
        PREV_SIB: jnp.logical_and(first_core, has_prev), PREV_Y: jnp.logical_and(j != 1, has_prev),
        PASS_PREV: jnp.logical_and(first_core, has_prev),
    }

    def start(route, h):
        pl.when(sent_if[route])(lambda: halo(route, h).start())

    def arrived(route, h):
        pl.when(got_if[route])(lambda: halo(route, h).arrived())

    def pass_one(h):
        arrived(OWN_Y, h)
        start(PASS_OWN, h)
        arrived(OWN_NEXT, h)
        start(PREV_SIB, h)
        start(PREV_Y, h)

    def pass_two(h):
        arrived(PREV_Y, h)
        start(PASS_PREV, h)

    part = half // 2

    def wide_at(which, n, width_from, width):
        rows = pl.ds(pl.multiple_of(which * half + core * part, 16), part)
        return rows, pl.ds(pl.multiple_of(n * WIDE + width_from, 128), width)

    def down_at(which, n, row_from, rows, col_from, cols):
        return (pl.ds(pl.multiple_of(row_from, 16), rows),
                pl.ds(pl.multiple_of(which * tall + n * 256 + col_from, 128), cols))

    def weights(stage, a, n):
        out = (gate, up, down)[a]
        which = y if stage == 0 else 1 - y
        rows = core * half
        if a < 2:
            size = [(z * 256 + x * 128, 128), (z * 256 + x * 128, 128), (z * 256, 256), (0, 512)][stage]
            region = out.at[wide_at(which, n, *size)]
        else:
            size = [(rows + z * part, part, x * 128, 128), (rows + z * part, part, x * 128, 128),
                    (rows + z * part, part, 0, 256), (rows, half, 0, 256)][stage]
            region = out.at[down_at(which, n, *size)]
        partner = (over_y, over_x, over_z, sibling)[stage]
        return Route(region, region, w_send.at[stage, a, n], w_recv.at[stage, a, n], partner)

    def hand_on(stage, a, n):
        weights(stage - 1, a, n).arrived()
        weights(stage, a, n).start()

    def store(a, n):
        if a < 2:
            cols = pl.ds(pl.multiple_of(n * WIDE, 128), WIDE)
            box, out = ((gate, gate_out), (up, up_out))[a]
            return [pltpu.make_async_copy(box.at[:, cols], out.at[:, cols], store_sem.at[a, n])]
        copies = []
        for which in range(2):
            some = pl.ds(pl.multiple_of(which * tall + n * 256, 128), 256)
            copies.append(pltpu.make_async_copy(down.at[:, some], down_out.at[:, some], store_sem.at[2 + which, n]))
        return copies

    def keep(a, n):
        weights(3, a, n).arrived()
        for copy in store(a, n):
            copy.start()

    def wo_part(which):
        return wo.at[pl.ds(pl.multiple_of(which * half + core * part, 16), part), :]

    wo_across = Route(wo_part(y), wo_part(y), wo_send.at[0], wo_recv.at[0], over_y)
    wo_within = Route(wo_part(1 - y), wo_part(1 - y), wo_send.at[1], wo_recv.at[1], sibling)
    wo_store = pltpu.make_async_copy(wo, wo_out, store_sem.at[0, WEIGHT_CHUNKS])

    def first(kind, i, which_x):
        row, count = FIRST_ROWS[which_x][i]
        at = (y if kind == 0 else 1 - y) * half + core * part + row
        region = w_qkv.at[pl.ds(pl.multiple_of(at, 16), count), :]
        return Route(region, region, first_send.at[kind, i], first_recv.at[kind, i], over_y if kind == 0 else over_x)

    def by_x(act, swap=False):
        for which_x in range(2):
            @pl.when(x == (1 - which_x if swap else which_x))
            def _(which_x=which_x):
                act(which_x)

    def first_part(which):
        return w_qkv.at[pl.ds(pl.multiple_of(which * half + core * part, 16), part), :]

    first_within = Route(first_part(1 - y), first_part(1 - y), first_send.at[2, 0], first_recv.at[2, 0], sibling)
    gains_across = Route(gains.at[own_rows, :], gains.at[own_rows, :], first_send.at[2, 1], first_recv.at[2, 1], over_y)
    first_store = pltpu.make_async_copy(w_qkv, qkv_out, store_sem.at[1, WEIGHT_CHUNKS])

    def across(n):
        for a in range(3):
            weights(0, a, n).start()

    def onward(stage, n):
        for a in range(3):
            hand_on(stage, a, n)

    for copy in flips:
        copy.wait()
    for i in range(2):
        w_qkv[own_rows, i * KV_HEADS * HEAD_DIM : (i + 1) * KV_HEADS * HEAD_DIM] = kv_flip[i].T
    loads[0].wait()
    loads[1].wait()
    gains_across.start()
    by_x(lambda which_x: [first(0, i, which_x).start() for i in range(2)])
    for copy in loads[2:]:
        copy.start()

    value = x_ref[...].astype(F32)
    scale = lax.rsqrt(jnp.mean(value * value, axis=0, keepdims=True) + EPSILON)
    scale_ref[...] = scale
    gains_across.arrived()
    h_ref[...] = (value * scale * gains[:, 0:1].astype(F32)).astype(BF16)
    for copy in loads[2:]:
        copy.wait()

    for i in range(2):
        def pass_first(which_x, i=i):
            first(0, i, which_x).arrived()
            first(1, i, which_x).start()

        by_x(pass_first)
        across(i)
    across(2)
    for i in range(2):
        by_x(lambda which_x, i=i: first(1, i, which_x).arrived(), swap=True)
    first_within.start()
    onward(1, 0)
    first_within.arrived()
    first_store.start()

    kv_width = KV_HEADS * HEAD_DIM
    turn = HEAD_DIM // 2

    def rotated(values):
        one, two = values[:turn], values[turn:]
        cos, sin = cosine[...], sine[...]
        return jnp.concatenate([one * cos - two * sin, two * cos + one * sin], axis=0)

    keys_values = over_first(w_qkv[:, : 2 * kv_width], h_ref[...])
    for h in range(KV_HEADS):
        at = h * HEAD_DIM
        both = jnp.concatenate(
            [rotated(keys_values[at : at + HEAD_DIM]), keys_values[kv_width + at : kv_width + at + HEAD_DIM]], axis=0
        ).astype(BF16)
        slot(h, 4 + j)[...] = both.T
        if h < 2:
            for route in (OWN_Y, OWN_NEXT, OWN_SIB):
                start(route, h)
    onward(2, 0)
    onward(1, 1)
    queries_all = over_first(w_qkv[:, 2 * kv_width :], h_ref[...])
    for h in range(HEADS):
        at = h * HEAD_DIM
        q_ref[at : at + HEAD_DIM, :] = rotated(queries_all[at : at + HEAD_DIM]).astype(BF16)
    pass_one(0)
    onward(2, 1)
    pass_two(0)

    def window(h):
        return pltpu.make_async_copy(
            kv.at[h, pl.ds(pl.multiple_of(j * own, own), 5 * own), :], kv_out.at[h], kv_sem.at[h])

    blocks = own // CHUNK
    third = GROUP * CHUNK

    def block(h, n, spans, diagonal):
        both = kv[h, pl.ds(pl.multiple_of(n * own, own), own), :]
        keys = both[:, :HEAD_DIM]
        values = jnp.concatenate([both[:, HEAD_DIM:].T, jnp.ones((16, own), BF16)], axis=0)
        begin_at = (n - 4 - j) * own
        for b in range(blocks):
            low_at, high_at = spans[b]
            low = low_ref[:, b * CHUNK : (b + 1) * CHUNK]
            for r in range(GROUP):
                cols = pl.ds(b * third + r * CHUNK, CHUNK)
                rows = pl.ds(pl.multiple_of(h * GROUP * HEAD_DIM + r * HEAD_DIM, HEAD_DIM), HEAD_DIM)
                queries = q_ref[rows, b * CHUNK : (b + 1) * CHUNK]
                old = top[:, cols]
                high = jnp.full((8, CHUNK), MASKED, F32)
                for at in range(low_at, high_at, STRIP):
                    rows = slice(at, at + STRIP)
                    s = masked(dot(keys[rows], queries), begin_at + at, low, b * CHUNK if diagonal else None)
                    s_all[rows, cols] = s
                    high = jnp.maximum(high, jnp.max(s.reshape(STRIP // 8, 8, CHUNK), axis=0))
                new = jnp.maximum(old, jnp.max(high, axis=0, keepdims=True))
                bound = new * SCALE2
                for at in range(low_at, high_at, STRIP):
                    rows = slice(at, at + STRIP)
                    p_all[rows, cols] = jnp.exp2(s_all[rows, cols] * SCALE2 - bound).astype(BF16)
                shrink[:, cols] = jnp.exp2(old * SCALE2 - bound)
                top[:, cols] = new
        for b in range(blocks):
            low_at, high_at = spans[b]
            cols = pl.ds(b * third, third)
            acc[:, cols] = acc[:, cols] * shrink[:, cols] + dot(values[:, low_at:high_at], p_all[low_at:high_at, cols])

    every = [(0, own)] * blocks
    plan = [(4 + j, [(0, (b + 1) * CHUNK) for b in range(blocks)], True),
            (j, [(b * CHUNK, own) for b in range(blocks)], False),
            (j + 2, every, False), (j + 1 + 2 * y, every, False), (j + 3 - 2 * y, every, False)]
    spots = len(plan)
    steps = [(functools.partial(hand_on, 1), 0, 2), (functools.partial(hand_on, 2), 3, 2),
             (functools.partial(hand_on, 3), 1, 1), (keep, 4, 1)]

    def head(h, carry):
        top[...] = jnp.full(top.shape, MASKED, F32)
        acc[...] = jnp.zeros(acc.shape, F32)

        for p in range(spots):
            if p == 0:
                @pl.when(h < KV_HEADS - 1)
                def _():
                    pass_one(h + 1)

                @pl.when(h < KV_HEADS - 2)
                def _():
                    for route in (OWN_Y, OWN_NEXT, OWN_SIB):
                        start(route, h + 2)

                pl.when(h == 0)(lambda: onward(3, 0))
            if p == 1:
                pl.when(h < KV_HEADS - 3)(lambda: across(h + 3))
                pl.when(h == 2)(lambda: wo_across.start())
            if p == 2:
                arrived(PREV_SIB, h)
                arrived(OWN_SIB, h)
            if p == 4:
                pl.when(h < KV_HEADS - 1)(lambda: pass_two(h + 1))
                arrived(PASS_PREV, h)
                arrived(PASS_OWN, h)

                @pl.when(h == KV_HEADS - 1)
                def _():
                    wo_across.arrived()
                    wo_within.start()
            if p == 1:
                pl.when(h == 0)(lambda: keep(0, 0))
            block(h, *plan[p])
            for step, spot, ahead in reversed(steps):
                for a in range(3):
                    if (p - a - spot) % spots == 0:
                        n = h + ahead + (p - a - spot) // spots
                        fits = jnp.logical_and(n >= (1 if ahead == 1 and step is not keep else 0), n < WEIGHT_CHUNKS)
                        fits = jnp.logical_and(fits, n >= 2) if ahead == 2 else fits
                        pl.when(fits)(lambda step=step, a=a, n=n: step(a, n))

        window(h).start()
        for r in range(GROUP):
            rows = pl.ds(pl.multiple_of(h * GROUP * HEAD_DIM + r * HEAD_DIM, HEAD_DIM), HEAD_DIM)
            for b in range(blocks):
                cols = pl.ds(b * third + r * CHUNK, CHUNK)
                total = acc[HEAD_DIM : HEAD_DIM + 1, cols]
                o_ref[rows, b * CHUNK : (b + 1) * CHUNK] = (acc[:HEAD_DIM, cols] / total).astype(BF16)
                lse_ref[h, r : r + 1, b * CHUNK : (b + 1) * CHUNK] = top[:, cols] * SCALE2 + jnp.log2(total)
        return carry

    lax.fori_loop(0, KV_HEADS, head, 0)
    wo_within.arrived()
    wo_store.start()

    def finish(h, carry):
        for a in range(3):
            for stage in range(4):
                weights(stage, a, h).sent()
            for copy in store(a, h):
                copy.wait()
        for route in range(7):
            pl.when(sent_if[route])(lambda route=route: halo(route, h).sent())
        window(h).wait()
        return carry

    lax.fori_loop(0, KV_HEADS, finish, 0)
    for route in (wo_across, wo_within, first_within, gains_across):
        route.sent()
    by_x(lambda which_x: [first(kind, i, which_x).sent() for kind in range(2) for i in range(2)])
    wo_store.wait()
    first_store.wait()


def attend(low, cosine, sine, x, w_query, w_key_t, w_value_t, gains, w_output, w_gate, w_up, w_down_t, dp_size):
    own = x.shape[1]
    width = GROUP * own
    any_spec = pl.BlockSpec(memory_space=pl.ANY)
    vmem = pl.BlockSpec(memory_space=pltpu.VMEM)
    later = [jax.ShapeDtypeStruct((2 * w.shape[0], w.shape[1]), BF16) for w in (w_output, w_gate, w_up)]
    later.insert(0, jax.ShapeDtypeStruct((D, D + 2 * w_key_t.shape[0]), BF16))
    later.append(jax.ShapeDtypeStruct((w_down_t.shape[0], 2 * w_down_t.shape[1]), BF16))
    return pl.pallas_call(
        functools.partial(forward_kernel, dp_size // 2),
        out_shape=[
            jax.ShapeDtypeStruct((D, own), BF16),
            jax.ShapeDtypeStruct((KV_HEADS, 8, own), F32),
            jax.ShapeDtypeStruct((D, own), BF16),
            jax.ShapeDtypeStruct((D, own), BF16),
            jax.ShapeDtypeStruct((1, own), F32),
            jax.ShapeDtypeStruct((2 * gains.shape[0], gains.shape[1]), BF16),
            jax.ShapeDtypeStruct((KV_HEADS, 5 * own, 2 * HEAD_DIM), BF16),
        ] + later,
        in_specs=[vmem] * 4 + [any_spec] * 8,
        out_specs=[vmem] * 6 + [any_spec] * 6,
        scratch_shapes=[pltpu.VMEM((KV_HEADS, 8 * own, 2 * HEAD_DIM), BF16), pltpu.VMEM((2,) + w_key_t.shape, BF16)]
        + [pltpu.VMEM(w.shape, BF16) for w in later]
        + [
            pltpu.VMEM((1, width), F32),
            pltpu.VMEM((HEAD_DIM + 16, width), F32),
            pltpu.VMEM((1, width), F32),
            pltpu.VMEM((own, width), F32),
            pltpu.VMEM((own, width), BF16),
            pltpu.SemaphoreType.DMA((KV_HEADS,)),
            pltpu.SemaphoreType.DMA((8,)),
            pltpu.SemaphoreType.DMA((4, WEIGHT_CHUNKS + 1)),
            pltpu.SemaphoreType.DMA((7, KV_HEADS)),
            pltpu.SemaphoreType.DMA((7, KV_HEADS)),
            pltpu.SemaphoreType.DMA((4, 3, WEIGHT_CHUNKS)),
            pltpu.SemaphoreType.DMA((4, 3, WEIGHT_CHUNKS)),
            pltpu.SemaphoreType.DMA((2,)),
            pltpu.SemaphoreType.DMA((2,)),
            pltpu.SemaphoreType.DMA((3, 2)),
            pltpu.SemaphoreType.DMA((3, 2)),
        ],
        compiler_params=pltpu.CompilerParams(
            collective_id=2, has_side_effects=True, vmem_limit_bytes=56 * 1024 * 1024),
        name="attend",
    )(low, cosine, sine, x, w_query, w_key_t, w_value_t, gains, w_output, w_gate, w_up, w_down_t)


FEED = 256


def middle_kernel(bits, groups, low_ref, cosine, sine, gains_ref, att_ref, lse_ref,
                  x_in, g_in, q_in, kv_in, wo_in, gate_in, up_in, down_in,
                  out_ref, dx_ref, branch_ref, row_ref, gate_out, up_out, down_out, dq_out, dkv_out,
                  ring, ring_down, far_in, sib_in, far_y, own_y, next_in, halo_send, halo_recv, feed_sem, load_sem, *scratch):
    own = x_in.shape[1]
    half_ff = gate_in.shape[1] // 2
    chunks = half_ff // FEED
    dp, y = place()
    core = dp % 2
    k = dp // 2
    j = 2 * core + y
    j_y = 2 * core + 1 - y
    has_prev, has_next = k > 0, k < groups - 1
    first_core, last_core = core == 0, core == 1
    half = D // 4
    sums = Sums(bits, [None, None], down_in, [gate_out, up_out, down_out], scratch, (ring, ring_down))

    barrier = pltpu.get_barrier_semaphore()
    for partner in sums.partners:
        pl.semaphore_signal(barrier, inc=1, device_id=partner, device_id_type=MESH)

    @pl.when(has_next)
    def _():
        pl.semaphore_signal(barrier, inc=1, device_id=(dp + 2, y), device_id_type=MESH)

    spots = 5
    begins = {0: (-1, 1, 4), 1: (0, 1, 3), 2: (1, 1, 3), 3: (3, 0, 2), 4: (4, 0, 1)}
    events = {(0, 0): [(sums.start_y, a, chunks - 2) for a in range(3)], (0, 2): [(sums.start_y, a, chunks - 1) for a in range(3)]}
    for n in range(chunks):
        turn, spot, lag = begins[n]
        for s in range(len(sums.stages)):
            for a in range(3):
                at = turn * spots + spot + a + lag * s
                events.setdefault((at // spots, at % spots), []).insert(0, (sums.stages[s], a, n))
    last_round = max(turn for turn, spot in events)

    def advance(p, h):
        if isinstance(h, int):
            for step, a, n in events.get((h, p), ()):
                step(a, n)
            return
        for turn in range(KV_HEADS):
            if (turn, p) in events:
                pl.when(h == turn)(lambda turn=turn: advance(p, turn))

    def feed_phase(weights, wo, h_t, g_t, x, h, g, acc):
        def load(n, s):
            cols = pl.ds(pl.multiple_of(s * half_ff + n * FEED, 128), FEED)
            return [pltpu.make_async_copy(w.at[:, cols], weights.at[s, i], feed_sem.at[s, i])
                    for i, w in enumerate((gate_in, up_in, down_in))]

        first = [pltpu.make_async_copy(a, b, load_sem.at[i]) for i, (a, b) in enumerate(((x_in, h_t), (g_in, g_t), (wo_in, wo)))]
        for copy in first + load(0, 0):
            copy.start()
        for copy in first:
            copy.wait()
        gain = gains_ref[:, 1:2].astype(F32)
        x[...] = h_t[...].astype(F32) + over_first(wo[...], att_ref[...])
        scale = lax.rsqrt(jnp.mean(x[...] * x[...], axis=0, keepdims=True) + EPSILON)
        h_t[...] = (x[...] * scale * gain).astype(BF16)
        h[...] = h_t[...].T
        g[...] = g_t[...].T
        acc[...] = x[...]
        dx_ref[...] = jnp.zeros(dx_ref.shape, F32)

        @pl.when(has_prev)
        def _():
            pl.semaphore_wait(barrier, len(sums.partners) + 1)

        @pl.when(jnp.logical_not(has_prev))
        def _():
            pl.semaphore_wait(barrier, len(sums.partners))

        def step(n, s):
            for copy in load(n, s):
                copy.wait()
            if s == 0:
                for copy in load(n, 1):
                    copy.start()
            else:
                @pl.when(n < chunks - 1)
                def _():
                    for copy in load(n + 1, 0):
                        copy.start()

            w_gate, w_up, w_down = weights[s, 0], weights[s, 1], weights[s, 2]
            gate = dot(h[...], w_gate)
            upper = dot(h[...], w_up)
            dm = dot(g[...], w_down)
            sigmoid = 1.0 / (1.0 + jnp.exp(-gate))
            active = gate * sigmoid
            inner = (active * upper).astype(BF16)
            dgate = (dm * upper * sigmoid * (1.0 + gate * (1.0 - sigmoid))).astype(BF16)
            dup = (dm * active).astype(BF16)
            acc[...] += against_rows(w_down, inner)
            dx_ref[...] += against_rows(w_gate, dgate) + against_rows(w_up, dup)
            cols = slice(s * FEED, (s + 1) * FEED)
            for c, shares in ((core, sums.own_share), (1 - core, sums.sibling_share)):
                for which in range(2):
                    rows = pl.ds(pl.multiple_of(which * 2 * half + c * half, 16), half)
                    left = h_t[rows, :]
                    for a, right in enumerate((dgate, dup)):
                        shares(a, n)[which, :, cols] = dot(left, right).astype(BF16)
                rows = pl.ds(pl.multiple_of(c * 2 * half, 16), 2 * half)
                shares(2, n)[s] = dot(g_t[rows, :], inner).astype(BF16)

        def round_of(n, carry):
            @pl.when(n > 1)
            def _():
                for a in range(3):
                    sums.core_sent(a, n - 2)

            step(n, 0)

            @pl.when(jnp.logical_and(n > 0, n < chunks - 1))
            def _():
                for a in range(3):
                    sums.start_y(a, n - 1)

            pl.when(n == chunks - 1)(lambda: (advance(1, -1), advance(2, -1))[0])
            step(n, 1)
            for a in range(3):
                sums.start_core(a, n)
            pl.when(n == chunks - 1)(lambda: (advance(3, -1), advance(4, -1))[0])
            return carry

        lax.fori_loop(0, chunks, round_of, 0)
        out_ref[...] = acc[...].astype(BF16)
        dh = dx_ref[...]
        acc[...] = dh * (x[...] * scale)
        ones = jnp.ones((8, own), F32)
        row_ref[...] = lax.dot_general(ones, acc[...], (((1,), (1,)), ((), ())), precision=lax.Precision.HIGHEST,
                                       preferred_element_type=F32)
        mean = jnp.sum(acc[...] * gain, axis=0, keepdims=True) * (1.0 / D)
        dx = g_t[...].astype(F32) + scale * (dx_ref[...] * gain - x[...] * scale * mean)
        dx_ref[...] = dx
        branch_ref[...] = dx.astype(BF16)

    pl.run_scoped(
        feed_phase,
        pltpu.VMEM((2, 3, D, FEED), BF16),
        pltpu.VMEM((D, D), BF16),
        pltpu.VMEM((D, own), BF16),
        pltpu.VMEM((D, own), BF16),
        pltpu.VMEM((D, own), F32),
        pltpu.VMEM((own, D), BF16),
        pltpu.VMEM((own, D), BF16),
        pltpu.VMEM((D, own), F32),
    )
    for n in (chunks - 2, chunks - 1):
        for a in range(3):
            sums.core_sent(a, n)

    blocks = own // CHUNK
    third = GROUP * CHUNK

    def attention_phase(wo, q, do, kv, q_all, do_all, q_rows, do_rows, delta, dq_acc, p_all, ds_all, part, dq, dkv):
        first = [pltpu.make_async_copy(a, b, load_sem.at[i]) for i, (a, b) in enumerate(((wo_in, wo), (q_in, q)))]

        def window(h, at):
            return pltpu.make_async_copy(kv_in.at[h], kv.at[at], feed_sem.at[at, 0])

        for copy in first + [window(0, 0)]:
            copy.start()
        part[...] = jnp.zeros(part.shape, BF16)
        for copy in first:
            copy.wait()
        do[...] = dot(wo[...], branch_ref[...]).astype(BF16)

        def slot(h, n):
            return part.at[h, pl.ds(pl.multiple_of(n * own, own), own), :]

        def halo(route, h):
            before = jnp.maximum(dp - 2, 0)
            sems = (halo_send.at[route, h], halo_recv.at[route, h])
            if route == PASS_PREV:
                return Route(slot(h, j_y + 2 - 4 * core), far_in.at[h], *sems, sums.sibling)
            if route == PASS_OWN:
                return Route(slot(h, 2 + j_y), far_in.at[h], *sems, sums.sibling)
            if route == PREV_SIB:
                return Route(slot(h, j + 2 - 4 * core), sib_in.at[h], *sems, sums.sibling)
            if route == OWN_SIB:
                return Route(slot(h, 2 + j), sib_in.at[h], *sems, sums.sibling)
            if route == PREV_Y:
                return Route(slot(h, j_y), far_y.at[h], *sems, sums.over_y)
            if route == OWN_Y:
                return Route(slot(h, 4 + j_y), own_y.at[h], *sems, sums.over_y)
            return Route(slot(h, j), next_in.at[h], *sems, (before, y))

        got_if = {
            OWN_SIB: first_core, OWN_Y: j != 3, OWN_NEXT: has_next, PASS_OWN: first_core,
            PREV_SIB: jnp.logical_and(last_core, has_prev), PREV_Y: jnp.logical_and(j != 0, has_prev),
            PASS_PREV: jnp.logical_and(last_core, has_prev),
        }
        sent_if = {
            OWN_SIB: last_core, OWN_Y: j != 2, OWN_NEXT: has_prev, PASS_OWN: last_core,
            PREV_SIB: jnp.logical_and(first_core, has_prev), PREV_Y: jnp.logical_and(j != 1, has_prev),
            PASS_PREV: jnp.logical_and(first_core, has_prev),
        }

        def start(route, h):
            pl.when(sent_if[route])(lambda: halo(route, h).start())

        def take(route, h, n, box):
            @pl.when(got_if[route])
            def _():
                halo(route, h).arrived()
                spot = slot(h, n)
                spot[...] = spot[...] + box[h]

        def return_one(h):
            for route in (PASS_PREV, PASS_OWN, PREV_SIB, OWN_SIB):
                start(route, h)

        def return_two(h):
            take(PASS_PREV, h, j_y, far_in)
            take(PASS_OWN, h, 4 + j_y, far_in)
            start(PREV_Y, h)
            start(OWN_Y, h)

        def return_three(h):
            for route, n, box in ((PREV_SIB, j, sib_in), (OWN_SIB, 4 + j, sib_in), (PREV_Y, j, far_y), (OWN_Y, 4 + j, own_y)):
                take(route, h, n, box)
            start(OWN_NEXT, h)

        def return_four(h):
            dkv[h] = slot(h, 4 + j)[...].astype(F32)

            @pl.when(has_next)
            def _():
                halo(OWN_NEXT, h).arrived()
                dkv[h] = dkv[h] + next_in[h].astype(F32)

        def head_rows(h, r):
            return pl.ds(pl.multiple_of(h * GROUP * HEAD_DIM + r * HEAD_DIM, HEAD_DIM), HEAD_DIM)

        def prepare(h):
            for r in range(GROUP):
                rows = head_rows(h, r)
                for b in range(blocks):
                    cols = pl.ds(b * third + r * CHUNK, CHUNK)
                    from_cols = slice(b * CHUNK, (b + 1) * CHUNK)
                    grad, queries = do[rows, from_cols], q[rows, from_cols]
                    q_all[:, cols] = queries
                    do_all[:, cols] = grad
                    q_rows[cols, :] = queries.T
                    do_rows[cols, :] = grad.T
                    delta[:, cols] = jnp.sum(grad.astype(F32) * att_ref[rows, from_cols].astype(F32), axis=0, keepdims=True)
            dq_acc[...] = jnp.zeros(dq_acc.shape, F32)

        def block(h, at, n, spans, diagonal):
            both = kv[at, n * own : (n + 1) * own, :]
            keys, values = both[:, :HEAD_DIM], both[:, HEAD_DIM:]
            begin_at = (n - 4) * own
            for i in range(own // CHUNK):
                row = i * CHUNK
                some_keys, some_values = keys[row : row + CHUNK], values[row : row + CHUNK]
                using = [b for b in range(blocks) if spans[b][0] <= row < spans[b][1]]
                for b in using:
                    low = low_ref[:, b * CHUNK : (b + 1) * CHUNK]
                    for r in range(GROUP):
                        cols = pl.ds(b * third + r * CHUNK, CHUNK)
                        lse = lse_ref[h, r : r + 1, b * CHUNK : (b + 1) * CHUNK]
                        s = masked(dot(some_keys, q_all[:, cols]), begin_at + row, low, b * CHUNK if diagonal and b == i else None)
                        p = jnp.exp2(s * SCALE2 - lse)
                        p_all[:, cols] = p.astype(BF16)
                        ds_all[:, cols] = (p * (dot(some_values, do_all[:, cols]) - delta[:, cols])).astype(BF16)
                cols = pl.ds(using[0] * third, len(using) * third)
                dq_acc[:, cols] += dot(some_keys.T, ds_all[:, cols])
                dk = dot(ds_all[:, cols], q_rows[cols, :]) * 0.125
                dv = dot(p_all[:, cols], do_rows[cols, :])
                spot = pl.ds(pl.multiple_of((n + j) * own + row, CHUNK), CHUNK)
                part[h, spot, :] = jnp.concatenate([dk, dv], axis=1).astype(BF16)

        every = [(0, own)] * blocks
        plan = [(0, [(b * CHUNK, own) for b in range(blocks)], False), (1, every, False), (2, every, False),
                (3, every, False), (4, [(0, (b + 1) * CHUNK) for b in range(blocks)], True)]
        def guarded(fn, h):
            pl.when(jnp.logical_and(h >= 0, h < KV_HEADS))(lambda: fn(h))

        def head(h, carry):
            at = h % 2
            window(h, at).wait()

            @pl.when(h < KV_HEADS - 1)
            def _():
                window(h + 1, 1 - at).start()

            prepare(h)
            for p in range(spots):
                block(h, at, *plan[p])
                advance(p, h)
                if p == 1:
                    guarded(return_two, h - 1)
                if p == 4:
                    guarded(return_three, h - 3)
            return_one(h)
            for r in range(GROUP):
                rows = head_rows(h, r)
                for b in range(blocks):
                    value = dq_acc[:, pl.ds(b * third + r * CHUNK, CHUNK)] * 0.125
                    spot = slice(b * CHUNK, (b + 1) * CHUNK)
                    cos, sin = cosine[:, spot], sine[:, spot]
                    one, two = value[: HEAD_DIM // 2], value[HEAD_DIM // 2 :]
                    back = jnp.concatenate([one * cos + two * sin, two * cos - one * sin], axis=0)
                    dq[rows, spot] = back.astype(BF16)
            return carry

        lax.fori_loop(0, KV_HEADS, head, 0)
        last = KV_HEADS - 1
        after = [(return_two, last), (return_three, 2), (return_three, 3), (return_four, 0), (return_four, 1),
                 (return_three, last), (return_four, 2), (return_four, 3)]
        for i in range((last_round - KV_HEADS + 1) * spots):
            if i < len(after):
                fn, h = after[i]
                fn(h)
            advance(i % spots, KV_HEADS + i // spots)
        for fn, h in after[(last_round - KV_HEADS + 1) * spots :]:
            fn(h)
        return_four(last)
        stores = [pltpu.make_async_copy(dq, dq_out, load_sem.at[0]), pltpu.make_async_copy(dkv, dkv_out, load_sem.at[1])]
        for store in stores:
            store.start()

        def finish(h, carry):
            for route in range(7):
                pl.when(sent_if[route])(lambda route=route: halo(route, h).sent())
            return carry

        lax.fori_loop(0, KV_HEADS, finish, 0)
        for store in stores:
            store.wait()

    width = GROUP * own
    pl.run_scoped(
        attention_phase,
        pltpu.VMEM((D, D), BF16),
        pltpu.VMEM((D, own), BF16),
        pltpu.VMEM((D, own), BF16),
        pltpu.VMEM((2, 5 * own, 2 * HEAD_DIM), BF16),
        pltpu.VMEM((HEAD_DIM, width), BF16),
        pltpu.VMEM((HEAD_DIM, width), BF16),
        pltpu.VMEM((width, HEAD_DIM), BF16),
        pltpu.VMEM((width, HEAD_DIM), BF16),
        pltpu.VMEM((1, width), F32),
        pltpu.VMEM((HEAD_DIM, width), F32),
        pltpu.VMEM((CHUNK, width), BF16),
        pltpu.VMEM((CHUNK, width), BF16),
        pltpu.VMEM((KV_HEADS, 8 * own, 2 * HEAD_DIM), BF16),
        pltpu.VMEM((D, own), BF16),
        pltpu.VMEM((KV_HEADS, own, 2 * HEAD_DIM), F32),
    )

    for n in range(chunks):
        for a in range(3):
            sums.drain(a, n)


def middle_and_back(low, cosine, sine, gains, attended, lse, x, cotangent, queries, both, w_output, w_gate, w_up, w_down_t,
           dp_size):
    own = x.shape[1]
    ff = w_gate.shape[1]
    bits = dp_size.bit_length() - 1
    half = D // 4
    chunks = ff // WIDE
    any_spec = pl.BlockSpec(memory_space=pl.ANY)
    vmem = pl.BlockSpec(memory_space=pltpu.VMEM)
    box = pltpu.VMEM((KV_HEADS, own, 2 * HEAD_DIM), BF16)
    return pl.pallas_call(
        functools.partial(middle_kernel, bits, dp_size // 2),
        out_shape=[
            jax.ShapeDtypeStruct((D, own), BF16),
            jax.ShapeDtypeStruct((D, own), F32),
            jax.ShapeDtypeStruct((D, own), BF16),
            jax.ShapeDtypeStruct((8, D), F32),
            jax.ShapeDtypeStruct((D // 2, ff), BF16),
            jax.ShapeDtypeStruct((D // 2, ff), BF16),
            jax.ShapeDtypeStruct((D, ff // 2), BF16),
            jax.ShapeDtypeStruct((D, own), BF16),
            jax.ShapeDtypeStruct((KV_HEADS, own, 2 * HEAD_DIM), F32),
        ],
        in_specs=[vmem] * 6 + [any_spec] * 8,
        out_specs=[vmem] * 4 + [any_spec] * 5,
        scratch_shapes=[
            pltpu.VMEM((2, 2, 2, half, WIDE), BF16),
            pltpu.VMEM((2, 2, 2 * half, FEED), BF16),
            box, box, box, box, box,
            pltpu.SemaphoreType.DMA((7, KV_HEADS)),
            pltpu.SemaphoreType.DMA((7, KV_HEADS)),
            pltpu.SemaphoreType.DMA((2, 3)),
            pltpu.SemaphoreType.DMA((3,)),
        ] + Sums.scratch(bits, 2, 1, chunks, half),
        compiler_params=pltpu.CompilerParams(
            collective_id=3, has_side_effects=True, vmem_limit_bytes=60 * 1024 * 1024),
        name="middle",
    )(low, cosine, sine, gains, attended, lse, x, cotangent, queries, both, w_output, w_gate, w_up, w_down_t)


def finish_kernel(bits, chunks, dq, dkv, cosine, sine, hidden, x, scale, gains, w_qkv, attended, branch, middle, feed_row,
                  out, gains_out, tokens_out, pack, grads, prod, *rest):
    sums = Sums(bits, [pack], None, [out], rest[:-5])
    g_loc, g_in, g_sem, g_send, g_recv = rest[-5:]
    half = HEAD_DIM // 2
    rows = pack.shape[1]
    greet(sums.partners)

    def gain_route(n):
        return Route(g_loc.at[n], g_in.at[n], g_send.at[n], g_recv.at[n], sums.partners[n])

    def unrotate(values, at):
        one, two = values[:half], values[half:]
        cos, sin = cosine[...], sine[...]
        grads[at : at + half, :] = (one * cos + two * sin).astype(BF16)
        grads[at + half : at + HEAD_DIM, :] = (two * cos - one * sin).astype(BF16)

    def columns(low, high):
        parts = []
        if low < D:
            parts.append((attended, branch, low, min(high, D)))
        if high > D:
            parts.append((hidden, grads, max(low, D) - D, high - D))
        return [against_rows(left[...], right[a:b, :]) for left, right, a, b in parts]

    def fill(n):
        parts = columns(n * WIDE, (n + 1) * WIDE)
        value = parts[0] if len(parts) == 1 else jnp.concatenate(parts, axis=1)
        value = value.astype(BF16)
        for which in range(2):
            pack[which, :, n * WIDE : (n + 1) * WIDE] = value[which * rows : (which + 1) * rows]
        sums.start_core(0, n)

    def heads():
        grads[:D, :] = dq[...]
        for h in range(KV_HEADS):
            both = dkv[h].T
            unrotate(both[:HEAD_DIM], D + h * HEAD_DIM)
            at = D + (KV_HEADS + h) * HEAD_DIM
            grads[at : at + HEAD_DIM, :] = both[HEAD_DIM:].astype(BF16)

    def hidden_grad():
        keys_values = 2 * KV_HEADS * HEAD_DIM
        dh = dot(w_qkv[:, keys_values:], grads[:D, :]) + dot(w_qkv[:, :keys_values], grads[D:, :])
        tokens_out[...] = dh
        prod[...] = dh * (x[...].astype(F32) * scale[...])
        g_loc[0] = jnp.zeros(g_loc.shape[1:], F32)
        ones = jnp.ones((8, dh.shape[1]), F32)
        total = lax.dot_general(ones, prod[...], (((1,), (1,)), ((), ())), precision=lax.Precision.HIGHEST,
                                preferred_element_type=F32)
        g_loc[0, 0:1, :] = total[0:1]
        g_loc[0, 1:2, :] = feed_row[0:1, :]
        gain_route(0).start()

    def tokens_grad():
        normed = x[...].astype(F32) * scale[...]
        gain = gains[:, 0:1].astype(F32)
        e = tokens_out[...] * gain
        mean = jnp.sum(prod[...] * gain, axis=0, keepdims=True) * (1.0 / D)
        tokens_out[...] = middle[...] + scale[...] * (e - normed * mean)

    def gain_step(n):
        gain_route(n - 1).arrived()
        g_loc[n] = g_loc[n - 1] + g_in[n - 1]
        if n < len(sums.partners):
            gain_route(n).start()

    work = [lambda: fill(0), lambda: (heads(), fill(1))] + [functools.partial(fill, n) for n in range(2, chunks)]
    work += [hidden_grad, tokens_grad] + [functools.partial(gain_step, n + 1) for n in range(len(sums.partners))]
    steps = [sums.start_y] + sums.stages
    delay = [1, 3]
    while len(delay) < len(steps):
        delay.append(delay[-1] + 1)
    for tick in range(max(chunks + delay[-1], len(work))):
        if tick < len(work):
            work[tick]()
        for s in [0] + list(range(len(steps) - 1, 0, -1)):
            if 0 <= tick - delay[s] < chunks:
                steps[s](0, tick - delay[s])
    store = pltpu.make_async_copy(g_loc.at[len(sums.partners)], gains_out, g_sem.at[0])
    store.start()
    for n in range(chunks):
        sums.core_sent(0, n)
        sums.drain(0, n)
    for n in range(len(sums.partners)):
        gain_route(n).sent()
    store.wait()


def finish(dq, dkv, cosine, sine, hidden, x, scale, gains, w_qkv, attended, branch, middle, feed_row, dp_size):
    bits = dp_size.bit_length() - 1
    own = x.shape[1]
    total = 2 * D + 2 * KV_HEADS * HEAD_DIM
    chunks = total // WIDE
    any_spec = pl.BlockSpec(memory_space=pl.ANY)
    vmem = pl.BlockSpec(memory_space=pltpu.VMEM)
    row = (8, D)
    return pl.pallas_call(
        functools.partial(finish_kernel, bits, chunks),
        out_shape=[
            jax.ShapeDtypeStruct((D // 2, total), BF16),
            jax.ShapeDtypeStruct(row, F32),
            jax.ShapeDtypeStruct((D, own), F32),
        ],
        in_specs=[vmem] * 13,
        out_specs=[any_spec, any_spec, vmem],
        scratch_shapes=[
            pltpu.VMEM((2, D // 2, total), BF16),
            pltpu.VMEM((total - D, own), BF16),
            pltpu.VMEM((D, own), F32),
        ] + Sums.scratch(bits, 1, 0, chunks, D // 4) + [
            pltpu.VMEM((bits + 2,) + row, F32),
            pltpu.VMEM((bits + 1,) + row, F32),
            pltpu.SemaphoreType.DMA((1,)),
            pltpu.SemaphoreType.DMA((bits + 1,)),
            pltpu.SemaphoreType.DMA((bits + 1,)),
        ],
        compiler_params=pltpu.CompilerParams(
            collective_id=0, has_side_effects=True, vmem_limit_bytes=56 * 1024 * 1024),
        name="finish",
    )(dq, dkv, cosine, sine, hidden, x, scale, gains, w_qkv, attended, branch, middle, feed_row)


def positions(seq_lengths, first, count):
    ends = jnp.cumsum(seq_lengths)
    index = first + jnp.arange(count, dtype=jnp.int32)
    passed = index[:, None] >= ends[None, :]
    begin = jnp.max(jnp.where(passed, ends[None, :], 0), axis=1)
    return index - begin


def rotary_tables(position):
    half = HEAD_DIM // 2
    inverse = jnp.exp(-jnp.arange(half, dtype=F32) * (2.0 / HEAD_DIM) * jnp.log(THETA))
    angle = inverse[:, None] * position.astype(F32)[None, :]
    return jnp.cos(angle), jnp.sin(angle)


def shards(tokens, cotangent, w_query, w_key, w_value, w_output, w_gate, w_up, w_down, attention_gain, feed_gain, seq_lengths):
    own = tokens.shape[0]
    kv = KV_HEADS * HEAD_DIM
    first = lax.axis_index(("dp", "shard")) * own
    position = positions(seq_lengths, first, own)
    low = jnp.arange(own, dtype=jnp.int32) - position
    cosine, sine = rotary_tables(position)
    gains = jnp.where(jnp.arange(128)[None, :] == 0, attention_gain[:, None], feed_gain[:, None])
    dp_size = lax.axis_size("dp")
    (attended, log_total, queries, hidden_one, scale_one, gains, both_all,
     qkv_full, output_full, gate_full, up_full, down_full) = attend(
        low[None, :], cosine, sine, tokens.T, w_query, w_key.T, w_value.T, gains,
        w_output, w_gate, w_up, w_down.T, dp_size
    )
    output, grad_middle, grad_branch, feed_rows, sum_gate, sum_up, sum_down, grad_queries, grad_own = middle_and_back(
        low[None, :], cosine, sine, gains, attended, log_total, tokens.T, cotangent.T, queries,
        both_all, output_full, gate_full, up_full, down_full, dp_size
    )
    sum_pack, sum_gains, grad_tokens = finish(
        grad_queries, grad_own, cosine, sine, hidden_one, tokens.T, scale_one, gains, qkv_full,
        attended, grad_branch, grad_middle, feed_rows, dp_size
    )
    sum_pack = sum_pack.astype(F32)
    half = D // 2
    begin = lax.axis_index("shard") * half
    return (
        output.T,
        grad_tokens.T,
        sum_pack[:, D : 2 * D],
        sum_pack[:, 2 * D : 2 * D + kv],
        sum_pack[:, 2 * D + kv :],
        sum_pack[:, :D],
        sum_gate.astype(F32),
        sum_up.astype(F32),
        sum_down.astype(F32).T,
        lax.dynamic_slice_in_dim(sum_gains[0], begin, half),
        lax.dynamic_slice_in_dim(sum_gains[1], begin, half),
    )


def solution(mesh):
    return jax.shard_map(
        shards,
        mesh=mesh,
        in_specs=(
            P(("dp", "shard"), None),
            P(("dp", "shard"), None),
            P("shard", None),
            P("shard", None),
            P("shard", None),
            P("shard", None),
            P("shard", None),
            P("shard", None),
            P("shard", None),
            P("shard"),
            P("shard"),
            P(),
        ),
        out_specs=(
            P(("dp", "shard"), None),
            P(("dp", "shard"), None),
            P("shard", None),
            P("shard", None),
            P("shard", None),
            P("shard", None),
            P("shard", None),
            P("shard", None),
            P("shard", None),
            P("shard"),
            P("shard"),
        ),
        check_vma=False,
    )
```
